32 devices in a mesh: groups: 2 (over y), rows: 4 (over z), cols: 4 (over x, core).
Axes of the slice: x: 2, y: 2, z: 4, core: 2. Of those that a mesh axis runs over, the one named last changes fastest.
Arguments:
- query: bfloat16 [128, 24, 1024], P(('groups', 'rows'), None, 'cols'), parts along dimension 0, may hold values from -8 to 8, as said below
- keys: bfloat16 [128, 24, 1024], P(('groups', 'rows'), None, 'cols'), parts along dimension 0, may hold values from -4 to 4, as said below
- values: bfloat16 [128, 24, 1024], P(('groups', 'rows'), None, 'cols'), parts along dimension 0, may hold values from -6 to 6
- registers: bfloat16 [2, 64, 1024], P(None, 'rows', 'cols'), may hold values from -6 to 6
- cotangent: bfloat16 [128, 24, 1024], P(('groups', 'rows'), None, 'cols'), parts along dimension 0, may hold values from -6 to 6
Outputs:
- attended: bfloat16 [128, 24, 1024], P(('groups', 'rows'), None, 'cols'), parts along dimension 0
- grad_query: bfloat16 [128, 24, 1024], P(('groups', 'rows'), None, 'cols'), parts along dimension 0
- grad_keys: bfloat16 [128, 24, 1024], P(('groups', 'rows'), None, 'cols'), parts along dimension 0
- grad_values: bfloat16 [128, 24, 1024], P(('groups', 'rows'), None, 'cols'), parts along dimension 0
- grad_registers: float32 [4, 64, 1024], P('groups', 'rows', 'cols'), parts along dimension 0
The draws below stay inside these ranges and needn't reach their ends.
There are 2 independent parts, one for each index of `groups`. The reference program is written for one: setup_inputs(seed, part) draws one part's arguments, and reference() takes and returns one part's arrays. A program takes and returns all parts, laid end to end along the dimension named above; an argument that names none is the same for every part. Nothing has to cross between parts.
Inputs may be any that keep to these rules, and one draw needn't show every extreme that they name: `query`: queries of order one; a few reach larger magnitudes. keys of order one.
All inputs are finite; a program needn't handle non-finite values.
Results may differ from the reference program's by a relative error of at most 0.0073.
Values may be sent and summed in bfloat16 or wider, within the bound.
No kernel may reach another device: no remote copies, remote signals or barrier semaphores. Data moves between devices by JAX's collectives and lax.ppermute only.
A program may use at most 128 MiB of HBM per device.

```python
import jax
import jax.numpy as jnp
from jax import lax

HEADS = 16
HEAD = 64
REG = 64
TILE = 8
PCOLS = 24
PROWS = 64


def paired_draw(key):
    shape = (PROWS, PCOLS, HEADS * HEAD)
    base_query = jnp.clip(jax.random.normal(jax.random.fold_in(key, 11), shape, jnp.float32), -4.0, 4.0)
    base_keys = jnp.clip(jax.random.normal(jax.random.fold_in(key, 12), shape, jnp.float32), -4.0, 4.0)
    query_all = base_query
    keys_all = base_keys
    return (query_all, keys_all)


def draw_query(key, part):
    return paired_draw(key)[0].astype(jnp.bfloat16)


def draw_keys(key, part):
    return paired_draw(key)[1].astype(jnp.bfloat16)


def block_levels(rng, extent, cuts, smallest, top_value):
    factor_of = 1.0
    for dim, parts in cuts:
        steps = jax.random.uniform(jax.random.fold_in(jax.random.fold_in(rng, 6), dim), (parts,), jnp.float32, smallest / len(cuts), top_value / len(cuts))
        factor_of = factor_of * jnp.repeat(jnp.exp(steps), extent[dim] // parts).reshape((-1,) + (1,) * (len(extent) - 1 - dim))
    return factor_of


def scatter_about(stream_key, extent, scale, limit, cuts=(), held_as=jnp.bfloat16):
    factor_of = block_levels(stream_key, extent, cuts, -0.22, 0.18) if cuts else 1.0
    values = jax.random.normal(stream_key, extent, jnp.float32) * scale * factor_of
    return jnp.minimum(jnp.maximum(values, -limit), limit).astype(held_as)


def setup_inputs(seed: int = 0, part: int = 0) -> dict:
    seeds = jax.random.split(jax.random.key(seed), 6)
    part_splits = jax.random.split(jax.random.fold_in(seeds[5], part), 6)
    query = draw_query(jax.random.fold_in(jax.random.fold_in(seeds[5], part), 71), part)
    keys = draw_keys(jax.random.fold_in(jax.random.fold_in(seeds[5], part), 71), part)
    values = scatter_about(part_splits[2], (PROWS, PCOLS, HEADS * HEAD), 1.0, 6.0, ((0, 4), (2, 4)))
    registers = scatter_about(seeds[3], (2, REG, HEADS * HEAD), 1.0, 6.0, ((1, 4), (2, 4)))
    cotangent = scatter_about(part_splits[4], (PROWS, PCOLS, HEADS * HEAD), 1.0, 6.0, ((0, 4), (2, 4)))
    return dict(query=query, keys=keys, values=values, registers=registers, cotangent=cotangent)


def neighbours(window, tile_cols, head_count):
    padded = jnp.pad(window, ((0, 0), (TILE, TILE), (0, 0)))
    tile_grid = padded.reshape(3 * TILE, tile_cols + 2, TILE, head_count, HEAD)
    return jnp.stack([tile_grid[:, offset:offset + tile_cols] for offset in range(3)], axis=1)


def spread_back(near, span_cols, feature):
    pieces = [jnp.pad(near[:, offset], ((0, 0), (offset, 2 - offset), (0, 0), (0, 0), (0, 0))) for offset in range(3)]
    total = pieces[0] + pieces[1] + pieces[2]
    return total[:, 1:-1].reshape(3 * TILE, span_cols, feature)


def attend_grads(query_row, key_window, value_window, reg_keys, reg_values, grad_row, row_valid):
    span_cols = query_row.shape[1]
    feature = query_row.shape[2]
    tile_cols = span_cols // TILE
    head_count = feature // HEAD
    factor = HEAD ** -0.5
    flat = jnp.float32
    queries = query_row.reshape(TILE, tile_cols, TILE, head_count, HEAD)
    grads_in = grad_row.reshape(TILE, tile_cols, TILE, head_count, HEAD)
    near_keys = neighbours(key_window, tile_cols, head_count)
    near_values = neighbours(value_window, tile_cols, head_count)
    reg_k = reg_keys.reshape(-1, head_count, HEAD)
    reg_v = reg_values.reshape(-1, head_count, HEAD)
    scores = jnp.einsum("icjhd,axcbhd->chijaxb", queries, near_keys, preferred_element_type=flat) * factor
    col_at = jnp.arange(tile_cols, dtype=jnp.int32)[:, None] + jnp.arange(3, dtype=jnp.int32)[None, :] - 1
    col_valid = (col_at >= 0) & (col_at < tile_cols)
    rows_valid = jnp.repeat(row_valid, TILE)
    allowed = rows_valid[None, None, None, None, :, None, None] & col_valid[:, None, None, None, None, :, None]
    scores = jnp.where(allowed, scores, -1e30)
    reg_scores = jnp.einsum("icjhd,ghd->chijg", queries, reg_k, preferred_element_type=flat) * factor
    local_count = 9 * TILE * TILE
    local_shape = (tile_cols, head_count, TILE, TILE, 3 * TILE, 3, TILE)
    all_scores = jnp.concatenate([scores.reshape(tile_cols, head_count, TILE, TILE, local_count), reg_scores], axis=-1)
    row_max = jnp.max(all_scores, axis=-1, keepdims=True)
    exp_scores = jnp.exp(all_scores - row_max)
    probs = exp_scores / jnp.sum(exp_scores, axis=-1, keepdims=True)
    weights = probs.astype(jnp.bfloat16)
    local_weights = weights[..., :local_count].reshape(local_shape)
    reg_weights = weights[..., local_count:]
    mixed = jnp.einsum("chijaxb,axcbhd->icjhd", local_weights, near_values, preferred_element_type=flat)
    mixed = mixed + jnp.einsum("chijg,ghd->icjhd", reg_weights, reg_v, preferred_element_type=flat)
    result = mixed.reshape(TILE, span_cols, feature).astype(jnp.bfloat16)
    d_local = jnp.einsum("icjhd,axcbhd->chijaxb", grads_in, near_values, preferred_element_type=flat)
    d_reg = jnp.einsum("icjhd,ghd->chijg", grads_in, reg_v, preferred_element_type=flat)
    d_weights = jnp.concatenate([d_local.reshape(tile_cols, head_count, TILE, TILE, local_count), d_reg],
                                axis=-1).astype(jnp.bfloat16)
    d_wide = lax.optimization_barrier(d_weights).astype(flat)
    row_dot = jnp.sum(probs * d_wide, axis=-1, keepdims=True)
    d_scores = (probs * (d_wide - row_dot)).astype(jnp.bfloat16)
    ds_local = d_scores[..., :local_count].reshape(local_shape)
    ds_reg = d_scores[..., local_count:]
    grad_q = jnp.einsum("chijaxb,axcbhd->icjhd", ds_local, near_keys, preferred_element_type=flat)
    grad_q = (grad_q + jnp.einsum("chijg,ghd->icjhd", ds_reg, reg_k, preferred_element_type=flat)) * factor
    grad_near_k = jnp.einsum("chijaxb,icjhd->axcbhd", ds_local, queries, preferred_element_type=flat) * factor
    grad_near_v = jnp.einsum("chijaxb,icjhd->axcbhd", local_weights, grads_in, preferred_element_type=flat)
    grad_rk = jnp.einsum("chijg,icjhd->ghd", ds_reg, queries, preferred_element_type=flat) * factor
    grad_rv = jnp.einsum("chijg,icjhd->ghd", reg_weights, grads_in, preferred_element_type=flat)
    return (result, grad_q.reshape(TILE, span_cols, feature),
            spread_back(grad_near_k, span_cols, feature), spread_back(grad_near_v, span_cols, feature),
            grad_rk.reshape(-1, feature), grad_rv.reshape(-1, feature))


def row_grads(query_row, key_window, value_window, reg_keys, reg_values, grad_row, row_at, total_rows):
    tile_at = row_at - 1 + jnp.arange(3, dtype=jnp.int32)
    row_valid = (tile_at >= 0) & (tile_at < total_rows)
    return attend_grads(query_row, key_window, value_window, reg_keys, reg_values, grad_row, row_valid)


def sweep(query_rows, grad_rows, key_rows, value_rows, reg_keys, reg_values, first_row, total_rows, own_low, own_high):
    query_count = query_rows.shape[0] // TILE
    acc_shape = (key_rows.shape[0], key_rows.shape[1], key_rows.shape[2])
    start_state = (jnp.zeros(acc_shape, jnp.float32), jnp.zeros(acc_shape, jnp.float32),
                   jnp.zeros(reg_keys.shape, jnp.float32), jnp.zeros(reg_keys.shape, jnp.float32))

    def advance(state_in, row_idx):
        acc_keys, acc_values, acc_reg_k, acc_reg_v = state_in
        leading = (row_idx * TILE).astype(jnp.int32)
        query_row = lax.dynamic_slice_in_dim(query_rows, leading, TILE, 0)
        grad_row = lax.dynamic_slice_in_dim(grad_rows, leading, TILE, 0)
        key_window = lax.dynamic_slice_in_dim(key_rows, leading, 3 * TILE, 0)
        value_window = lax.dynamic_slice_in_dim(value_rows, leading, 3 * TILE, 0)
        result, grad_q, grad_k, grad_v, grad_rk, grad_rv = row_grads(
            query_row, key_window, value_window, reg_keys, reg_values, grad_row, first_row + row_idx, total_rows)
        acc_keys = lax.dynamic_update_slice_in_dim(
            acc_keys, lax.dynamic_slice_in_dim(acc_keys, leading, 3 * TILE, 0) + grad_k, leading, 0)
        acc_values = lax.dynamic_update_slice_in_dim(
            acc_values, lax.dynamic_slice_in_dim(acc_values, leading, 3 * TILE, 0) + grad_v, leading, 0)
        inside = ((row_idx >= own_low) & (row_idx < own_high)).astype(jnp.float32)
        acc_reg_k = acc_reg_k + inside * grad_rk
        acc_reg_v = acc_reg_v + inside * grad_rv
        return (acc_keys, acc_values, acc_reg_k, acc_reg_v), (result, grad_q)

    final_state, outputs = lax.scan(advance, start_state, jnp.arange(query_count, dtype=jnp.int32))
    results, grads_q = outputs
    tail_shape = (query_count * TILE, query_rows.shape[1], query_rows.shape[2])
    return (results.reshape(tail_shape), grads_q.reshape(tail_shape)) + tuple(final_state)


def reference(query, keys, values, registers, cotangent):
    total_rows = query.shape[0] // TILE
    margins = ((TILE, TILE), (0, 0), (0, 0))
    key_rows = jnp.pad(keys, margins)
    value_rows = jnp.pad(values, margins)
    attended, grad_query, acc_keys, acc_values, grad_rk, grad_rv = sweep(
        query, cotangent, key_rows, value_rows, registers[0], registers[1], 0, total_rows, 0, total_rows)
    grad_keys = acc_keys[TILE:-TILE].astype(jnp.bfloat16)
    grad_values = acc_values[TILE:-TILE].astype(jnp.bfloat16)
    return attended, grad_query.astype(jnp.bfloat16), grad_keys, grad_values, jnp.stack([grad_rk, grad_rv])
```

```python
import functools

import jax
import jax.numpy as jnp
from jax import lax
from jax.experimental import pallas as pl
from jax.experimental.pallas import tpu as pltpu
from jax.sharding import PartitionSpec as P

HEAD = 64
TILE = 8
PATCH = TILE * TILE
FACTOR = HEAD ** (-0.5)
BF = jnp.bfloat16
F32 = jnp.float32
VMEM = pl.BlockSpec(memory_space=pltpu.VMEM)


def swap(array, pairs):
    return lax.ppermute(array, "rows", pairs)


def pairs_a(count):
    return [(i, i ^ 1) for i in range(count)]


def pairs_b(count):
    return [p for i in range(1, count - 1, 2) for p in ((i, i + 1), (i + 1, i))]


def column_tiles(block, tile_cols):
    feature = block.shape[1]
    wide = block.astype(F32).reshape(-1, tile_cols, TILE, feature)
    return [wide[:, c].reshape(-1, feature) for c in range(tile_cols)]


def patch_order(columns):
    feature = columns[0].shape[1]
    parts = [x.reshape(-1, 1, TILE, feature) for x in columns]
    return jnp.concatenate(parts, axis=1).reshape(-1, feature)


def slots(heads):
    return [0, 2, 1, 3] if heads == 4 else list(range(heads))


def block_diagonal(tile, heads):
    order = slots(heads)
    feature = tile.shape[1]
    lane_head = lax.broadcasted_iota(jnp.int32, tile.shape, 1) // HEAD
    zero = jnp.zeros_like(tile)
    return jnp.concatenate([jnp.where(lane_head == h, tile, zero) for h in order], axis=0)


def from_transposed(out_t, heads):
    if heads == 4:
        first = lax.broadcasted_iota(jnp.int32, (HEAD, 2 * PATCH), 1) < PATCH
        left = jnp.where(first, out_t[:HEAD, : 2 * PATCH], out_t[2 * HEAD : 3 * HEAD, : 2 * PATCH])
        right = jnp.where(first, out_t[HEAD : 2 * HEAD, 2 * PATCH :], out_t[3 * HEAD :, 2 * PATCH :])
        turned = jnp.concatenate([left, right], axis=0).T
        return jnp.concatenate([turned[:PATCH], turned[PATCH:]], axis=1)
    turned = out_t.T
    lane_head = lax.broadcasted_iota(jnp.int32, (PATCH, heads * HEAD), 1) // HEAD
    total = turned[:PATCH]
    for h in range(1, heads):
        total = jnp.where(lane_head == h, turned[h * PATCH : (h + 1) * PATCH], total)
    return total


def dot_nt(a, b):
    return lax.dot_general(a, b, (((1,), (1,)), ((), ())), preferred_element_type=F32)


def dot_nn(a, b):
    return lax.dot_general(a, b, (((1,), (0,)), ((), ())), preferred_element_type=F32)


def prepare_kernel(k_ref, v_ref, reg_ref, a_ref, b_ref):
    even = lax.rem(lax.axis_index("rows"), 2) == 0
    edge = b_ref.shape[0] // 2
    last = k_ref.shape[0] - edge
    for n, ref in enumerate((k_ref, v_ref)):
        top, bottom = ref[:edge], ref[last:]
        a_ref[n * edge : (n + 1) * edge] = jnp.where(even, bottom, top)
        b_ref[n * edge : (n + 1) * edge] = jnp.where(even, top, bottom)
    own = reg_ref.shape[1]
    if a_ref.shape[0] > 2 * edge:
        a_ref[2 * edge : 2 * edge + own] = reg_ref[0]
        a_ref[2 * edge + own :] = reg_ref[1]


def attention_kernel(
    tile_cols,
    q_ref,
    g_ref,
    k_ref,
    v_ref,
    a_ref,
    b_ref,
    *refs,
    split_regs,
):
    if split_regs:
        own_ref, c_ref, e_ref = refs[:3]
        refs = refs[3:]
    else:
        all_ref = refs[0]
        refs = refs[1:]
    o_ref, dq_ref, dk_ref, dv_ref, back_a_ref, back_b_ref, dreg_ref = refs[:7]
    kw_ref, vw_ref, kt_ref, vt_ref, acck_ref, accv_ref, accr_ref = refs[7:]
    feature = q_ref.shape[1]
    heads = feature // HEAD
    line = tile_cols * PATCH
    tile_rows = q_ref.shape[0] // line
    near = 3 * PATCH
    me = lax.axis_index("rows")
    even = lax.rem(me, 2) == 0
    has_top = me > 0
    has_bottom = me < lax.axis_size("rows") - 1

    a_rows = b_ref.shape[0] // 2
    for n, (x_ref, w_ref, t_ref) in enumerate(((k_ref, kw_ref, kt_ref), (v_ref, vw_ref, vt_ref))):
        from_a = a_ref[n * a_rows : (n + 1) * a_rows]
        from_b = b_ref[n * a_rows : (n + 1) * a_rows]
        top = column_tiles(jnp.where(even, from_b, from_a), tile_cols)
        bottom = column_tiles(jnp.where(even, from_a, from_b), tile_cols)
        own = column_tiles(x_ref[...], tile_cols)
        if split_regs:
            cut = own_ref.shape[1]
            base = 2 * a_rows + n * cut
            regs = jnp.concatenate(
                [
                    own_ref[n],
                    a_ref[base : base + cut],
                    c_ref[n],
                    e_ref[n],
                ],
                axis=0,
            )
        else:
            regs = all_ref[n]
        for c in range(tile_cols):
            column = jnp.concatenate([top[c], own[c], bottom[c]], axis=0).astype(BF)
            for t in range(tile_rows):
                window = jnp.concatenate([column[t * PATCH : t * PATCH + near], regs], axis=0)
                w_ref[t, c] = window
                t_ref[t, c] = window.T

    seen = set()

    def add(ref, at, rows, value):
        key = (id(ref), at, rows.start)
        if key in seen:
            ref[at, rows] += value
        else:
            seen.add(key)
            ref[at, rows] = value

    for t in range(tile_rows):
        q_cols = column_tiles(q_ref[t * line : (t + 1) * line], tile_cols)
        g_cols = column_tiles(g_ref[t * line : (t + 1) * line], tile_cols)
        o_cols, dq_cols = [], []
        for c in range(tile_cols):
            q_bd = block_diagonal((q_cols[c] * FACTOR).astype(BF), heads)
            g_bd = block_diagonal(g_cols[c].astype(BF), heads)
            across = [x for x in (c - 1, c, c + 1) if 0 <= x < tile_cols]
            scores, grads = [], []
            for x in across:
                size = kw_ref.shape[2] if x == c else near
                s = dot_nt(kw_ref[t, x, :size], q_bd)
                parts = [s[n * PATCH : (n + 1) * PATCH] for n in range(3)] + [s[near:]]
                if t == 0:
                    parts[0] = jnp.where(has_top, parts[0], -1e30)
                if t == tile_rows - 1:
                    parts[2] = jnp.where(has_bottom, parts[2], -1e30)
                if x != c:
                    parts = parts[:3]
                scores.append(jnp.concatenate(parts, axis=0))
                grads.append(dot_nt(vw_ref[t, x, :size], g_bd).astype(BF).astype(F32))
            top_score = functools.reduce(jnp.maximum, [jnp.max(s, axis=0, keepdims=True) for s in scores])
            exps = [jnp.exp(s - top_score) for s in scores]
            inverse = 1.0 / sum(jnp.sum(e, axis=0, keepdims=True) for e in exps)
            probs = [e * inverse for e in exps]
            row_dot = sum(jnp.sum(p * d, axis=0, keepdims=True) for p, d in zip(probs, grads))
            o_t = dq_t = None
            for x, p, d in zip(across, probs, grads):
                weights = p.astype(BF)
                d_scores = (p * (d - row_dot)).astype(BF)
                dk = dot_nn(d_scores, q_bd)
                dv = dot_nn(weights, g_bd)
                window = slice(t * PATCH, t * PATCH + near)
                for a in range(3):
                    rows = slice((t + a) * PATCH, (t + a + 1) * PATCH)
                    add(acck_ref, x, rows, dk[a * PATCH : (a + 1) * PATCH])
                    add(accv_ref, x, rows, dv[a * PATCH : (a + 1) * PATCH])
                if x == c:
                    add(accr_ref, 0, slice(0, p.shape[0] - near), dk[near:])
                    add(accr_ref, 1, slice(0, p.shape[0] - near), dv[near:])
                else:
                    rest = jnp.zeros((kw_ref.shape[2] - near, feature), BF)
                    weights = jnp.concatenate([weights, rest], axis=0)
                    d_scores = jnp.concatenate([d_scores, rest], axis=0)
                o_x = dot_nn(vt_ref[t, x], weights)
                dq_x = dot_nn(kt_ref[t, x], d_scores)
                o_t = o_x if o_t is None else o_t + o_x
                dq_t = dq_x if dq_t is None else dq_t + dq_x
            o_cols.append(from_transposed(o_t, heads))
            dq_cols.append(from_transposed(dq_t, heads) * FACTOR)
        o_ref[t * line : (t + 1) * line] = patch_order(o_cols).astype(BF)
        dq_ref[t * line : (t + 1) * line] = patch_order(dq_cols).astype(BF)

    last = (tile_rows + 1) * PATCH
    for n, (acc_ref, out_ref) in enumerate(((acck_ref, dk_ref), (accv_ref, dv_ref))):
        top = jnp.concatenate([acc_ref[c, :PATCH] for c in range(tile_cols)], axis=0)
        bottom = jnp.concatenate([acc_ref[c, last:] for c in range(tile_cols)], axis=0)
        back_a_ref[n * a_rows : (n + 1) * a_rows] = jnp.where(even, bottom, top).astype(BF)
        back_b_ref[n * a_rows : (n + 1) * a_rows] = jnp.where(even, top, bottom).astype(BF)
        for c in range(tile_cols):
            out_ref[c] = acc_ref[c, PATCH:last]
        if split_regs:
            base = 2 * a_rows + n * cut
            back_a_ref[base : base + cut] = accr_ref[n, cut : 2 * cut].astype(BF)
    dreg_ref[...] = accr_ref[...]


def finish_kernel(dk_ref, dv_ref, a_ref, b_ref, *refs, split_regs):
    if split_regs:
        dreg_ref, c_ref, e_ref = refs[:3]
        refs = refs[3:]
    gk_ref, gv_ref = refs[:2]
    even = lax.rem(lax.axis_index("rows"), 2) == 0
    tile_cols = dk_ref.shape[0]
    edge = b_ref.shape[0] // 2
    for n, (acc_ref, out_ref) in enumerate(((dk_ref, gk_ref), (dv_ref, gv_ref))):
        from_a = a_ref[n * edge : (n + 1) * edge]
        from_b = b_ref[n * edge : (n + 1) * edge]
        top = jnp.where(even, from_b, from_a).astype(F32)
        bottom = jnp.where(even, from_a, from_b).astype(F32)
        rows = acc_ref.shape[1]
        columns = []
        for c in range(tile_cols):
            high = top[c * PATCH : (c + 1) * PATCH]
            low = bottom[c * PATCH : (c + 1) * PATCH]
            if rows == PATCH:
                columns.append(acc_ref[c] + high + low)
                continue
            columns.append(
                jnp.concatenate(
                    [acc_ref[c, :PATCH] + high, acc_ref[c, PATCH : rows - PATCH], acc_ref[c, rows - PATCH :] + low]
                    if rows > 2 * PATCH
                    else [acc_ref[c, :PATCH] + high, acc_ref[c, PATCH:] + low],
                    axis=0,
                )
            )
        out_ref[...] = patch_order(columns).astype(BF)
        if split_regs:
            cut = c_ref.shape[1]
            base = 2 * edge + n * cut
            refs[2][n] = (
                dreg_ref[n, :cut]
                + a_ref[base : base + cut].astype(F32)
                + c_ref[n].astype(F32)
                + e_ref[n].astype(F32)
            )


def shape(dims, dtype):
    return jax.ShapeDtypeStruct(dims, dtype)


def params():
    return pltpu.CompilerParams(vmem_limit_bytes=48 * 1024 * 1024)


def shards(query, keys, values, registers, cotangent):
    count = lax.axis_size("rows")
    split_regs = count == 4
    tile_cols = query.shape[1] // TILE
    tile_rows = query.shape[0] // TILE
    feature = query.shape[2]
    total = query.shape[0] * query.shape[1]
    edge = tile_cols * PATCH
    own = registers.shape[1]
    reg_count = own * count
    q, k, v, g = (x.reshape(total, feature) for x in (query, keys, values, cotangent))
    extra = 2 * own if split_regs else 0

    pay_a, pay_b = pl.pallas_call(
        prepare_kernel,
        out_shape=(shape((2 * edge + extra, feature), BF), shape((2 * edge, feature), BF)),
        in_specs=[VMEM] * 3,
        out_specs=(VMEM, VMEM),
        compiler_params=params(),
        name="prepare",
    )(k, v, registers)
    got_b = swap(pay_b, pairs_b(count))
    got_a = swap(pay_a, pairs_a(count))
    if split_regs:
        two = [(i, i ^ 2) for i in range(count)]
        three = [(i, i ^ 3) for i in range(count)]
        regs = (registers, swap(registers, two), swap(registers, three))
    else:
        regs = (lax.all_gather(registers, "rows", axis=1, tiled=True),)

    span = (tile_rows + 2) * PATCH
    window = 3 * PATCH + reg_count
    attended, grad_query, dk, dv, back_a, back_b, dreg = pl.pallas_call(
        functools.partial(attention_kernel, tile_cols, split_regs=split_regs),
        out_shape=(
            shape((total, feature), BF),
            shape((total, feature), BF),
            shape((tile_cols, tile_rows * PATCH, feature), F32),
            shape((tile_cols, tile_rows * PATCH, feature), F32),
            shape((2 * edge + extra, feature), BF),
            shape((2 * edge, feature), BF),
            shape((2, reg_count, feature), F32),
        ),
        in_specs=[VMEM] * (6 + len(regs)),
        out_specs=(VMEM,) * 7,
        scratch_shapes=[
            pltpu.VMEM((tile_rows, tile_cols, window, feature), BF),
            pltpu.VMEM((tile_rows, tile_cols, window, feature), BF),
            pltpu.VMEM((tile_rows, tile_cols, feature, window), BF),
            pltpu.VMEM((tile_rows, tile_cols, feature, window), BF),
            pltpu.VMEM((tile_cols, span, feature), F32),
            pltpu.VMEM((tile_cols, span, feature), F32),
            pltpu.VMEM((2, reg_count, feature), F32),
        ],
        compiler_params=params(),
        name="attention",
    )(q, g, k, v, got_a, got_b, *regs)

    back_from_b = swap(back_b, pairs_b(count))
    back_from_a = swap(back_a, pairs_a(count))
    if split_regs:
        tails = dreg.astype(BF)
        rest = (
            dreg,
            swap(tails[:, 2 * own : 3 * own], two),
            swap(tails[:, 3 * own :], three),
        )
        last_shapes = (shape((2, own, feature), F32),)
    else:
        rest = ()
        last_shapes = ()
    outs = pl.pallas_call(
        functools.partial(finish_kernel, split_regs=split_regs),
        out_shape=(shape((total, feature), BF), shape((total, feature), BF)) + last_shapes,
        in_specs=[VMEM] * (4 + len(rest)),
        out_specs=(VMEM,) * (2 + len(last_shapes)),
        compiler_params=params(),
        name="finish",
    )(dk, dv, back_from_a, back_from_b, *rest)
    if split_regs:
        grad_registers = outs[2]
    else:
        grad_registers = lax.psum_scatter(dreg, "rows", scatter_dimension=1, tiled=True)
    whole = query.shape
    return (
        attended.reshape(whole),
        grad_query.reshape(whole),
        outs[0].reshape(whole),
        outs[1].reshape(whole),
        grad_registers,
    )


def solution(mesh):
    slab = P(("groups", "rows"), None, "cols")
    in_specs = (slab, slab, slab, P(None, "rows", "cols"), slab)
    out_specs = (slab, slab, slab, slab, P("groups", "rows", "cols"))
    return jax.shard_map(shards, mesh=mesh, in_specs=in_specs, out_specs=out_specs, check_vma=False)
```

```python
import functools

import jax
import jax.numpy as jnp
from jax import lax
from jax.experimental import pallas as pl
from jax.experimental.pallas import tpu as pltpu
from jax.sharding import PartitionSpec as P

HEAD = 64
TILE = 8
PATCH = TILE * TILE
FACTOR = HEAD ** (-0.5)
BF = jnp.bfloat16
F32 = jnp.float32
VMEM = pl.BlockSpec(memory_space=pltpu.VMEM)


def swap(array, pairs):
    return lax.ppermute(array, "rows", pairs)


def pairs_a(count):
    return [(i, i ^ 1) for i in range(count)]


def pairs_b(count):
    return [p for i in range(1, count - 1, 2) for p in ((i, i + 1), (i + 1, i))]


def column_tiles(block, tile_cols):
    feature = block.shape[1]
    wide = block.astype(F32).reshape(-1, tile_cols, TILE, feature)
    return [wide[:, c].reshape(-1, feature) for c in range(tile_cols)]


def patch_order(columns):
    feature = columns[0].shape[1]
    parts = [x.reshape(-1, 1, TILE, feature) for x in columns]
    return jnp.concatenate(parts, axis=1).reshape(-1, feature)


def slots(heads):
    return [0, 2, 1, 3] if heads == 4 else list(range(heads))


def block_diagonal(tile, heads):
    order = slots(heads)
    feature = tile.shape[1]
    lane_head = lax.broadcasted_iota(jnp.int32, tile.shape, 1) // HEAD
    zero = jnp.zeros_like(tile)
    return jnp.concatenate([jnp.where(lane_head == h, tile, zero) for h in order], axis=0)


def from_transposed(out_t, heads):
    if heads == 4:
        first = lax.broadcasted_iota(jnp.int32, (HEAD, 2 * PATCH), 1) < PATCH
        left = jnp.where(first, out_t[:HEAD, : 2 * PATCH], out_t[2 * HEAD : 3 * HEAD, : 2 * PATCH])
        right = jnp.where(first, out_t[HEAD : 2 * HEAD, 2 * PATCH :], out_t[3 * HEAD :, 2 * PATCH :])
        turned = jnp.concatenate([left, right], axis=0).T
        return jnp.concatenate([turned[:PATCH], turned[PATCH:]], axis=1)
    turned = out_t.T
    lane_head = lax.broadcasted_iota(jnp.int32, (PATCH, heads * HEAD), 1) // HEAD
    total = turned[:PATCH]
    for h in range(1, heads):
        total = jnp.where(lane_head == h, turned[h * PATCH : (h + 1) * PATCH], total)
    return total


def dot_nt(a, b):
    return lax.dot_general(a, b, (((1,), (1,)), ((), ())), preferred_element_type=F32)


def dot_nn(a, b):
    return lax.dot_general(a, b, (((1,), (0,)), ((), ())), preferred_element_type=F32)


def prepare_kernel(k_ref, v_ref, reg_ref, a_ref, b_ref, sems):
    even = lax.rem(lax.axis_index("rows"), 2) == 0
    edge = b_ref.shape[0] // 2
    last = k_ref.shape[0] - edge
    at_a = pl.multiple_of(jnp.where(even, last, 0), edge)
    at_b = pl.multiple_of(jnp.where(even, 0, last), edge)
    moves = []
    for n, ref in enumerate((k_ref, v_ref)):
        moves.append((ref.at[pl.ds(at_a, edge)], a_ref.at[pl.ds(n * edge, edge)]))
        moves.append((ref.at[pl.ds(at_b, edge)], b_ref.at[pl.ds(n * edge, edge)]))
    own = reg_ref.shape[1]
    if a_ref.shape[0] > 2 * edge:
        for n in range(2):
            moves.append((reg_ref.at[n], a_ref.at[pl.ds(2 * edge + n * own, own)]))
    copies = [pltpu.make_async_copy(x, y, sems.at[n]) for n, (x, y) in enumerate(moves)]
    for copy in copies:
        copy.start()
    for copy in copies:
        copy.wait()


def columns_near(c, tile_cols):
    return max(c - 1, 0), min(c + 2, tile_cols)


def own_kernel(
    tile_cols,
    q_ref,
    g_ref,
    k_ref,
    v_ref,
    qbd_ref,
    gbd_ref,
    kt_ref,
    vt_ref,
    exp_ref,
    dw_ref,
    stat_ref,
    kc_ref,
    vc_ref,
):
    heads = q_ref.shape[1] // HEAD
    line = tile_cols * PATCH
    tile_rows = q_ref.shape[0] // line
    rows = tile_rows * PATCH
    for x_ref, c_ref, t_ref in ((k_ref, kc_ref, kt_ref), (v_ref, vc_ref, vt_ref)):
        for c, column in enumerate(column_tiles(x_ref[...], tile_cols)):
            column = column.astype(BF)
            c_ref[c * rows : (c + 1) * rows] = column
            t_ref[:, c * rows : (c + 1) * rows] = column.T
    for t in range(tile_rows):
        q_cols = column_tiles(q_ref[t * line : (t + 1) * line], tile_cols)
        g_cols = column_tiles(g_ref[t * line : (t + 1) * line], tile_cols)
        for c in range(tile_cols):
            tile = t * tile_cols + c
            q_bd = block_diagonal((q_cols[c] * FACTOR).astype(BF), heads)
            g_bd = block_diagonal(g_cols[c].astype(BF), heads)
            qbd_ref[tile] = q_bd
            gbd_ref[tile] = g_bd
            low, high = columns_near(c, tile_cols)
            near = slice(low * rows, high * rows)
            size = (high - low) * rows
            s = dot_nt(kc_ref[near], q_bd)
            d = dot_nt(vc_ref[near], g_bd).astype(BF)
            top = jnp.max(s, axis=0, keepdims=True)
            e = jnp.exp(s - top)
            exp_ref[tile, :size] = e
            dw_ref[tile, :size] = d
            stat_ref[tile, 0:1] = top
            stat_ref[tile, 1:2] = jnp.sum(e, axis=0, keepdims=True)
            stat_ref[tile, 2:3] = jnp.sum(e * d.astype(F32), axis=0, keepdims=True)


def far_kernel(tile_cols, split_regs, *refs):
    qbd_ref, gbd_ref, stat_ref, a_ref, b_ref = refs[:5]
    if split_regs:
        own_ref, two_ref, three_ref = refs[5:8]
        refs = refs[8:]
    else:
        all_ref = refs[5]
        refs = refs[6:]
    final_ref, px_ref, dsx_ref, kx_ref, vx_ref, back_a_ref, back_b_ref = refs[:7]
    reg_outs = refs[7:]
    feature = a_ref.shape[1]
    tile_rows = qbd_ref.shape[0] // tile_cols
    edge = tile_cols * PATCH
    me = lax.axis_index("rows")
    even = lax.rem(me, 2) == 0
    has = (me > 0, me < lax.axis_size("rows") - 1)
    for n, ref in enumerate((kx_ref, vx_ref)):
        from_a = a_ref[n * edge : (n + 1) * edge]
        from_b = b_ref[n * edge : (n + 1) * edge]
        top = column_tiles(jnp.where(even, from_b, from_a), tile_cols)
        bottom = column_tiles(jnp.where(even, from_a, from_b), tile_cols)
        if split_regs:
            cut = own_ref.shape[1]
            base = 2 * edge + n * cut
            regs = jnp.concatenate([own_ref[n], a_ref[base : base + cut], two_ref[n], three_ref[n]], axis=0)
        else:
            regs = all_ref[n]
        for t, halo in enumerate((top, bottom)):
            ref[t, :edge] = jnp.concatenate(halo, axis=0).astype(BF)
            ref[t, edge:] = regs
    dk_reg = dv_reg = None
    dk_halo, dv_halo = [], []
    for t in range(tile_rows):
        dk_t = dv_t = None
        for c in range(tile_cols):
            tile = t * tile_cols + c
            q_bd = qbd_ref[tile]
            g_bd = gbd_ref[tile]
            low, high = columns_near(c, tile_cols)
            s = dot_nt(kx_ref[t], q_bd)
            d = dot_nt(vx_ref[t], g_bd)
            s_near = jnp.where(has[t], s[low * PATCH : high * PATCH], -1e30)
            s = jnp.concatenate([s_near, s[edge:]], axis=0)
            d = jnp.concatenate([d[low * PATCH : high * PATCH], d[edge:]], axis=0)
            d = d.astype(BF).astype(F32)
            own_top = stat_ref[tile, 0:1]
            top = jnp.maximum(own_top, jnp.max(s, axis=0, keepdims=True))
            e = jnp.exp(s - top)
            ratio = jnp.exp(own_top - top)
            inverse = 1.0 / (stat_ref[tile, 1:2] * ratio + jnp.sum(e, axis=0, keepdims=True))
            row_dot = (stat_ref[tile, 2:3] * ratio + jnp.sum(e * d, axis=0, keepdims=True)) * inverse
            final_ref[tile, 0:1] = ratio * inverse
            final_ref[tile, 1:2] = row_dot
            p = e * inverse
            parts = []
            for x in (p, p * (d - row_dot)):
                x = x.astype(BF)
                pieces = [x]
                size = (high - low) * PATCH
                if low > 0 or high < tile_cols:
                    pieces = [x[:size], x[size:]]
                    if high < tile_cols:
                        pieces.insert(1, jnp.zeros(((tile_cols - high) * PATCH, feature), BF))
                    if low > 0:
                        pieces.insert(0, jnp.zeros((low * PATCH, feature), BF))
                parts.append(jnp.concatenate(pieces, axis=0))
            weights, d_scores = parts
            px_ref[tile] = weights
            dsx_ref[tile] = d_scores
            dk = dot_nn(d_scores, q_bd)
            dv = dot_nn(weights, g_bd)
            dk_t = dk if dk_t is None else dk_t + dk
            dv_t = dv if dv_t is None else dv_t + dv
        dk_halo.append(dk_t[:edge])
        dv_halo.append(dv_t[:edge])
        dk_reg = dk_t[edge:] if dk_reg is None else dk_reg + dk_t[edge:]
        dv_reg = dv_t[edge:] if dv_reg is None else dv_reg + dv_t[edge:]
    for n, (halo, reg) in enumerate(((dk_halo, dk_reg), (dv_halo, dv_reg))):
        top, bottom = halo
        back_a_ref[n * edge : (n + 1) * edge] = jnp.where(even, bottom, top).astype(BF)
        back_b_ref[n * edge : (n + 1) * edge] = jnp.where(even, top, bottom).astype(BF)
        if split_regs:
            base = 2 * edge + n * cut
            reg_outs[0][n] = reg[:cut]
            back_a_ref[base : base + cut] = reg[cut : 2 * cut].astype(BF)
            reg_outs[1][n] = reg[2 * cut : 3 * cut].astype(BF)
            reg_outs[2][n] = reg[3 * cut :].astype(BF)
        else:
            reg_outs[0][n] = reg


def rest_kernel(
    tile_cols,
    qbd_ref,
    gbd_ref,
    kt_ref,
    vt_ref,
    exp_ref,
    dw_ref,
    final_ref,
    px_ref,
    dsx_ref,
    kx_ref,
    vx_ref,
    o_ref,
    dq_ref,
    dk_ref,
    dv_ref,
):
    feature = kt_ref.shape[0]
    heads = feature // HEAD
    line = tile_cols * PATCH
    tile_rows = qbd_ref.shape[0] // tile_cols
    rows = tile_rows * PATCH
    for t in range(tile_rows):
        kxt = kx_ref[t].T
        vxt = vx_ref[t].T
        o_cols, dq_cols = [], []
        for c in range(tile_cols):
            tile = t * tile_cols + c
            low, high = columns_near(c, tile_cols)
            near = slice(low * rows, high * rows)
            size = (high - low) * rows
            p = exp_ref[tile, :size] * final_ref[tile, 0:1]
            d_scores = (p * (dw_ref[tile, :size].astype(F32) - final_ref[tile, 1:2])).astype(BF)
            weights = p.astype(BF)
            dk = dot_nn(d_scores, qbd_ref[tile])
            dv = dot_nn(weights, gbd_ref[tile])
            first = t == 0
            for ref, value in ((dk_ref, dk), (dv_ref, dv)):
                for x in range(low, high):
                    part = value[(x - low) * rows : (x - low + 1) * rows]
                    if first and (x == c + 1 or (c == 0)):
                        ref[x] = part
                    else:
                        ref[x] += part
            o_t = dot_nn(vt_ref[:, near], weights) + dot_nn(vxt, px_ref[tile])
            dq_t = dot_nn(kt_ref[:, near], d_scores) + dot_nn(kxt, dsx_ref[tile])
            o_cols.append(from_transposed(o_t, heads))
            dq_cols.append(from_transposed(dq_t, heads) * FACTOR)
        o_ref[t * line : (t + 1) * line] = patch_order(o_cols).astype(BF)
        dq_ref[t * line : (t + 1) * line] = patch_order(dq_cols).astype(BF)


def finish_kernel(dk_ref, dv_ref, a_ref, b_ref, *refs, split_regs):
    if split_regs:
        dreg_ref, c_ref, e_ref = refs[:3]
        refs = refs[3:]
    gk_ref, gv_ref = refs[:2]
    even = lax.rem(lax.axis_index("rows"), 2) == 0
    tile_cols = dk_ref.shape[0]
    edge = b_ref.shape[0] // 2
    for n, (acc_ref, out_ref) in enumerate(((dk_ref, gk_ref), (dv_ref, gv_ref))):
        from_a = a_ref[n * edge : (n + 1) * edge]
        from_b = b_ref[n * edge : (n + 1) * edge]
        top = jnp.where(even, from_b, from_a).astype(F32)
        bottom = jnp.where(even, from_a, from_b).astype(F32)
        rows = acc_ref.shape[1]
        columns = []
        for c in range(tile_cols):
            high = top[c * PATCH : (c + 1) * PATCH]
            low = bottom[c * PATCH : (c + 1) * PATCH]
            if rows == PATCH:
                columns.append(acc_ref[c] + high + low)
                continue
            columns.append(
                jnp.concatenate(
                    [acc_ref[c, :PATCH] + high, acc_ref[c, PATCH : rows - PATCH], acc_ref[c, rows - PATCH :] + low]
                    if rows > 2 * PATCH
                    else [acc_ref[c, :PATCH] + high, acc_ref[c, PATCH:] + low],
                    axis=0,
                )
            )
        out_ref[...] = patch_order(columns).astype(BF)
        if split_regs:
            cut = c_ref.shape[1]
            base = 2 * edge + n * cut
            refs[2][n] = (
                dreg_ref[n, :cut]
                + a_ref[base : base + cut].astype(F32)
                + c_ref[n].astype(F32)
                + e_ref[n].astype(F32)
            )


def shape(dims, dtype):
    return jax.ShapeDtypeStruct(dims, dtype)


def call(kernel, name, ins, outs, flops, in_specs=None, scratch=()):
    size = sum(x.size * x.dtype.itemsize for x in ins) + sum(x.size * x.dtype.itemsize for x in outs)
    return pl.pallas_call(
        kernel,
        out_shape=tuple(outs),
        in_specs=in_specs or [VMEM] * len(ins),
        out_specs=(VMEM,) * len(outs),
        scratch_shapes=list(scratch),
        compiler_params=pltpu.CompilerParams(vmem_limit_bytes=24 * 1024 * 1024),
        cost_estimate=pl.CostEstimate(flops=flops, bytes_accessed=size, transcendentals=0),
        name=name,
    )(*ins)


def shards(query, keys, values, registers, cotangent):
    count = lax.axis_size("rows")
    split_regs = count == 4
    tile_cols = query.shape[1] // TILE
    tile_rows = query.shape[0] // TILE
    assert tile_rows == 2
    feature = query.shape[2]
    total = query.shape[0] * query.shape[1]
    edge = tile_cols * PATCH
    own = registers.shape[1]
    reg_count = own * count
    q, k, v, g = (x.reshape(total, feature) for x in (query, keys, values, cotangent))
    extra = 2 * own if split_regs else 0
    two = [(i, i ^ 2) for i in range(count)]
    three = [(i, i ^ 3) for i in range(count)]

    if split_regs:
        regs = (registers, swap(registers, two), swap(registers, three))
    else:
        regs = (lax.all_gather(registers, "rows", axis=1, tiled=True),)
    pay_a, pay_b = call(
        prepare_kernel,
        "prepare",
        (k, v, registers),
        (shape((2 * edge + extra, feature), BF), shape((2 * edge, feature), BF)),
        0,
        in_specs=[pl.BlockSpec(memory_space=pl.ANY)] * 3,
        scratch=[pltpu.SemaphoreType.DMA((6,))],
    )
    got_b = swap(pay_b, pairs_b(count))
    got_a = swap(pay_a, pairs_a(count))

    tiles = tile_rows * tile_cols
    rows = tile_rows * PATCH
    most = min(3, tile_cols) * rows
    window = edge + reg_count
    qbd, gbd, kt, vt, exps, dw, stats = call(
        functools.partial(own_kernel, tile_cols),
        "own",
        (q, g, k, v),
        (
            shape((tiles, feature, feature), BF),
            shape((tiles, feature, feature), BF),
            shape((feature, total), BF),
            shape((feature, total), BF),
            shape((tiles, most, feature), F32),
            shape((tiles, most, feature), BF),
            shape((tiles, 8, feature), F32),
        ),
        4 * tiles * most * feature * feature,
        scratch=[pltpu.VMEM((total, feature), BF)] * 2,
    )
    if split_regs:
        reg_shapes = (
            shape((2, own, feature), F32),
            shape((2, own, feature), BF),
            shape((2, own, feature), BF),
        )
    else:
        reg_shapes = (shape((2, reg_count, feature), F32),)
    final, px, dsx, kx, vx, back_a, back_b, *back_regs = call(
        functools.partial(far_kernel, tile_cols, split_regs),
        "far",
        (qbd, gbd, stats, got_a, got_b) + regs,
        (
            shape((tiles, 8, feature), F32),
            shape((tiles, window, feature), BF),
            shape((tiles, window, feature), BF),
            shape((tile_rows, window, feature), BF),
            shape((tile_rows, window, feature), BF),
            shape((2 * edge + extra, feature), BF),
            shape((2 * edge, feature), BF),
        )
        + reg_shapes,
        8 * tiles * window * feature * feature,
    )
    back_from_b = swap(back_b, pairs_b(count))
    back_from_a = swap(back_a, pairs_a(count))
    if split_regs:
        rest = (back_regs[0], swap(back_regs[1], two), swap(back_regs[2], three))
        last_shapes = (shape((2, own, feature), F32),)
    else:
        rest = ()
        last_shapes = ()
    attended, grad_query, dk, dv = call(
        functools.partial(rest_kernel, tile_cols),
        "rest",
        (qbd, gbd, kt, vt, exps, dw, final, px, dsx, kx, vx),
        (
            shape((total, feature), BF),
            shape((total, feature), BF),
            shape((tile_cols, rows, feature), F32),
            shape((tile_cols, rows, feature), F32),
        ),
        8 * tiles * most * feature * feature,
    )
    outs = call(
        functools.partial(finish_kernel, split_regs=split_regs),
        "finish",
        (dk, dv, back_from_a, back_from_b) + rest,
        (shape((total, feature), BF), shape((total, feature), BF)) + last_shapes,
        0,
    )
    if split_regs:
        grad_registers = outs[2]
    else:
        grad_registers = lax.psum_scatter(back_regs[0], "rows", scatter_dimension=1, tiled=True)
    whole = query.shape
    return (
        attended.reshape(whole),
        grad_query.reshape(whole),
        outs[0].reshape(whole),
        outs[1].reshape(whole),
        grad_registers,
    )


def solution(mesh):
    slab = P(("groups", "rows"), None, "cols")
    in_specs = (slab, slab, slab, P(None, "rows", "cols"), slab)
    out_specs = (slab, slab, slab, slab, P("groups", "rows", "cols"))
    return jax.shard_map(shards, mesh=mesh, in_specs=in_specs, out_specs=out_specs, check_vma=False)
```

```python
import functools

import jax
import jax.numpy as jnp
from jax import lax
from jax.experimental import pallas as pl
from jax.experimental.pallas import tpu as pltpu
from jax.sharding import PartitionSpec as P

HEAD = 64
TILE = 8
PATCH = TILE * TILE
FACTOR = HEAD ** (-0.5)
HEAVY = 20_000_000_000
BF = jnp.bfloat16
F32 = jnp.float32
VMEM = pl.BlockSpec(memory_space=pltpu.VMEM)
HBM = pl.BlockSpec(memory_space=pltpu.HBM)


def swap(array, pairs):
    return lax.ppermute(array, "rows", pairs)


def pairs_a(count):
    return [(i, i ^ 1) for i in range(count)]


def pairs_b(count):
    return [p for i in range(1, count - 1, 2) for p in ((i, i + 1), (i + 1, i))]


def column_tiles(block, tile_cols):
    feature = block.shape[1]
    wide = block.astype(F32).reshape(-1, tile_cols, TILE, feature)
    return [wide[:, c].reshape(-1, feature) for c in range(tile_cols)]


def patch_order(columns):
    feature = columns[0].shape[1]
    parts = [x.reshape(-1, 1, TILE, feature) for x in columns]
    return jnp.concatenate(parts, axis=1).reshape(-1, feature)


def slots(heads):
    return [0, 2, 1, 3] if heads == 4 else list(range(heads))


def block_diagonal(tile, heads):
    order = slots(heads)
    feature = tile.shape[1]
    lane_head = lax.broadcasted_iota(jnp.int32, tile.shape, 1) // HEAD
    zero = jnp.zeros_like(tile)
    return jnp.concatenate([jnp.where(lane_head == h, tile, zero) for h in order], axis=0)


def from_transposed(out_t, heads):
    if heads == 4:
        first = lax.broadcasted_iota(jnp.int32, (HEAD, 2 * PATCH), 1) < PATCH
        left = jnp.where(first, out_t[:HEAD, : 2 * PATCH], out_t[2 * HEAD : 3 * HEAD, : 2 * PATCH])
        right = jnp.where(first, out_t[HEAD : 2 * HEAD, 2 * PATCH :], out_t[3 * HEAD :, 2 * PATCH :])
        turned = jnp.concatenate([left, right], axis=0).T
        return jnp.concatenate([turned[:PATCH], turned[PATCH:]], axis=1)
    turned = out_t.T
    lane_head = lax.broadcasted_iota(jnp.int32, (PATCH, heads * HEAD), 1) // HEAD
    total = turned[:PATCH]
    for h in range(1, heads):
        total = jnp.where(lane_head == h, turned[h * PATCH : (h + 1) * PATCH], total)
    return total


def dot_nt(a, b):
    return lax.dot_general(a, b, (((1,), (1,)), ((), ())), preferred_element_type=F32)


def dot_nn(a, b):
    return lax.dot_general(a, b, (((1,), (0,)), ((), ())), preferred_element_type=F32)


def prepare_kernel(k_ref, v_ref, reg_ref, a_ref, b_ref, sems):
    even = lax.rem(lax.axis_index("rows"), 2) == 0
    edge = b_ref.shape[0] // 2
    last = k_ref.shape[0] - edge
    at_a = pl.multiple_of(jnp.where(even, last, 0), edge)
    at_b = pl.multiple_of(jnp.where(even, 0, last), edge)
    moves = []
    for n, ref in enumerate((k_ref, v_ref)):
        moves.append((ref.at[pl.ds(at_a, edge)], a_ref.at[pl.ds(n * edge, edge)]))
        moves.append((ref.at[pl.ds(at_b, edge)], b_ref.at[pl.ds(n * edge, edge)]))
    own = reg_ref.shape[1]
    if a_ref.shape[0] > 2 * edge:
        for n in range(2):
            moves.append((reg_ref.at[n], a_ref.at[pl.ds(2 * edge + n * own, own)]))
    copies = [pltpu.make_async_copy(x, y, sems.at[n]) for n, (x, y) in enumerate(moves)]
    for copy in copies:
        copy.start()
    for copy in copies:
        copy.wait()


def columns_near(c, tile_cols):
    return max(c - 1, 0), min(c + 2, tile_cols)


def own_kernel(tile_cols, split_regs, *refs):
    whole, regs, refs = refs[:4], refs[4 : 7 if split_regs else 5], refs[7 if split_regs else 5 :]
    qbd_ref, gbd_ref, kt_ref, vt_ref, exp_ref, dw_ref, stat_ref, regx_ref, kc_ref, vc_ref = refs[:10]
    held, sems = refs[10:14], refs[14]
    copies = [pltpu.make_async_copy(x, y, sems.at[n]) for n, (x, y) in enumerate(zip(whole, held))]
    for copy in copies:
        copy.start()
    own = regs[0].shape[1]
    for n, ref in enumerate(regs):
        regx_ref[:, n * own : (n + 1) * own] = ref[...]
    for copy in copies:
        copy.wait()
    q_ref, g_ref, k_ref, v_ref = held
    heads = q_ref.shape[1] // HEAD
    line = tile_cols * PATCH
    tile_rows = q_ref.shape[0] // line
    rows = tile_rows * PATCH
    for x_ref, c_ref, t_ref in ((k_ref, kc_ref, kt_ref), (v_ref, vc_ref, vt_ref)):
        for c, column in enumerate(column_tiles(x_ref[...], tile_cols)):
            column = column.astype(BF)
            c_ref[c * rows : (c + 1) * rows] = column
            t_ref[:, c * rows : (c + 1) * rows] = column.T
    for t in range(tile_rows):
        q_cols = column_tiles(q_ref[t * line : (t + 1) * line], tile_cols)
        g_cols = column_tiles(g_ref[t * line : (t + 1) * line], tile_cols)
        for c in range(tile_cols):
            tile = t * tile_cols + c
            q_bd = block_diagonal((q_cols[c] * FACTOR).astype(BF), heads)
            g_bd = block_diagonal(g_cols[c].astype(BF), heads)
            qbd_ref[tile] = q_bd
            gbd_ref[tile] = g_bd
            low, high = columns_near(c, tile_cols)
            near = slice(low * rows, high * rows)
            size = (high - low) * rows
            s = dot_nt(kc_ref[near], q_bd)
            d = dot_nt(vc_ref[near], g_bd).astype(BF)
            top = jnp.max(s, axis=0, keepdims=True)
            e = jnp.exp(s - top)
            exp_ref[tile, :size] = e
            dw_ref[tile, :size] = d
            stat_ref[tile, 0:1] = top
            stat_ref[tile, 1:2] = jnp.sum(e, axis=0, keepdims=True)
            stat_ref[tile, 2:3] = jnp.sum(e * d.astype(F32), axis=0, keepdims=True)


def far_kernel(tile_cols, split_regs, *refs):
    qbd_ref, gbd_ref, stat_ref, regx_ref, a_ref, b_ref = refs[:6]
    refs = refs[6:]
    cut = (a_ref.shape[0] - b_ref.shape[0]) // 2
    final_ref, px_ref, dsx_ref, kx_ref, vx_ref, back_a_ref, back_b_ref = refs[:7]
    reg_outs = refs[7:]
    feature = a_ref.shape[1]
    tile_rows = qbd_ref.shape[0] // tile_cols
    edge = tile_cols * PATCH
    me = lax.axis_index("rows")
    even = lax.rem(me, 2) == 0
    has = (me > 0, me < lax.axis_size("rows") - 1)
    for n, ref in enumerate((kx_ref, vx_ref)):
        from_a = a_ref[n * edge : (n + 1) * edge]
        from_b = b_ref[n * edge : (n + 1) * edge]
        top = column_tiles(jnp.where(even, from_b, from_a), tile_cols)
        bottom = column_tiles(jnp.where(even, from_a, from_b), tile_cols)
        regs = regx_ref[n]
        if split_regs:
            base = 2 * edge + n * cut
            regs = jnp.concatenate([regs, a_ref[base : base + cut]], axis=0)
        for t, halo in enumerate((top, bottom)):
            ref[t, :edge] = jnp.concatenate(halo, axis=0).astype(BF)
            ref[t, edge:] = regs
    dk_reg = dv_reg = None
    dk_halo, dv_halo = [], []
    for t in range(tile_rows):
        dk_t = dv_t = None
        for c in range(tile_cols):
            tile = t * tile_cols + c
            q_bd = qbd_ref[tile]
            g_bd = gbd_ref[tile]
            low, high = columns_near(c, tile_cols)
            s = dot_nt(kx_ref[t], q_bd)
            d = dot_nt(vx_ref[t], g_bd)
            s_near = jnp.where(has[t], s[low * PATCH : high * PATCH], -1e30)
            s = jnp.concatenate([s_near, s[edge:]], axis=0)
            d = jnp.concatenate([d[low * PATCH : high * PATCH], d[edge:]], axis=0)
            d = d.astype(BF).astype(F32)
            own_top = stat_ref[tile, 0:1]
            top = jnp.maximum(own_top, jnp.max(s, axis=0, keepdims=True))
            e = jnp.exp(s - top)
            ratio = jnp.exp(own_top - top)
            inverse = 1.0 / (stat_ref[tile, 1:2] * ratio + jnp.sum(e, axis=0, keepdims=True))
            row_dot = (stat_ref[tile, 2:3] * ratio + jnp.sum(e * d, axis=0, keepdims=True)) * inverse
            final_ref[tile, 0:1] = ratio * inverse
            final_ref[tile, 1:2] = row_dot
            p = e * inverse
            parts = []
            for x in (p, p * (d - row_dot)):
                x = x.astype(BF)
                pieces = [x]
                size = (high - low) * PATCH
                if low > 0 or high < tile_cols:
                    pieces = [x[:size], x[size:]]
                    if high < tile_cols:
                        pieces.insert(1, jnp.zeros(((tile_cols - high) * PATCH, feature), BF))
                    if low > 0:
                        pieces.insert(0, jnp.zeros((low * PATCH, feature), BF))
                parts.append(jnp.concatenate(pieces, axis=0))
            weights, d_scores = parts
            px_ref[tile] = weights
            dsx_ref[tile] = d_scores
            dk = dot_nn(d_scores, q_bd)
            dv = dot_nn(weights, g_bd)
            dk_t = dk if dk_t is None else dk_t + dk
            dv_t = dv if dv_t is None else dv_t + dv
        dk_halo.append(dk_t[:edge])
        dv_halo.append(dv_t[:edge])
        dk_reg = dk_t[edge:] if dk_reg is None else dk_reg + dk_t[edge:]
        dv_reg = dv_t[edge:] if dv_reg is None else dv_reg + dv_t[edge:]
    for n, (halo, reg) in enumerate(((dk_halo, dk_reg), (dv_halo, dv_reg))):
        top, bottom = halo
        back_a_ref[n * edge : (n + 1) * edge] = jnp.where(even, bottom, top).astype(BF)
        back_b_ref[n * edge : (n + 1) * edge] = jnp.where(even, top, bottom).astype(BF)
        if split_regs:
            base = 2 * edge + n * cut
            reg_outs[0][n] = reg[:cut]
            reg_outs[1][n] = reg[cut : 2 * cut].astype(BF)
            reg_outs[2][n] = reg[2 * cut : 3 * cut].astype(BF)
            back_a_ref[base : base + cut] = reg[3 * cut :].astype(BF)
        else:
            reg_outs[0][n] = reg


def rest_kernel(
    tile_cols,
    qbd_ref,
    gbd_ref,
    kt_ref,
    vt_ref,
    exp_ref,
    dw_ref,
    final_ref,
    px_ref,
    dsx_ref,
    kx_ref,
    vx_ref,
    *refs,
):
    if len(refs) > 4:
        own_ref, two_ref, three_ref, *refs = refs
        refs[4][...] = own_ref[...] + two_ref[...].astype(F32) + three_ref[...].astype(F32)
    o_ref, dq_ref, dk_ref, dv_ref = refs[:4]
    feature = kt_ref.shape[0]
    heads = feature // HEAD
    line = tile_cols * PATCH
    tile_rows = qbd_ref.shape[0] // tile_cols
    rows = tile_rows * PATCH
    for t in range(tile_rows):
        kxt = kx_ref[t].T
        vxt = vx_ref[t].T
        o_cols, dq_cols = [], []
        for c in range(tile_cols):
            tile = t * tile_cols + c
            low, high = columns_near(c, tile_cols)
            near = slice(low * rows, high * rows)
            size = (high - low) * rows
            p = exp_ref[tile, :size] * final_ref[tile, 0:1]
            d_scores = (p * (dw_ref[tile, :size].astype(F32) - final_ref[tile, 1:2])).astype(BF)
            weights = p.astype(BF)
            dk = dot_nn(d_scores, qbd_ref[tile])
            dv = dot_nn(weights, gbd_ref[tile])
            first = t == 0
            for ref, value in ((dk_ref, dk), (dv_ref, dv)):
                for x in range(low, high):
                    part = value[(x - low) * rows : (x - low + 1) * rows]
                    if first and (x == c + 1 or (c == 0)):
                        ref[x] = part
                    else:
                        ref[x] += part
            o_t = dot_nn(vt_ref[:, near], weights) + dot_nn(vxt, px_ref[tile])
            dq_t = dot_nn(kt_ref[:, near], d_scores) + dot_nn(kxt, dsx_ref[tile])
            o_cols.append(from_transposed(o_t, heads))
            dq_cols.append(from_transposed(dq_t, heads) * FACTOR)
        o_ref[t * line : (t + 1) * line] = patch_order(o_cols).astype(BF)
        dq_ref[t * line : (t + 1) * line] = patch_order(dq_cols).astype(BF)


def finish_kernel(dk_ref, dv_ref, a_ref, b_ref, *refs, split_regs):
    if split_regs:
        dreg_ref, *refs = refs
    gk_ref, gv_ref = refs[:2]
    me = lax.axis_index("rows")
    even = lax.rem(me, 2) == 0
    has_top = me > 0
    has_bottom = me < lax.axis_size("rows") - 1
    tile_cols = dk_ref.shape[0]
    edge = b_ref.shape[0] // 2
    for n, (acc_ref, out_ref) in enumerate(((dk_ref, gk_ref), (dv_ref, gv_ref))):
        from_a = a_ref[n * edge : (n + 1) * edge]
        from_b = b_ref[n * edge : (n + 1) * edge]
        top = jnp.where(has_top, jnp.where(even, from_b, from_a).astype(F32), 0.0)
        bottom = jnp.where(has_bottom, jnp.where(even, from_a, from_b).astype(F32), 0.0)
        rows = acc_ref.shape[1]
        columns = []
        for c in range(tile_cols):
            high = acc_ref[c, :PATCH] + top[c * PATCH : (c + 1) * PATCH]
            low = acc_ref[c, rows - PATCH :] + bottom[c * PATCH : (c + 1) * PATCH]
            columns.append(jnp.concatenate([high, low], axis=0))
        out_ref[...] = patch_order(columns).astype(BF)
        if split_regs:
            cut = dreg_ref.shape[1]
            base = 2 * edge + n * cut
            refs[2][n] = dreg_ref[n] + a_ref[base : base + cut].astype(F32)


def shape(dims, dtype):
    return jax.ShapeDtypeStruct(dims, dtype)


def call(kernel, name, ins, outs, flops, in_specs=None, scratch=()):
    size = sum(x.size * x.dtype.itemsize for x in ins) + sum(x.size * x.dtype.itemsize for x in outs)
    return pl.pallas_call(
        kernel,
        out_shape=tuple(outs),
        in_specs=in_specs or [VMEM] * len(ins),
        out_specs=(VMEM,) * len(outs),
        scratch_shapes=list(scratch),
        compiler_params=pltpu.CompilerParams(vmem_limit_bytes=24 * 1024 * 1024),
        cost_estimate=pl.CostEstimate(flops=flops, bytes_accessed=size, transcendentals=0),
        name=name,
    )(*ins)


def shards(query, keys, values, registers, cotangent):
    count = lax.axis_size("rows")
    split_regs = count == 4
    tile_cols = query.shape[1] // TILE
    tile_rows = query.shape[0] // TILE
    assert tile_rows == 2
    feature = query.shape[2]
    total = query.shape[0] * query.shape[1]
    edge = tile_cols * PATCH
    own = registers.shape[1]
    reg_count = own * count
    q, k, v, g = (x.reshape(total, feature) for x in (query, keys, values, cotangent))
    extra = 2 * own if split_regs else 0
    two = [(i, i ^ 2) for i in range(count)]
    three = [(i, i ^ 3) for i in range(count)]

    if split_regs:
        regs = (registers, swap(registers, two), swap(registers, three))
    else:
        regs = (lax.all_gather(registers, "rows", axis=1, tiled=True),)
    pay_a, pay_b = call(
        prepare_kernel,
        "prepare",
        (k, v, registers),
        (shape((2 * edge + extra, feature), BF), shape((2 * edge, feature), BF)),
        0,
        in_specs=[HBM] * 3,
        scratch=[pltpu.SemaphoreType.DMA((6,))],
    )
    got_b = swap(pay_b, pairs_b(count))
    got_a = swap(pay_a, pairs_a(count))

    tiles = tile_rows * tile_cols
    rows = tile_rows * PATCH
    most = min(3, tile_cols) * rows
    window = edge + reg_count
    qbd, gbd, kt, vt, exps, dw, stats, regx = call(
        functools.partial(own_kernel, tile_cols, split_regs),
        "own",
        (q, g, k, v) + regs,
        (
            shape((tiles, feature, feature), BF),
            shape((tiles, feature, feature), BF),
            shape((feature, total), BF),
            shape((feature, total), BF),
            shape((tiles, most, feature), F32),
            shape((tiles, most, feature), BF),
            shape((tiles, 8, feature), F32),
            shape((2, len(regs) * regs[0].shape[1], feature), BF),
        ),
        HEAVY,
        in_specs=[HBM] * 4 + [VMEM] * len(regs),
        scratch=[pltpu.VMEM((total, feature), BF)] * 6 + [pltpu.SemaphoreType.DMA((4,))],
    )
    if split_regs:
        reg_shapes = (
            shape((2, own, feature), F32),
            shape((2, own, feature), BF),
            shape((2, own, feature), BF),
        )
    else:
        reg_shapes = (shape((2, reg_count, feature), F32),)
    final, px, dsx, kx, vx, back_a, back_b, *back_regs = call(
        functools.partial(far_kernel, tile_cols, split_regs),
        "far",
        (qbd, gbd, stats, regx, got_a, got_b),
        (
            shape((tiles, 8, feature), F32),
            shape((tiles, window, feature), BF),
            shape((tiles, window, feature), BF),
            shape((tile_rows, window, feature), BF),
            shape((tile_rows, window, feature), BF),
            shape((2 * edge + extra, feature), BF),
            shape((2 * edge, feature), BF),
        )
        + reg_shapes,
        8 * tiles * window * feature * feature,
    )
    back_from_b = swap(back_b, pairs_b(count))
    back_from_a = swap(back_a, pairs_a(count))
    if split_regs:
        rest = (back_regs[0], swap(back_regs[1], two), swap(back_regs[2], three))
        last_shapes = (shape((2, own, feature), F32),)
    else:
        rest = ()
        last_shapes = ()
    attended, grad_query, dk, dv, *reg_part = call(
        functools.partial(rest_kernel, tile_cols),
        "rest",
        (qbd, gbd, kt, vt, exps, dw, final, px, dsx, kx, vx) + rest,
        (
            shape((total, feature), BF),
            shape((total, feature), BF),
            shape((tile_cols, rows, feature), F32),
            shape((tile_cols, rows, feature), F32),
        )
        + last_shapes,
        HEAVY,
    )
    outs = call(
        functools.partial(finish_kernel, split_regs=split_regs),
        "finish",
        (dk, dv, back_from_a, back_from_b) + tuple(reg_part),
        (shape((total, feature), BF), shape((total, feature), BF)) + last_shapes,
        0,
    )
    if split_regs:
        grad_registers = outs[2]
    else:
        grad_registers = lax.psum_scatter(back_regs[0], "rows", scatter_dimension=1, tiled=True)
    whole = query.shape
    return (
        attended.reshape(whole),
        grad_query.reshape(whole),
        outs[0].reshape(whole),
        outs[1].reshape(whole),
        grad_registers,
    )


def solution(mesh):
    slab = P(("groups", "rows"), None, "cols")
    in_specs = (slab, slab, slab, P(None, "rows", "cols"), slab)
    out_specs = (slab, slab, slab, slab, P("groups", "rows", "cols"))
    return jax.shard_map(shards, mesh=mesh, in_specs=in_specs, out_specs=out_specs, check_vma=False)
```

```python
import functools

import jax
import jax.numpy as jnp
from jax import lax
from jax.experimental import pallas as pl
from jax.experimental.pallas import tpu as pltpu
from jax.sharding import PartitionSpec as P

HEAD = 64
TILE = 8
PATCH = TILE * TILE
FACTOR = HEAD ** (-0.5)
HEAVY = 20_000_000_000
BF = jnp.bfloat16
F32 = jnp.float32
VMEM = pl.BlockSpec(memory_space=pltpu.VMEM)
HBM = pl.BlockSpec(memory_space=pltpu.HBM)


def swap(array, pairs):
    return lax.ppermute(array, "rows", pairs)


def pairs_a(count):
    return [(i, i ^ 1) for i in range(count)]


def swap_b(array):
    count, across = lax.axis_size("rows"), lax.axis_size("cols")
    pairs = []
    for row in range(count):
        other = row if row in (0, count - 1) else row + 1 if row % 2 else row - 1
        for col in range(across):
            to = min(col ^ 1, across - 1) if other == row else col
            pairs.append((row * across + col, other * across + to))
    return lax.ppermute(array, ("rows", "cols"), pairs)


def column_tiles(block, tile_cols):
    feature = block.shape[1]
    wide = block.astype(F32).reshape(-1, tile_cols, TILE, feature)
    return [wide[:, c].reshape(-1, feature) for c in range(tile_cols)]


def patch_order(columns):
    feature = columns[0].shape[1]
    parts = [x.reshape(-1, 1, TILE, feature) for x in columns]
    return jnp.concatenate(parts, axis=1).reshape(-1, feature)


def slots(heads):
    return [0, 2, 1, 3] if heads == 4 else list(range(heads))


def block_diagonal(tile, heads):
    order = slots(heads)
    feature = tile.shape[1]
    lane_head = lax.broadcasted_iota(jnp.int32, tile.shape, 1) // HEAD
    zero = jnp.zeros_like(tile)
    return jnp.concatenate([jnp.where(lane_head == h, tile, zero) for h in order], axis=0)


def from_transposed(out_t, heads):
    if heads == 4:
        first = lax.broadcasted_iota(jnp.int32, (HEAD, 2 * PATCH), 1) < PATCH
        left = jnp.where(first, out_t[:HEAD, : 2 * PATCH], out_t[2 * HEAD : 3 * HEAD, : 2 * PATCH])
        right = jnp.where(first, out_t[HEAD : 2 * HEAD, 2 * PATCH :], out_t[3 * HEAD :, 2 * PATCH :])
        turned = jnp.concatenate([left, right], axis=0).T
        return jnp.concatenate([turned[:PATCH], turned[PATCH:]], axis=1)
    turned = out_t.T
    lane_head = lax.broadcasted_iota(jnp.int32, (PATCH, heads * HEAD), 1) // HEAD
    total = turned[:PATCH]
    for h in range(1, heads):
        total = jnp.where(lane_head == h, turned[h * PATCH : (h + 1) * PATCH], total)
    return total


def dot_nt(a, b):
    return lax.dot_general(a, b, (((1,), (1,)), ((), ())), preferred_element_type=F32)


def dot_nn(a, b):
    return lax.dot_general(a, b, (((1,), (0,)), ((), ())), preferred_element_type=F32)


def prepare_kernel(q_ref, g_ref, k_ref, v_ref, reg_ref, *refs):
    a_ref, b_ref, sems = refs[0], refs[1], refs[-1]
    if b_ref.shape[0] > k_ref.shape[0]:
        b_ref[k_ref.shape[0] :] = jnp.zeros((b_ref.shape[0] - k_ref.shape[0], b_ref.shape[1]), BF)
    even = lax.rem(lax.axis_index("rows"), 2) == 0
    edge = k_ref.shape[0] // 2
    last = k_ref.shape[0] - edge
    at_a = pl.multiple_of(jnp.where(even, last, 0), edge)
    at_b = pl.multiple_of(jnp.where(even, 0, last), edge)
    moves = []
    for n, ref in enumerate((k_ref, v_ref)):
        moves.append((ref.at[pl.ds(at_a, edge)], a_ref.at[pl.ds(n * edge, edge)]))
        moves.append((ref.at[pl.ds(at_b, edge)], b_ref.at[pl.ds(n * edge, edge)]))
    own = reg_ref.shape[1]
    if a_ref.shape[0] > 2 * edge:
        for n in range(2):
            moves.append((reg_ref.at[n], a_ref.at[pl.ds(2 * edge + n * own, own)]))
    moves += list(zip((q_ref, g_ref, k_ref, v_ref, reg_ref), refs[2:7]))
    copies = [pltpu.make_async_copy(x, y, sems.at[n]) for n, (x, y) in enumerate(moves)]
    for copy in copies:
        copy.start()
    for copy in copies:
        copy.wait()


def columns_near(c, tile_cols):
    return max(c - 1, 0), min(c + 2, tile_cols)


def own_kernel(
    tile_cols,
    q_ref,
    g_ref,
    k_ref,
    v_ref,
    qbd_ref,
    gbd_ref,
    kt_ref,
    vt_ref,
    exp_ref,
    dw_ref,
    stat_ref,
    kc_ref,
    vc_ref,
):
    heads = q_ref.shape[1] // HEAD
    line = tile_cols * PATCH
    tile_rows = q_ref.shape[0] // line
    rows = tile_rows * PATCH
    for x_ref, c_ref, t_ref in ((k_ref, kc_ref, kt_ref), (v_ref, vc_ref, vt_ref)):
        for c, column in enumerate(column_tiles(x_ref[...], tile_cols)):
            column = column.astype(BF)
            c_ref[c * rows : (c + 1) * rows] = column
            t_ref[:, c * rows : (c + 1) * rows] = column.T
    for t in range(tile_rows):
        q_cols = column_tiles(q_ref[t * line : (t + 1) * line], tile_cols)
        g_cols = column_tiles(g_ref[t * line : (t + 1) * line], tile_cols)
        for c in range(tile_cols):
            tile = t * tile_cols + c
            q_bd = block_diagonal((q_cols[c] * FACTOR).astype(BF), heads)
            g_bd = block_diagonal(g_cols[c].astype(BF), heads)
            qbd_ref[tile] = q_bd
            gbd_ref[tile] = g_bd
            low, high = columns_near(c, tile_cols)
            near = slice(low * rows, high * rows)
            size = (high - low) * rows
            s = dot_nt(kc_ref[near], q_bd)
            d = dot_nt(vc_ref[near], g_bd).astype(BF)
            top = jnp.max(s, axis=0, keepdims=True)
            e = jnp.exp(s - top)
            exp_ref[tile, :size] = e
            dw_ref[tile, :size] = d
            stat_ref[tile, 0:1] = top
            stat_ref[tile, 1:2] = jnp.sum(e, axis=0, keepdims=True)
            stat_ref[tile, 2:3] = jnp.sum(e * d.astype(F32), axis=0, keepdims=True)


def far_kernel(tile_cols, split_regs, *refs):
    qbd_ref, gbd_ref, stat_ref, a_ref, b_ref = refs[:5]
    if split_regs:
        own_ref, two_ref, three_ref = refs[5:8]
        cut = own_ref.shape[1]
        refs = refs[8:]
    else:
        all_ref = refs[5]
        refs = refs[6:]
    final_ref, px_ref, dsx_ref, kx_ref, vx_ref, back_a_ref, back_b_ref = refs[:7]
    reg_outs = refs[7:]
    feature = a_ref.shape[1]
    tile_rows = qbd_ref.shape[0] // tile_cols
    edge = tile_cols * PATCH
    me = lax.axis_index("rows")
    even = lax.rem(me, 2) == 0
    has = (me > 0, me < lax.axis_size("rows") - 1)
    for n, ref in enumerate((kx_ref, vx_ref)):
        from_a = a_ref[n * edge : (n + 1) * edge]
        from_b = b_ref[n * edge : (n + 1) * edge]
        top = column_tiles(jnp.where(even, from_b, from_a), tile_cols)
        bottom = column_tiles(jnp.where(even, from_a, from_b), tile_cols)
        if split_regs:
            base = 2 * edge + n * cut
            regs = jnp.concatenate([own_ref[n], two_ref[n], three_ref[n], a_ref[base : base + cut]], axis=0)
        else:
            regs = all_ref[n]
        for t, halo in enumerate((top, bottom)):
            ref[t, :edge] = jnp.concatenate(halo, axis=0).astype(BF)
            ref[t, edge:] = regs
    if back_b_ref.shape[0] > 2 * edge:
        back_b_ref[2 * edge :] = jnp.zeros((back_b_ref.shape[0] - 2 * edge, feature), BF)
    dk_reg = dv_reg = None
    dk_halo, dv_halo = [], []
    for t in range(tile_rows):
        dk_t = dv_t = None
        for c in range(tile_cols):
            tile = t * tile_cols + c
            q_bd = qbd_ref[tile]
            g_bd = gbd_ref[tile]
            low, high = columns_near(c, tile_cols)
            s = dot_nt(kx_ref[t], q_bd)
            d = dot_nt(vx_ref[t], g_bd)
            s_near = jnp.where(has[t], s[low * PATCH : high * PATCH], -1e30)
            s = jnp.concatenate([s_near, s[edge:]], axis=0)
            d = jnp.concatenate([d[low * PATCH : high * PATCH], d[edge:]], axis=0)
            d = d.astype(BF).astype(F32)
            own_top = stat_ref[tile, 0:1]
            top = jnp.maximum(own_top, jnp.max(s, axis=0, keepdims=True))
            e = jnp.exp(s - top)
            ratio = jnp.exp(own_top - top)
            inverse = 1.0 / (stat_ref[tile, 1:2] * ratio + jnp.sum(e, axis=0, keepdims=True))
            row_dot = (stat_ref[tile, 2:3] * ratio + jnp.sum(e * d, axis=0, keepdims=True)) * inverse
            final_ref[tile, 0:1] = ratio * inverse
            final_ref[tile, 1:2] = row_dot
            p = e * inverse
            parts = []
            for x in (p, p * (d - row_dot)):
                x = x.astype(BF)
                pieces = [x]
                size = (high - low) * PATCH
                if low > 0 or high < tile_cols:
                    pieces = [x[:size], x[size:]]
                    if high < tile_cols:
                        pieces.insert(1, jnp.zeros(((tile_cols - high) * PATCH, feature), BF))
                    if low > 0:
                        pieces.insert(0, jnp.zeros((low * PATCH, feature), BF))
                parts.append(jnp.concatenate(pieces, axis=0))
            weights, d_scores = parts
            px_ref[tile] = weights
            dsx_ref[tile] = d_scores
            dk = dot_nn(d_scores, q_bd)
            dv = dot_nn(weights, g_bd)
            dk_t = dk if dk_t is None else dk_t + dk
            dv_t = dv if dv_t is None else dv_t + dv
        dk_halo.append(dk_t[:edge])
        dv_halo.append(dv_t[:edge])
        dk_reg = dk_t[edge:] if dk_reg is None else dk_reg + dk_t[edge:]
        dv_reg = dv_t[edge:] if dv_reg is None else dv_reg + dv_t[edge:]
    for n, (halo, reg) in enumerate(((dk_halo, dk_reg), (dv_halo, dv_reg))):
        top, bottom = halo
        back_a_ref[n * edge : (n + 1) * edge] = jnp.where(even, bottom, top).astype(BF)
        back_b_ref[n * edge : (n + 1) * edge] = jnp.where(even, top, bottom).astype(BF)
        if split_regs:
            base = 2 * edge + n * cut
            reg_outs[0][n] = reg[:cut]
            reg_outs[1][n] = reg[cut : 2 * cut].astype(BF)
            reg_outs[2][n] = reg[2 * cut : 3 * cut].astype(BF)
            back_a_ref[base : base + cut] = reg[3 * cut :].astype(BF)
        else:
            reg_outs[0][n] = reg


def rest_kernel(
    tile_cols,
    qbd_ref,
    gbd_ref,
    kt_ref,
    vt_ref,
    exp_ref,
    dw_ref,
    final_ref,
    px_ref,
    dsx_ref,
    kx_ref,
    vx_ref,
    *refs,
):
    o_ref, dq_ref, dk_ref, dv_ref = refs[:4]
    feature = kt_ref.shape[0]
    heads = feature // HEAD
    line = tile_cols * PATCH
    tile_rows = qbd_ref.shape[0] // tile_cols
    rows = tile_rows * PATCH
    for t in range(tile_rows):
        kxt = kx_ref[t].T
        vxt = vx_ref[t].T
        o_cols, dq_cols = [], []
        for c in range(tile_cols):
            tile = t * tile_cols + c
            low, high = columns_near(c, tile_cols)
            near = slice(low * rows, high * rows)
            size = (high - low) * rows
            p = exp_ref[tile, :size] * final_ref[tile, 0:1]
            d_scores = (p * (dw_ref[tile, :size].astype(F32) - final_ref[tile, 1:2])).astype(BF)
            weights = p.astype(BF)
            dk = dot_nn(d_scores, qbd_ref[tile])
            dv = dot_nn(weights, gbd_ref[tile])
            first = t == 0
            for ref, value in ((dk_ref, dk), (dv_ref, dv)):
                for x in range(low, high):
                    part = value[(x - low) * rows : (x - low + 1) * rows]
                    if first and (x == c + 1 or (c == 0)):
                        ref[x] = part
                    else:
                        ref[x] += part
            o_t = dot_nn(vt_ref[:, near], weights) + dot_nn(vxt, px_ref[tile])
            dq_t = dot_nn(kt_ref[:, near], d_scores) + dot_nn(kxt, dsx_ref[tile])
            o_cols.append(from_transposed(o_t, heads))
            dq_cols.append(from_transposed(dq_t, heads) * FACTOR)
        o_ref[t * line : (t + 1) * line] = patch_order(o_cols).astype(BF)
        dq_ref[t * line : (t + 1) * line] = patch_order(dq_cols).astype(BF)


def finish_kernel(dk_ref, dv_ref, a_ref, b_ref, *refs, split_regs):
    if split_regs:
        dreg_ref, two_ref, three_ref, *refs = refs
    gk_ref, gv_ref = refs[:2]
    me = lax.axis_index("rows")
    even = lax.rem(me, 2) == 0
    has_top = me > 0
    has_bottom = me < lax.axis_size("rows") - 1
    tile_cols = dk_ref.shape[0]
    edge = tile_cols * PATCH
    for n, (acc_ref, out_ref) in enumerate(((dk_ref, gk_ref), (dv_ref, gv_ref))):
        from_a = a_ref[n * edge : (n + 1) * edge]
        from_b = b_ref[n * edge : (n + 1) * edge]
        top = jnp.where(has_top, jnp.where(even, from_b, from_a).astype(F32), 0.0)
        bottom = jnp.where(has_bottom, jnp.where(even, from_a, from_b).astype(F32), 0.0)
        rows = acc_ref.shape[1]
        columns = []
        for c in range(tile_cols):
            high = acc_ref[c, :PATCH] + top[c * PATCH : (c + 1) * PATCH]
            low = acc_ref[c, rows - PATCH :] + bottom[c * PATCH : (c + 1) * PATCH]
            columns.append(jnp.concatenate([high, low], axis=0))
        out_ref[...] = patch_order(columns).astype(BF)
        if split_regs:
            cut = dreg_ref.shape[1]
            base = 2 * edge + n * cut
            received = a_ref[base : base + cut].astype(F32) + two_ref[n].astype(F32) + three_ref[n].astype(F32)
            refs[2][n] = dreg_ref[n] + received


def shape(dims, dtype):
    return jax.ShapeDtypeStruct(dims, dtype)


def call(kernel, name, ins, outs, flops, in_specs=None, scratch=()):
    size = sum(x.size * x.dtype.itemsize for x in ins) + sum(x.size * x.dtype.itemsize for x in outs)
    return pl.pallas_call(
        kernel,
        out_shape=tuple(outs),
        in_specs=in_specs or [VMEM] * len(ins),
        out_specs=(VMEM,) * len(outs),
        scratch_shapes=list(scratch),
        compiler_params=pltpu.CompilerParams(vmem_limit_bytes=24 * 1024 * 1024),
        cost_estimate=pl.CostEstimate(flops=flops, bytes_accessed=size, transcendentals=0),
        name=name,
    )(*ins)


def shards(query, keys, values, registers, cotangent):
    count = lax.axis_size("rows")
    split_regs = count == 4
    tile_cols = query.shape[1] // TILE
    tile_rows = query.shape[0] // TILE
    assert tile_rows == 2
    feature = query.shape[2]
    total = query.shape[0] * query.shape[1]
    edge = tile_cols * PATCH
    own = registers.shape[1]
    reg_count = own * count
    q, k, v, g = (
        pltpu.with_memory_space_constraint(x.reshape(total, feature), pltpu.HBM)
        for x in (query, keys, values, cotangent)
    )
    extra = 2 * own if split_regs else 0
    pad = 2 * extra
    two = [(i, i ^ 2) for i in range(count)]
    three = [(i, i ^ 3) for i in range(count)]

    registers = pltpu.with_memory_space_constraint(registers, pltpu.HBM)
    pay_a, pay_b, q, g, k, v, reg_held = call(
        prepare_kernel,
        "prepare",
        (q, g, k, v, registers),
        (shape((2 * edge + extra, feature), BF), shape((2 * edge + pad, feature), BF))
        + tuple(shape((total, feature), BF) for _ in range(4))
        + (shape(registers.shape, BF),),
        0,
        in_specs=[HBM] * 5,
        scratch=[pltpu.SemaphoreType.DMA((11,))],
    )
    got_b = swap_b(pay_b)
    got_a = swap(pay_a, pairs_a(count))
    if split_regs:
        regs = (reg_held, swap(reg_held, two), swap(reg_held, three))
    else:
        regs = (lax.all_gather(registers, "rows", axis=1, tiled=True),)

    tiles = tile_rows * tile_cols
    rows = tile_rows * PATCH
    most = min(3, tile_cols) * rows
    window = edge + reg_count
    qbd, gbd, kt, vt, exps, dw, stats = call(
        functools.partial(own_kernel, tile_cols),
        "own",
        (q, g, k, v),
        (
            shape((tiles, feature, feature), BF),
            shape((tiles, feature, feature), BF),
            shape((feature, total), BF),
            shape((feature, total), BF),
            shape((tiles, most, feature), F32),
            shape((tiles, most, feature), BF),
            shape((tiles, 8, feature), F32),
        ),
        600_000_000,
        scratch=[pltpu.VMEM((total, feature), BF)] * 2,
    )
    if split_regs:
        reg_shapes = (
            shape((2, own, feature), F32),
            shape((2, own, feature), BF),
            shape((2, own, feature), BF),
        )
    else:
        reg_shapes = (shape((2, reg_count, feature), F32),)
    final, px, dsx, kx, vx, back_a, back_b, *back_regs = call(
        functools.partial(far_kernel, tile_cols, split_regs),
        "far",
        (qbd, gbd, stats, got_a, got_b) + regs,
        (
            shape((tiles, 8, feature), F32),
            shape((tiles, window, feature), BF),
            shape((tiles, window, feature), BF),
            shape((tile_rows, window, feature), BF),
            shape((tile_rows, window, feature), BF),
            shape((2 * edge + extra, feature), BF),
            shape((2 * edge + pad, feature), BF),
        )
        + reg_shapes,
        8 * tiles * window * feature * feature,
    )
    back_from_b = swap_b(back_b)
    back_from_a = swap(back_a, pairs_a(count))
    if split_regs:
        rest = (back_regs[0], swap(back_regs[1], two), swap(back_regs[2], three))
        last_shapes = (shape((2, own, feature), F32),)
    else:
        rest = ()
        last_shapes = ()
    attended, grad_query, dk, dv = call(
        functools.partial(rest_kernel, tile_cols),
        "rest",
        (qbd, gbd, kt, vt, exps, dw, final, px, dsx, kx, vx),
        (
            shape((total, feature), BF),
            shape((total, feature), BF),
            shape((tile_cols, rows, feature), F32),
            shape((tile_cols, rows, feature), F32),
        ),
        600_000_000,
    )
    outs = call(
        functools.partial(finish_kernel, split_regs=split_regs),
        "finish",
        (dk, dv, back_from_a, back_from_b) + rest,
        (shape((total, feature), BF), shape((total, feature), BF)) + last_shapes,
        0,
    )
    if split_regs:
        grad_registers = outs[2]
    else:
        grad_registers = lax.psum_scatter(back_regs[0], "rows", scatter_dimension=1, tiled=True)
    whole = query.shape
    return (
        attended.reshape(whole),
        grad_query.reshape(whole),
        outs[0].reshape(whole),
        outs[1].reshape(whole),
        grad_registers,
    )


def solution(mesh):
    slab = P(("groups", "rows"), None, "cols")
    in_specs = (slab, slab, slab, P(None, "rows", "cols"), slab)
    out_specs = (slab, slab, slab, slab, P("groups", "rows", "cols"))
    return jax.shard_map(shards, mesh=mesh, in_specs=in_specs, out_specs=out_specs, check_vma=False)
```

```python
import functools

import jax
import jax.numpy as jnp
from jax import lax
from jax.experimental import pallas as pl
from jax.experimental.pallas import tpu as pltpu
from jax.sharding import PartitionSpec as P

HEAD = 64
TILE = 8
PATCH = TILE * TILE
FACTOR = HEAD ** (-0.5)
HEAVY = 20_000_000_000
BF = jnp.bfloat16
F32 = jnp.float32
VMEM = pl.BlockSpec(memory_space=pltpu.VMEM)
HBM = pl.BlockSpec(memory_space=pltpu.HBM)


def swap(array, pairs):
    return lax.ppermute(array, "rows", pairs)


def pairs_a(count):
    return [(i, i ^ 1) for i in range(count)]


def swap_b(array):
    count, across = lax.axis_size("rows"), lax.axis_size("cols")
    pairs = []
    for row in range(count):
        other = row if row in (0, count - 1) else row + 1 if row % 2 else row - 1
        for col in range(across):
            to = min(col ^ 1, across - 1) if other == row else col
            pairs.append((row * across + col, other * across + to))
    return lax.ppermute(array, ("rows", "cols"), pairs)


def column_tiles(block, tile_cols):
    feature = block.shape[1]
    wide = block.astype(F32).reshape(-1, tile_cols, TILE, feature)
    return [wide[:, c].reshape(-1, feature) for c in range(tile_cols)]


def patch_order(columns):
    feature = columns[0].shape[1]
    parts = [x.reshape(-1, 1, TILE, feature) for x in columns]
    return jnp.concatenate(parts, axis=1).reshape(-1, feature)


def slots(heads):
    return [0, 2, 1, 3] if heads == 4 else list(range(heads))


def block_diagonal(tile, heads):
    order = slots(heads)
    feature = tile.shape[1]
    lane_head = lax.broadcasted_iota(jnp.int32, tile.shape, 1) // HEAD
    zero = jnp.zeros_like(tile)
    return jnp.concatenate([jnp.where(lane_head == h, tile, zero) for h in order], axis=0)


def from_transposed(out_t, heads):
    if heads == 4:
        first = lax.broadcasted_iota(jnp.int32, (HEAD, 2 * PATCH), 1) < PATCH
        left = jnp.where(first, out_t[:HEAD, : 2 * PATCH], out_t[2 * HEAD : 3 * HEAD, : 2 * PATCH])
        right = jnp.where(first, out_t[HEAD : 2 * HEAD, 2 * PATCH :], out_t[3 * HEAD :, 2 * PATCH :])
        turned = jnp.concatenate([left, right], axis=0).T
        return jnp.concatenate([turned[:PATCH], turned[PATCH:]], axis=1)
    turned = out_t.T
    lane_head = lax.broadcasted_iota(jnp.int32, (PATCH, heads * HEAD), 1) // HEAD
    total = turned[:PATCH]
    for h in range(1, heads):
        total = jnp.where(lane_head == h, turned[h * PATCH : (h + 1) * PATCH], total)
    return total


def dot_nt(a, b):
    return lax.dot_general(a, b, (((1,), (1,)), ((), ())), preferred_element_type=F32)


def dot_nn(a, b):
    return lax.dot_general(a, b, (((1,), (0,)), ((), ())), preferred_element_type=F32)


def copy_all(moves, sems):
    copies = [pltpu.make_async_copy(x, y, sems.at[n]) for n, (x, y) in enumerate(moves)]
    for copy in copies:
        copy.start()
    for copy in copies:
        copy.wait()


def prepare_kernel(k_ref, v_ref, reg_ref, a_ref, b_ref, held_ref, sems):
    if b_ref.shape[0] > k_ref.shape[0]:
        b_ref[k_ref.shape[0] :] = jnp.zeros((b_ref.shape[0] - k_ref.shape[0], b_ref.shape[1]), BF)
    even = lax.rem(lax.axis_index("rows"), 2) == 0
    edge = k_ref.shape[0] // 2
    last = k_ref.shape[0] - edge
    at_a = pl.multiple_of(jnp.where(even, last, 0), edge)
    at_b = pl.multiple_of(jnp.where(even, 0, last), edge)
    moves = []
    for n, ref in enumerate((k_ref, v_ref)):
        moves.append((ref.at[pl.ds(at_b, edge)], b_ref.at[pl.ds(n * edge, edge)]))
        moves.append((ref.at[pl.ds(at_a, edge)], a_ref.at[pl.ds(n * edge, edge)]))
    own = reg_ref.shape[1]
    if a_ref.shape[0] > 2 * edge:
        for n in range(2):
            moves.append((reg_ref.at[n], a_ref.at[pl.ds(2 * edge + n * own, own)]))
    moves.append((reg_ref, held_ref))
    copy_all(moves, sems)


def columns_near(c, tile_cols):
    return max(c - 1, 0), min(c + 2, tile_cols)


def own_kernel(tile_cols, *refs):
    qbd_ref, gbd_ref, kt_ref, vt_ref, exp_ref, dw_ref, stat_ref, kc_ref, vc_ref = refs[4:13]
    q_ref, g_ref, k_ref, v_ref = held = refs[13:17]
    copy_all(list(zip(refs[:4], held)), refs[17])
    heads = q_ref.shape[1] // HEAD
    line = tile_cols * PATCH
    tile_rows = q_ref.shape[0] // line
    rows = tile_rows * PATCH
    for x_ref, c_ref, t_ref in ((k_ref, kc_ref, kt_ref), (v_ref, vc_ref, vt_ref)):
        for c, column in enumerate(column_tiles(x_ref[...], tile_cols)):
            column = column.astype(BF)
            c_ref[c * rows : (c + 1) * rows] = column
            t_ref[:, c * rows : (c + 1) * rows] = column.T
    for t in range(tile_rows):
        q_cols = column_tiles(q_ref[t * line : (t + 1) * line], tile_cols)
        g_cols = column_tiles(g_ref[t * line : (t + 1) * line], tile_cols)
        for c in range(tile_cols):
            tile = t * tile_cols + c
            q_bd = block_diagonal((q_cols[c] * FACTOR).astype(BF), heads)
            g_bd = block_diagonal(g_cols[c].astype(BF), heads)
            qbd_ref[tile] = q_bd
            gbd_ref[tile] = g_bd
            low, high = columns_near(c, tile_cols)
            near = slice(low * rows, high * rows)
            size = (high - low) * rows
            s = dot_nt(kc_ref[near], q_bd)
            d = dot_nt(vc_ref[near], g_bd).astype(BF)
            top = jnp.max(s, axis=0, keepdims=True)
            e = jnp.exp(s - top)
            exp_ref[tile, :size] = e
            dw_ref[tile, :size] = d
            stat_ref[tile, 0:1] = top
            stat_ref[tile, 1:2] = jnp.sum(e, axis=0, keepdims=True)
            stat_ref[tile, 2:3] = jnp.sum(e * d.astype(F32), axis=0, keepdims=True)


def halo_kernel(tile_cols, qbd_ref, gbd_ref, stat_ref, a_ref, b_ref, exp_ref, dw_ref, sum_ref, kx_ref, vx_ref):
    tile_rows = qbd_ref.shape[0] // tile_cols
    edge = tile_cols * PATCH
    me = lax.axis_index("rows")
    even = lax.rem(me, 2) == 0
    has = (me > 0, me < lax.axis_size("rows") - 1)
    for n, ref in enumerate((kx_ref, vx_ref)):
        from_a = a_ref[n * edge : (n + 1) * edge]
        from_b = b_ref[n * edge : (n + 1) * edge]
        for t, halo in enumerate((jnp.where(even, from_b, from_a), jnp.where(even, from_a, from_b))):
            ref[t] = jnp.concatenate(column_tiles(halo, tile_cols), axis=0).astype(BF)
    for t in range(tile_rows):
        for c in range(tile_cols):
            tile = t * tile_cols + c
            low, high = columns_near(c, tile_cols)
            near = slice(low * PATCH, high * PATCH)
            s = jnp.where(has[t], dot_nt(kx_ref[t, near], qbd_ref[tile]), -1e30)
            d = dot_nt(vx_ref[t, near], gbd_ref[tile]).astype(BF)
            own_top = stat_ref[tile, 0:1]
            top = jnp.maximum(own_top, jnp.max(s, axis=0, keepdims=True))
            e = jnp.exp(s - top)
            ratio = jnp.exp(own_top - top)
            exp_ref[tile, near] = e
            dw_ref[tile, near] = d
            sum_ref[tile, 0:1] = top
            sum_ref[tile, 1:2] = stat_ref[tile, 1:2] * ratio + jnp.sum(e, axis=0, keepdims=True)
            sum_ref[tile, 2:3] = stat_ref[tile, 2:3] * ratio + jnp.sum(e * d.astype(F32), axis=0, keepdims=True)
            sum_ref[tile, 3:4] = ratio


def far_kernel(tile_cols, split_regs, *refs):
    qbd_ref, gbd_ref, exp_ref, dw_ref, sum_ref, a_ref = refs[:6]
    edge = tile_cols * PATCH
    regs = []
    if split_regs:
        own_ref, two_ref, three_ref = refs[6:9]
        refs = refs[9:]
        cut = own_ref.shape[1]
        for n in range(2):
            base = 2 * edge + n * cut
            regs.append(jnp.concatenate([own_ref[n], two_ref[n], three_ref[n], a_ref[base : base + cut]], axis=0))
    else:
        regs = [refs[6][n] for n in range(2)]
        refs = refs[7:]
    final_ref, px_ref, dsx_ref, kr_ref, vr_ref, back_a_ref, back_b_ref = refs[:7]
    reg_outs = refs[7:]
    kr_ref[...], vr_ref[...] = regs
    feature = a_ref.shape[1]
    tile_rows = qbd_ref.shape[0] // tile_cols
    even = lax.rem(lax.axis_index("rows"), 2) == 0
    if back_b_ref.shape[0] > 2 * edge:
        back_b_ref[2 * edge :] = jnp.zeros((back_b_ref.shape[0] - 2 * edge, feature), BF)
    dk_reg = dv_reg = None
    dk_halo, dv_halo = [], []
    for t in range(tile_rows):
        dk_t = dv_t = None
        for c in range(tile_cols):
            tile = t * tile_cols + c
            q_bd = qbd_ref[tile]
            g_bd = gbd_ref[tile]
            low, high = columns_near(c, tile_cols)
            near = slice(low * PATCH, high * PATCH)
            s = dot_nt(kr_ref[...], q_bd)
            d = dot_nt(vr_ref[...], g_bd).astype(BF).astype(F32)
            old_top = sum_ref[tile, 0:1]
            top = jnp.maximum(old_top, jnp.max(s, axis=0, keepdims=True))
            e = jnp.exp(s - top)
            ratio = jnp.exp(old_top - top)
            inverse = 1.0 / (sum_ref[tile, 1:2] * ratio + jnp.sum(e, axis=0, keepdims=True))
            row_dot = (sum_ref[tile, 2:3] * ratio + jnp.sum(e * d, axis=0, keepdims=True)) * inverse
            scale = ratio * inverse
            final_ref[tile, 0:1] = sum_ref[tile, 3:4] * scale
            final_ref[tile, 1:2] = row_dot
            p_near = exp_ref[tile, near] * scale
            p_reg = e * inverse
            ds_near = p_near * (dw_ref[tile, near].astype(F32) - row_dot)
            ds_reg = p_reg * (d - row_dot)
            parts = []
            for x_near, x_reg in ((p_near, p_reg), (ds_near, ds_reg)):
                pieces = [x_near.astype(BF), x_reg.astype(BF)]
                if high < tile_cols:
                    pieces.insert(1, jnp.zeros(((tile_cols - high) * PATCH, feature), BF))
                if low > 0:
                    pieces.insert(0, jnp.zeros((low * PATCH, feature), BF))
                parts.append(jnp.concatenate(pieces, axis=0))
            weights, d_scores = parts
            px_ref[tile] = weights
            dsx_ref[tile] = d_scores
            dk = dot_nn(d_scores, q_bd)
            dv = dot_nn(weights, g_bd)
            dk_t = dk if dk_t is None else dk_t + dk
            dv_t = dv if dv_t is None else dv_t + dv
        dk_halo.append(dk_t[:edge])
        dv_halo.append(dv_t[:edge])
        dk_reg = dk_t[edge:] if dk_reg is None else dk_reg + dk_t[edge:]
        dv_reg = dv_t[edge:] if dv_reg is None else dv_reg + dv_t[edge:]
    for n, (halo, reg) in enumerate(((dk_halo, dk_reg), (dv_halo, dv_reg))):
        top, bottom = halo
        back_a_ref[n * edge : (n + 1) * edge] = jnp.where(even, bottom, top).astype(BF)
        back_b_ref[n * edge : (n + 1) * edge] = jnp.where(even, top, bottom).astype(BF)
        if split_regs:
            base = 2 * edge + n * cut
            reg_outs[0][n] = reg[:cut]
            reg_outs[1][n] = reg[cut : 2 * cut].astype(BF)
            reg_outs[2][n] = reg[2 * cut : 3 * cut].astype(BF)
            back_a_ref[base : base + cut] = reg[3 * cut :].astype(BF)
        else:
            reg_outs[0][n] = reg


def rest_kernel(
    tile_cols,
    qbd_ref,
    gbd_ref,
    kt_ref,
    vt_ref,
    exp_ref,
    dw_ref,
    final_ref,
    px_ref,
    dsx_ref,
    kx_ref,
    vx_ref,
    kr_ref,
    vr_ref,
    *refs,
):
    o_ref, dq_ref, dk_ref, dv_ref = refs[:4]
    feature = kt_ref.shape[0]
    heads = feature // HEAD
    line = tile_cols * PATCH
    tile_rows = qbd_ref.shape[0] // tile_cols
    rows = tile_rows * PATCH
    for t in range(tile_rows):
        kxt = jnp.concatenate([kx_ref[t], kr_ref[...]], axis=0).T
        vxt = jnp.concatenate([vx_ref[t], vr_ref[...]], axis=0).T
        o_cols, dq_cols = [], []
        for c in range(tile_cols):
            tile = t * tile_cols + c
            low, high = columns_near(c, tile_cols)
            near = slice(low * rows, high * rows)
            size = (high - low) * rows
            p = exp_ref[tile, :size] * final_ref[tile, 0:1]
            d_scores = (p * (dw_ref[tile, :size].astype(F32) - final_ref[tile, 1:2])).astype(BF)
            weights = p.astype(BF)
            dk = dot_nn(d_scores, qbd_ref[tile])
            dv = dot_nn(weights, gbd_ref[tile])
            first = t == 0
            for ref, value in ((dk_ref, dk), (dv_ref, dv)):
                for x in range(low, high):
                    part = value[(x - low) * rows : (x - low + 1) * rows]
                    if first and (x == c + 1 or (c == 0)):
                        ref[x] = part
                    else:
                        ref[x] += part
            o_t = dot_nn(vt_ref[:, near], weights) + dot_nn(vxt, px_ref[tile])
            dq_t = dot_nn(kt_ref[:, near], d_scores) + dot_nn(kxt, dsx_ref[tile])
            o_cols.append(from_transposed(o_t, heads))
            dq_cols.append(from_transposed(dq_t, heads) * FACTOR)
        o_ref[t * line : (t + 1) * line] = patch_order(o_cols).astype(BF)
        dq_ref[t * line : (t + 1) * line] = patch_order(dq_cols).astype(BF)


def registers_kernel(part_ref, three_ref, two_ref, out_ref):
    out_ref[...] = part_ref[...] + two_ref[...].astype(F32) + three_ref[...].astype(F32)


def finish_kernel(split_regs, dk_ref, dv_ref, a_ref, b_ref, *refs):
    if split_regs:
        own_ref, gk_ref, gv_ref, part_ref = refs
        cut = own_ref.shape[1]
        base = a_ref.shape[0] - 2 * cut
        for n in range(2):
            part_ref[n] = own_ref[n] + a_ref[base + n * cut : base + (n + 1) * cut].astype(F32)
    else:
        gk_ref, gv_ref = refs
    me = lax.axis_index("rows")
    even = lax.rem(me, 2) == 0
    has_top = me > 0
    has_bottom = me < lax.axis_size("rows") - 1
    tile_cols = dk_ref.shape[0]
    edge = tile_cols * PATCH
    for n, (acc_ref, out_ref) in enumerate(((dk_ref, gk_ref), (dv_ref, gv_ref))):
        from_a = a_ref[n * edge : (n + 1) * edge]
        from_b = b_ref[n * edge : (n + 1) * edge]
        top = jnp.where(has_top, jnp.where(even, from_b, from_a).astype(F32), 0.0)
        bottom = jnp.where(has_bottom, jnp.where(even, from_a, from_b).astype(F32), 0.0)
        rows = acc_ref.shape[1]
        columns = []
        for c in range(tile_cols):
            high = acc_ref[c, :PATCH] + top[c * PATCH : (c + 1) * PATCH]
            low = acc_ref[c, rows - PATCH :] + bottom[c * PATCH : (c + 1) * PATCH]
            columns.append(jnp.concatenate([high, low], axis=0))
        out_ref[...] = patch_order(columns).astype(BF)


def shape(dims, dtype):
    return jax.ShapeDtypeStruct(dims, dtype)


def call(kernel, name, ins, outs, flops, in_specs=None, scratch=()):
    size = sum(x.size * x.dtype.itemsize for x in ins) + sum(x.size * x.dtype.itemsize for x in outs)
    return pl.pallas_call(
        kernel,
        out_shape=tuple(outs),
        in_specs=in_specs or [VMEM] * len(ins),
        out_specs=(VMEM,) * len(outs),
        scratch_shapes=list(scratch),
        compiler_params=pltpu.CompilerParams(vmem_limit_bytes=24 * 1024 * 1024),
        cost_estimate=pl.CostEstimate(flops=flops, bytes_accessed=size, transcendentals=0),
        name=name,
    )(*ins)


def shards(query, keys, values, registers, cotangent):
    count = lax.axis_size("rows")
    split_regs = count == 4
    tile_cols = query.shape[1] // TILE
    tile_rows = query.shape[0] // TILE
    assert tile_rows == 2
    feature = query.shape[2]
    total = query.shape[0] * query.shape[1]
    edge = tile_cols * PATCH
    own = registers.shape[1]
    reg_count = own * count
    q, k, v, g = (
        pltpu.with_memory_space_constraint(x.reshape(total, feature), pltpu.HBM)
        for x in (query, keys, values, cotangent)
    )
    extra = 2 * own if split_regs else 0
    pad = 2 * extra
    two = [(i, i ^ 2) for i in range(count)]
    three = [(i, i ^ 3) for i in range(count)]

    registers = pltpu.with_memory_space_constraint(registers, pltpu.HBM)
    pay_a, pay_b, reg_held = call(
        prepare_kernel,
        "prepare",
        (k, v, registers),
        (
            shape((2 * edge + extra, feature), BF),
            shape((2 * edge + pad, feature), BF),
            shape(registers.shape, BF),
        ),
        0,
        in_specs=[HBM] * 3,
        scratch=[pltpu.SemaphoreType.DMA((7,))],
    )
    got_b = swap_b(pay_b)
    got_a = swap(pay_a, pairs_a(count))
    if split_regs:
        regs = (reg_held, swap(reg_held, two), swap(reg_held, three))
    else:
        regs = (lax.all_gather(registers, "rows", axis=1, tiled=True),)

    tiles = tile_rows * tile_cols
    rows = tile_rows * PATCH
    most = min(3, tile_cols) * rows
    window = edge + reg_count
    qbd, gbd, kt, vt, exps, dw, stats = call(
        functools.partial(own_kernel, tile_cols),
        "own",
        (q, g, k, v),
        (
            shape((tiles, feature, feature), BF),
            shape((tiles, feature, feature), BF),
            shape((feature, total), BF),
            shape((feature, total), BF),
            shape((tiles, most, feature), F32),
            shape((tiles, most, feature), BF),
            shape((tiles, 8, feature), F32),
        ),
        600_000_000,
        in_specs=[HBM] * 4,
        scratch=[pltpu.VMEM((total, feature), BF)] * 6 + [pltpu.SemaphoreType.DMA((4,))],
    )
    if split_regs:
        reg_shapes = (
            shape((2, own, feature), F32),
            shape((2, own, feature), BF),
            shape((2, own, feature), BF),
        )
    else:
        reg_shapes = (shape((2, reg_count, feature), F32),)
    halo_exps, halo_dw, sums, kx, vx = call(
        functools.partial(halo_kernel, tile_cols),
        "halo",
        (qbd, gbd, stats, got_a, got_b),
        (
            shape((tiles, edge, feature), F32),
            shape((tiles, edge, feature), BF),
            shape((tiles, 8, feature), F32),
            shape((tile_rows, edge, feature), BF),
            shape((tile_rows, edge, feature), BF),
        ),
        4 * tiles * edge * feature * feature,
    )
    final, px, dsx, kr, vr, back_a, back_b, *back_regs = call(
        functools.partial(far_kernel, tile_cols, split_regs),
        "far",
        (qbd, gbd, halo_exps, halo_dw, sums, got_a) + regs,
        (
            shape((tiles, 8, feature), F32),
            shape((tiles, window, feature), BF),
            shape((tiles, window, feature), BF),
            shape((reg_count, feature), BF),
            shape((reg_count, feature), BF),
            shape((2 * edge + extra, feature), BF),
            shape((2 * edge + pad, feature), BF),
        )
        + reg_shapes,
        8 * tiles * window * feature * feature,
    )
    back_from_b = swap_b(back_b)
    back_from_a = swap(back_a, pairs_a(count))
    attended, grad_query, dk, dv = call(
        functools.partial(rest_kernel, tile_cols),
        "rest",
        (qbd, gbd, kt, vt, exps, dw, final, px, dsx, kx, vx, kr, vr),
        (
            shape((total, feature), BF),
            shape((total, feature), BF),
            shape((tile_cols, rows, feature), F32),
            shape((tile_cols, rows, feature), F32),
        ),
        600_000_000,
    )
    mine = (back_regs[0],) if split_regs else ()
    grad_keys, grad_values, *part = call(
        functools.partial(finish_kernel, split_regs),
        "finish",
        (dk, dv, back_from_a, back_from_b) + mine,
        (shape((total, feature), BF), shape((total, feature), BF)) + tuple(shape(x.shape, F32) for x in mine),
        0,
    )
    if split_regs:
        (grad_registers,) = call(
            registers_kernel,
            "registers",
            (part[0], swap(back_regs[2], three), swap(back_regs[1], two)),
            (shape((2, own, feature), F32),),
            0,
        )
    else:
        grad_registers = lax.psum_scatter(back_regs[0], "rows", scatter_dimension=1, tiled=True)
    whole = query.shape
    return (
        attended.reshape(whole),
        grad_query.reshape(whole),
        grad_keys.reshape(whole),
        grad_values.reshape(whole),
        grad_registers,
    )


def solution(mesh):
    slab = P(("groups", "rows"), None, "cols")
    in_specs = (slab, slab, slab, P(None, "rows", "cols"), slab)
    out_specs = (slab, slab, slab, slab, P("groups", "rows", "cols"))
    return jax.shard_map(shards, mesh=mesh, in_specs=in_specs, out_specs=out_specs, check_vma=False)
```

```python
import functools

import jax
import jax.numpy as jnp
from jax import lax
from jax.experimental import pallas as pl
from jax.experimental.pallas import tpu as pltpu
from jax.sharding import PartitionSpec as P

HEAD = 64
TILE = 8
PATCH = TILE * TILE
FACTOR = HEAD ** (-0.5)
BF = jnp.bfloat16
F32 = jnp.float32
VMEM = pl.BlockSpec(memory_space=pltpu.VMEM)
HBM = pl.BlockSpec(memory_space=pltpu.HBM)


def swap(array, pairs):
    return lax.ppermute(array, "rows", pairs)


def pairs_a(count):
    return [(i, i ^ 1) for i in range(count)]


def swap_b(array):
    count, across = lax.axis_size("rows"), lax.axis_size("cols")
    pairs = []
    for row in range(count):
        other = row if row in (0, count - 1) else row + 1 if row % 2 else row - 1
        for col in range(across):
            to = min(col ^ 1, across - 1) if other == row else col
            pairs.append((row * across + col, other * across + to))
    return lax.ppermute(array, ("rows", "cols"), pairs)


def column_tiles(block, tile_cols):
    feature = block.shape[1]
    wide = block.astype(F32).reshape(-1, tile_cols, TILE, feature)
    return [wide[:, c].reshape(-1, feature) for c in range(tile_cols)]


def patch_order(columns):
    feature = columns[0].shape[1]
    parts = [x.reshape(-1, 1, TILE, feature) for x in columns]
    return jnp.concatenate(parts, axis=1).reshape(-1, feature)


def slots(heads):
    return [0, 2, 1, 3] if heads == 4 else list(range(heads))


def block_diagonal(tile, heads):
    order = slots(heads)
    feature = tile.shape[1]
    lane_head = lax.broadcasted_iota(jnp.int32, tile.shape, 1) // HEAD
    zero = jnp.zeros_like(tile)
    return jnp.concatenate([jnp.where(lane_head == h, tile, zero) for h in order], axis=0)


def from_transposed(out_t, heads):
    if heads == 4:
        first = lax.broadcasted_iota(jnp.int32, (HEAD, 2 * PATCH), 1) < PATCH
        left = jnp.where(first, out_t[:HEAD, : 2 * PATCH], out_t[2 * HEAD : 3 * HEAD, : 2 * PATCH])
        right = jnp.where(first, out_t[HEAD : 2 * HEAD, 2 * PATCH :], out_t[3 * HEAD :, 2 * PATCH :])
        turned = jnp.concatenate([left, right], axis=0).T
        return jnp.concatenate([turned[:PATCH], turned[PATCH:]], axis=1)
    turned = out_t.T
    lane_head = lax.broadcasted_iota(jnp.int32, (PATCH, heads * HEAD), 1) // HEAD
    total = turned[:PATCH]
    for h in range(1, heads):
        total = jnp.where(lane_head == h, turned[h * PATCH : (h + 1) * PATCH], total)
    return total


def dot_nt(a, b):
    return lax.dot_general(a, b, (((1,), (1,)), ((), ())), preferred_element_type=F32)


def dot_nn(a, b):
    return lax.dot_general(a, b, (((1,), (0,)), ((), ())), preferred_element_type=F32)


def copy_all(moves, sems):
    copies = [pltpu.make_async_copy(x, y, sems.at[n]) for n, (x, y) in enumerate(moves)]
    for copy in copies:
        copy.start()
    for copy in copies:
        copy.wait()


def prepare_kernel(k_ref, v_ref, reg_ref, a_ref, b_ref, held_ref, sems):
    even = lax.rem(lax.axis_index("rows"), 2) == 0
    edge = k_ref.shape[0] // 2
    last = k_ref.shape[0] - edge
    at_a = pl.multiple_of(jnp.where(even, last, 0), edge)
    at_b = pl.multiple_of(jnp.where(even, 0, last), edge)
    moves = []
    for n, ref in enumerate((k_ref, v_ref)):
        moves.append((ref.at[pl.ds(at_b, edge)], b_ref.at[pl.ds(n * edge, edge)]))
        moves.append((ref.at[pl.ds(at_a, edge)], a_ref.at[pl.ds(n * edge, edge)]))
    own = reg_ref.shape[1]
    if a_ref.shape[0] > 2 * edge:
        for n in range(2):
            moves.append((reg_ref.at[n], a_ref.at[pl.ds(2 * edge + n * own, own)]))
    moves.append((reg_ref, held_ref))
    copy_all(moves, sems)


def columns_near(c, tile_cols):
    return max(c - 1, 0), min(c + 2, tile_cols)


def own_kernel(tile_cols, *refs):
    qbd_ref, gbd_ref, kt_ref, vt_ref, exp_ref, dw_ref, stat_ref, kc_ref, vc_ref = refs[4:13]
    q_ref, g_ref, k_ref, v_ref = held = refs[13:17]
    copy_all(list(zip(refs[:4], held)), refs[17])
    heads = q_ref.shape[1] // HEAD
    line = tile_cols * PATCH
    tile_rows = q_ref.shape[0] // line
    rows = tile_rows * PATCH
    for x_ref, c_ref, t_ref in ((k_ref, kc_ref, kt_ref), (v_ref, vc_ref, vt_ref)):
        for c, column in enumerate(column_tiles(x_ref[...], tile_cols)):
            column = column.astype(BF)
            c_ref[c * rows : (c + 1) * rows] = column
            t_ref[:, c * rows : (c + 1) * rows] = column.T
    for t in range(tile_rows):
        q_cols = column_tiles(q_ref[t * line : (t + 1) * line], tile_cols)
        g_cols = column_tiles(g_ref[t * line : (t + 1) * line], tile_cols)
        for c in range(tile_cols):
            tile = t * tile_cols + c
            q_bd = block_diagonal((q_cols[c] * FACTOR).astype(BF), heads)
            g_bd = block_diagonal(g_cols[c].astype(BF), heads)
            qbd_ref[tile] = q_bd
            gbd_ref[tile] = g_bd
            low, high = columns_near(c, tile_cols)
            near = slice(low * rows, high * rows)
            size = (high - low) * rows
            s = dot_nt(kc_ref[near], q_bd)
            d = dot_nt(vc_ref[near], g_bd).astype(BF)
            top = jnp.max(s, axis=0, keepdims=True)
            e = jnp.exp(s - top)
            exp_ref[tile, :size] = e
            dw_ref[tile, :size] = d
            stat_ref[tile, 0:1] = top
            stat_ref[tile, 1:2] = jnp.sum(e, axis=0, keepdims=True)
            stat_ref[tile, 2:3] = jnp.sum(e * d.astype(F32), axis=0, keepdims=True)


def tile_row_of(group):
    odd = lax.rem(lax.axis_index("rows"), 2)
    return odd if group == 0 else 1 - odd


def halo_kernel(tile_cols, group, qbd_ref, gbd_ref, stat_ref, halo_ref, exp_ref, dw_ref, sum_ref, kx_ref, vx_ref):
    edge = tile_cols * PATCH
    me = lax.axis_index("rows")
    inner = (me > 0) & (me < lax.axis_size("rows") - 1)
    for n, ref in enumerate((kx_ref, vx_ref)):
        ref[...] = jnp.concatenate(column_tiles(halo_ref[n * edge : (n + 1) * edge], tile_cols), axis=0).astype(BF)
    for c in range(tile_cols):
        tile = tile_row_of(group) * tile_cols + c
        low, high = columns_near(c, tile_cols)
        near = slice(low * PATCH, high * PATCH)
        s = dot_nt(kx_ref[near], qbd_ref[tile])
        if group == 0:
            s = jnp.where(inner, s, -1e30)
        d = dot_nt(vx_ref[near], gbd_ref[tile]).astype(BF)
        own_top = stat_ref[tile, 0:1]
        top = jnp.maximum(own_top, jnp.max(s, axis=0, keepdims=True))
        e = jnp.exp(s - top)
        ratio = jnp.exp(own_top - top)
        exp_ref[c, near] = e
        dw_ref[c, near] = d
        sum_ref[c, 0:1] = top
        sum_ref[c, 1:2] = stat_ref[tile, 1:2] * ratio + jnp.sum(e, axis=0, keepdims=True)
        sum_ref[c, 2:3] = stat_ref[tile, 2:3] * ratio + jnp.sum(e * d.astype(F32), axis=0, keepdims=True)
        sum_ref[c, 3:4] = ratio


def far_kernel(tile_cols, split_regs, *refs):
    qbd_ref, gbd_ref = refs[:2]
    halos, a_ref = (refs[2:5], refs[5:8]), refs[8]
    refs = refs[3:]
    edge = tile_cols * PATCH
    regs = []
    if split_regs:
        own_ref, two_ref, three_ref = refs[6:9]
        refs = refs[9:]
        cut = own_ref.shape[1]
        for n in range(2):
            base = 2 * edge + n * cut
            regs.append(jnp.concatenate([own_ref[n], two_ref[n], three_ref[n], a_ref[base : base + cut]], axis=0))
    else:
        regs = [refs[6][n] for n in range(2)]
        refs = refs[7:]
    final_ref, px_ref, dsx_ref, kr_ref, vr_ref, back_a_ref, back_b_ref = refs[:7]
    reg_outs = refs[7:]
    kr_ref[...], vr_ref[...] = regs
    feature = a_ref.shape[1]
    dk_reg = dv_reg = None
    for group, (exp_ref, dw_ref, sum_ref) in enumerate(halos):
        dk_t = dv_t = None
        for c in range(tile_cols):
            tile = tile_row_of(group) * tile_cols + c
            q_bd = qbd_ref[tile]
            g_bd = gbd_ref[tile]
            low, high = columns_near(c, tile_cols)
            near = slice(low * PATCH, high * PATCH)
            s = dot_nt(kr_ref[...], q_bd)
            d = dot_nt(vr_ref[...], g_bd).astype(BF).astype(F32)
            old_top = sum_ref[c, 0:1]
            top = jnp.maximum(old_top, jnp.max(s, axis=0, keepdims=True))
            e = jnp.exp(s - top)
            ratio = jnp.exp(old_top - top)
            inverse = 1.0 / (sum_ref[c, 1:2] * ratio + jnp.sum(e, axis=0, keepdims=True))
            row_dot = (sum_ref[c, 2:3] * ratio + jnp.sum(e * d, axis=0, keepdims=True)) * inverse
            scale = ratio * inverse
            final_ref[tile, 0:1] = sum_ref[c, 3:4] * scale
            final_ref[tile, 1:2] = row_dot
            p_near = exp_ref[c, near] * scale
            p_reg = e * inverse
            ds_near = p_near * (dw_ref[c, near].astype(F32) - row_dot)
            ds_reg = p_reg * (d - row_dot)
            parts = []
            for x_near, x_reg in ((p_near, p_reg), (ds_near, ds_reg)):
                pieces = [x_near.astype(BF), x_reg.astype(BF)]
                if high < tile_cols:
                    pieces.insert(1, jnp.zeros(((tile_cols - high) * PATCH, feature), BF))
                if low > 0:
                    pieces.insert(0, jnp.zeros((low * PATCH, feature), BF))
                parts.append(jnp.concatenate(pieces, axis=0))
            weights, d_scores = parts
            px_ref[tile] = weights
            dsx_ref[tile] = d_scores
            dk = dot_nn(d_scores, q_bd)
            dv = dot_nn(weights, g_bd)
            dk_t = dk if dk_t is None else dk_t + dk
            dv_t = dv if dv_t is None else dv_t + dv
        back_ref = (back_b_ref, back_a_ref)[group]
        back_ref[:edge] = dk_t[:edge].astype(BF)
        back_ref[edge : 2 * edge] = dv_t[:edge].astype(BF)
        dk_reg = dk_t[edge:] if dk_reg is None else dk_reg + dk_t[edge:]
        dv_reg = dv_t[edge:] if dv_reg is None else dv_reg + dv_t[edge:]
    for n, reg in enumerate((dk_reg, dv_reg)):
        if split_regs:
            base = 2 * edge + n * cut
            reg_outs[0][n] = reg[:cut]
            reg_outs[1][n] = reg[cut : 2 * cut].astype(BF)
            reg_outs[2][n] = reg[2 * cut : 3 * cut].astype(BF)
            back_a_ref[base : base + cut] = reg[3 * cut :].astype(BF)
        else:
            reg_outs[0][n] = reg


def rest_kernel(
    tile_cols,
    qbd_ref,
    gbd_ref,
    kt_ref,
    vt_ref,
    exp_ref,
    dw_ref,
    final_ref,
    px_ref,
    dsx_ref,
    kb_ref,
    vb_ref,
    ka_ref,
    va_ref,
    kr_ref,
    vr_ref,
    *refs,
):
    o_ref, dq_ref, dk_ref, dv_ref = refs[:4]
    feature = kt_ref.shape[0]
    heads = feature // HEAD
    line = tile_cols * PATCH
    tile_rows = qbd_ref.shape[0] // tile_cols
    rows = tile_rows * PATCH
    for group, (kx_ref, vx_ref) in enumerate(((kb_ref, vb_ref), (ka_ref, va_ref))):
        t = tile_row_of(group)
        kxt = jnp.concatenate([kx_ref[...], kr_ref[...]], axis=0).T
        vxt = jnp.concatenate([vx_ref[...], vr_ref[...]], axis=0).T
        o_cols, dq_cols = [], []
        for c in range(tile_cols):
            tile = t * tile_cols + c
            low, high = columns_near(c, tile_cols)
            near = slice(low * rows, high * rows)
            size = (high - low) * rows
            p = exp_ref[tile, :size] * final_ref[tile, 0:1]
            d_scores = (p * (dw_ref[tile, :size].astype(F32) - final_ref[tile, 1:2])).astype(BF)
            weights = p.astype(BF)
            dk = dot_nn(d_scores, qbd_ref[tile])
            dv = dot_nn(weights, gbd_ref[tile])
            first = group == 0
            for ref, value in ((dk_ref, dk), (dv_ref, dv)):
                for x in range(low, high):
                    part = value[(x - low) * rows : (x - low + 1) * rows]
                    if first and (x == c + 1 or (c == 0)):
                        ref[x] = part
                    else:
                        ref[x] += part
            o_t = dot_nn(vt_ref[:, near], weights) + dot_nn(vxt, px_ref[tile])
            dq_t = dot_nn(kt_ref[:, near], d_scores) + dot_nn(kxt, dsx_ref[tile])
            o_cols.append(from_transposed(o_t, heads))
            dq_cols.append(from_transposed(dq_t, heads) * FACTOR)
        lines = pl.ds(pl.multiple_of(t * line, line), line)
        o_ref[lines] = patch_order(o_cols).astype(BF)
        dq_ref[lines] = patch_order(dq_cols).astype(BF)


def registers_kernel(part_ref, three_ref, two_ref, out_ref):
    out_ref[...] = part_ref[...] + two_ref[...].astype(F32) + three_ref[...].astype(F32)


def finish_kernel(split_regs, dk_ref, dv_ref, a_ref, b_ref, *refs):
    if split_regs:
        own_ref, gk_ref, gv_ref, part_ref = refs
        cut = own_ref.shape[1]
        base = a_ref.shape[0] - 2 * cut
        for n in range(2):
            part_ref[n] = own_ref[n] + a_ref[base + n * cut : base + (n + 1) * cut].astype(F32)
    else:
        gk_ref, gv_ref = refs
    me = lax.axis_index("rows")
    even = lax.rem(me, 2) == 0
    has_top = me > 0
    has_bottom = me < lax.axis_size("rows") - 1
    tile_cols = dk_ref.shape[0]
    edge = tile_cols * PATCH
    for n, (acc_ref, out_ref) in enumerate(((dk_ref, gk_ref), (dv_ref, gv_ref))):
        from_a = a_ref[n * edge : (n + 1) * edge]
        from_b = b_ref[n * edge : (n + 1) * edge]
        top = jnp.where(has_top, jnp.where(even, from_b, from_a).astype(F32), 0.0)
        bottom = jnp.where(has_bottom, jnp.where(even, from_a, from_b).astype(F32), 0.0)
        rows = acc_ref.shape[1]
        columns = []
        for c in range(tile_cols):
            high = acc_ref[c, :PATCH] + top[c * PATCH : (c + 1) * PATCH]
            low = acc_ref[c, rows - PATCH :] + bottom[c * PATCH : (c + 1) * PATCH]
            columns.append(jnp.concatenate([high, low], axis=0))
        out_ref[...] = patch_order(columns).astype(BF)


def shape(dims, dtype):
    return jax.ShapeDtypeStruct(dims, dtype)


def call(kernel, name, ins, outs, flops, in_specs=None, scratch=()):
    size = sum(x.size * x.dtype.itemsize for x in ins) + sum(x.size * x.dtype.itemsize for x in outs)
    return pl.pallas_call(
        kernel,
        out_shape=tuple(outs),
        in_specs=in_specs or [VMEM] * len(ins),
        out_specs=(VMEM,) * len(outs),
        scratch_shapes=list(scratch),
        compiler_params=pltpu.CompilerParams(vmem_limit_bytes=24 * 1024 * 1024),
        cost_estimate=pl.CostEstimate(flops=flops, bytes_accessed=size, transcendentals=0),
        name=name,
    )(*ins)


def shards(query, keys, values, registers, cotangent):
    count = lax.axis_size("rows")
    split_regs = count == 4
    tile_cols = query.shape[1] // TILE
    tile_rows = query.shape[0] // TILE
    assert tile_rows == 2
    feature = query.shape[2]
    total = query.shape[0] * query.shape[1]
    edge = tile_cols * PATCH
    own = registers.shape[1]
    reg_count = own * count
    q, k, v, g = (
        pltpu.with_memory_space_constraint(x.reshape(total, feature), pltpu.HBM)
        for x in (query, keys, values, cotangent)
    )
    extra = 2 * own if split_regs else 0
    two = [(i, i ^ 2) for i in range(count)]
    three = [(i, i ^ 3) for i in range(count)]

    registers = pltpu.with_memory_space_constraint(registers, pltpu.HBM)
    pay_a, pay_b, reg_held = call(
        prepare_kernel,
        "prepare",
        (k, v, registers),
        (
            shape((2 * edge + extra, feature), BF),
            shape((2 * edge, feature), BF),
            shape(registers.shape, BF),
        ),
        0,
        in_specs=[HBM] * 3,
        scratch=[pltpu.SemaphoreType.DMA((7,))],
    )
    got_b = swap_b(pay_b)
    got_a = swap(pay_a, pairs_a(count))
    if split_regs:
        regs = (reg_held, swap(reg_held, two), swap(reg_held, three))
    else:
        regs = (lax.all_gather(registers, "rows", axis=1, tiled=True),)

    tiles = tile_rows * tile_cols
    rows = tile_rows * PATCH
    most = min(3, tile_cols) * rows
    window = edge + reg_count
    qbd, gbd, kt, vt, exps, dw, stats = call(
        functools.partial(own_kernel, tile_cols),
        "own",
        (q, g, k, v),
        (
            shape((tiles, feature, feature), BF),
            shape((tiles, feature, feature), BF),
            shape((feature, total), BF),
            shape((feature, total), BF),
            shape((tiles, most, feature), F32),
            shape((tiles, most, feature), BF),
            shape((tiles, 8, feature), F32),
        ),
        600_000_000,
        in_specs=[HBM] * 4,
        scratch=[pltpu.VMEM((total, feature), BF)] * 6 + [pltpu.SemaphoreType.DMA((4,))],
    )
    if split_regs:
        reg_shapes = (
            shape((2, own, feature), F32),
            shape((2, own, feature), BF),
            shape((2, own, feature), BF),
        )
    else:
        reg_shapes = (shape((2, reg_count, feature), F32),)
    halos = []
    for group, got in enumerate((got_b, got_a)):
        halos.append(
            call(
                functools.partial(halo_kernel, tile_cols, group),
                "halo",
                (qbd, gbd, stats, got),
                (
                    shape((tile_cols, edge, feature), F32),
                    shape((tile_cols, edge, feature), BF),
                    shape((tile_cols, 8, feature), F32),
                    shape((edge, feature), BF),
                    shape((edge, feature), BF),
                ),
                32 * tile_cols * edge * feature * feature,
            )
        )
    final, px, dsx, kr, vr, back_a, back_b, *back_regs = call(
        functools.partial(far_kernel, tile_cols, split_regs),
        "far",
        (qbd, gbd) + tuple(halos[0][:3]) + tuple(halos[1][:3]) + (got_a,) + regs,
        (
            shape((tiles, 8, feature), F32),
            shape((tiles, window, feature), BF),
            shape((tiles, window, feature), BF),
            shape((reg_count, feature), BF),
            shape((reg_count, feature), BF),
            shape((2 * edge + extra, feature), BF),
            shape((2 * edge, feature), BF),
        )
        + reg_shapes,
        8 * tiles * window * feature * feature,
    )
    back_from_b = swap_b(back_b)
    back_from_a = swap(back_a, pairs_a(count))
    attended, grad_query, dk, dv = call(
        functools.partial(rest_kernel, tile_cols),
        "rest",
        (qbd, gbd, kt, vt, exps, dw, final, px, dsx) + tuple(halos[0][3:]) + tuple(halos[1][3:]) + (kr, vr),
        (
            shape((total, feature), BF),
            shape((total, feature), BF),
            shape((tile_cols, rows, feature), F32),
            shape((tile_cols, rows, feature), F32),
        ),
        600_000_000,
    )
    mine = (back_regs[0],) if split_regs else ()
    grad_keys, grad_values, *part = call(
        functools.partial(finish_kernel, split_regs),
        "finish",
        (dk, dv, back_from_a, back_from_b) + mine,
        (shape((total, feature), BF), shape((total, feature), BF)) + tuple(shape(x.shape, F32) for x in mine),
        0,
    )
    if split_regs:
        (grad_registers,) = call(
            registers_kernel,
            "registers",
            (part[0], swap(back_regs[2], three), swap(back_regs[1], two)),
            (shape((2, own, feature), F32),),
            0,
        )
    else:
        grad_registers = lax.psum_scatter(back_regs[0], "rows", scatter_dimension=1, tiled=True)
    whole = query.shape
    return (
        attended.reshape(whole),
        grad_query.reshape(whole),
        grad_keys.reshape(whole),
        grad_values.reshape(whole),
        grad_registers,
    )


def solution(mesh):
    slab = P(("groups", "rows"), None, "cols")
    in_specs = (slab, slab, slab, P(None, "rows", "cols"), slab)
    out_specs = (slab, slab, slab, slab, P("groups", "rows", "cols"))
    return jax.shard_map(shards, mesh=mesh, in_specs=in_specs, out_specs=out_specs, check_vma=False)
```

```python
import functools

import jax
import jax.numpy as jnp
from jax import lax
from jax.experimental import pallas as pl
from jax.experimental.pallas import tpu as pltpu
from jax.sharding import PartitionSpec as P

HEAD = 64
TILE = 8
PATCH = TILE * TILE
FACTOR = HEAD ** (-0.5)
BF = jnp.bfloat16
F32 = jnp.float32
VMEM = pl.BlockSpec(memory_space=pltpu.VMEM)
HBM = pl.BlockSpec(memory_space=pltpu.HBM)


def swap(array, pairs):
    return lax.ppermute(array, "rows", pairs)


def pairs_a(count):
    return [(i, i ^ 1) for i in range(count)]


def swap_b(array):
    count, across = lax.axis_size("rows"), lax.axis_size("cols")
    pairs = []
    for row in range(count):
        other = row if row in (0, count - 1) else row + 1 if row % 2 else row - 1
        for col in range(across):
            to = min(col ^ 1, across - 1) if other == row else col
            pairs.append((row * across + col, other * across + to))
    return lax.ppermute(array, ("rows", "cols"), pairs)


def column_tiles(block, tile_cols):
    feature = block.shape[1]
    wide = block.astype(F32).reshape(-1, tile_cols, TILE, feature)
    return [wide[:, c].reshape(-1, feature) for c in range(tile_cols)]


def patch_order(columns):
    feature = columns[0].shape[1]
    parts = [x.reshape(-1, 1, TILE, feature) for x in columns]
    return jnp.concatenate(parts, axis=1).reshape(-1, feature)


def slots(heads):
    return [0, 2, 1, 3] if heads == 4 else list(range(heads))


def block_diagonal(tile, heads):
    order = slots(heads)
    feature = tile.shape[1]
    lane_head = lax.broadcasted_iota(jnp.int32, tile.shape, 1) // HEAD
    zero = jnp.zeros_like(tile)
    return jnp.concatenate([jnp.where(lane_head == h, tile, zero) for h in order], axis=0)


def from_transposed(out_t, heads):
    if heads == 4:
        first = lax.broadcasted_iota(jnp.int32, (HEAD, 2 * PATCH), 1) < PATCH
        left = jnp.where(first, out_t[:HEAD, : 2 * PATCH], out_t[2 * HEAD : 3 * HEAD, : 2 * PATCH])
        right = jnp.where(first, out_t[HEAD : 2 * HEAD, 2 * PATCH :], out_t[3 * HEAD :, 2 * PATCH :])
        turned = jnp.concatenate([left, right], axis=0).T
        return jnp.concatenate([turned[:PATCH], turned[PATCH:]], axis=1)
    turned = out_t.T
    lane_head = lax.broadcasted_iota(jnp.int32, (PATCH, heads * HEAD), 1) // HEAD
    total = turned[:PATCH]
    for h in range(1, heads):
        total = jnp.where(lane_head == h, turned[h * PATCH : (h + 1) * PATCH], total)
    return total


def dot_nt(a, b):
    return lax.dot_general(a, b, (((1,), (1,)), ((), ())), preferred_element_type=F32)


def dot_nn(a, b):
    return lax.dot_general(a, b, (((1,), (0,)), ((), ())), preferred_element_type=F32)


def copy_all(moves, sems):
    copies = [pltpu.make_async_copy(x, y, sems.at[n]) for n, (x, y) in enumerate(moves)]
    for copy in copies:
        copy.start()
    for copy in copies:
        copy.wait()


def prepare_kernel(k_ref, v_ref, reg_ref, a_ref, b_ref, held_ref, sems):
    even = lax.rem(lax.axis_index("rows"), 2) == 0
    edge = k_ref.shape[0] // 2
    last = k_ref.shape[0] - edge
    at_a = pl.multiple_of(jnp.where(even, last, 0), edge)
    at_b = pl.multiple_of(jnp.where(even, 0, last), edge)
    moves = []
    for n, ref in enumerate((k_ref, v_ref)):
        moves.append((ref.at[pl.ds(at_b, edge)], b_ref.at[pl.ds(n * edge, edge)]))
        moves.append((ref.at[pl.ds(at_a, edge)], a_ref.at[pl.ds(n * edge, edge)]))
    own = reg_ref.shape[1]
    if a_ref.shape[0] > 2 * edge:
        for n in range(2):
            moves.append((reg_ref.at[n], a_ref.at[pl.ds(2 * edge + n * own, own)]))
    moves.append((reg_ref, held_ref))
    copy_all(moves, sems)


def columns_near(c, tile_cols):
    return max(c - 1, 0), min(c + 2, tile_cols)


def own_kernel(tile_cols, *refs):
    qbd_ref, gbd_ref, kt_ref, vt_ref, exp_ref, dw_ref, stat_ref, kc_ref, vc_ref = refs[4:13]
    q_ref, g_ref, k_ref, v_ref = held = refs[13:17]
    copy_all(list(zip(refs[:4], held)), refs[17])
    heads = q_ref.shape[1] // HEAD
    line = tile_cols * PATCH
    tile_rows = q_ref.shape[0] // line
    rows = tile_rows * PATCH
    for x_ref, c_ref, t_ref in ((k_ref, kc_ref, kt_ref), (v_ref, vc_ref, vt_ref)):
        for c, column in enumerate(column_tiles(x_ref[...], tile_cols)):
            column = column.astype(BF)
            c_ref[c * rows : (c + 1) * rows] = column
            t_ref[:, c * rows : (c + 1) * rows] = column.T
    for t in range(tile_rows):
        q_cols = column_tiles(q_ref[t * line : (t + 1) * line], tile_cols)
        g_cols = column_tiles(g_ref[t * line : (t + 1) * line], tile_cols)
        for c in range(tile_cols):
            tile = t * tile_cols + c
            q_bd = block_diagonal((q_cols[c] * FACTOR).astype(BF), heads)
            g_bd = block_diagonal(g_cols[c].astype(BF), heads)
            qbd_ref[tile] = q_bd
            gbd_ref[tile] = g_bd
            low, high = columns_near(c, tile_cols)
            near = slice(low * rows, high * rows)
            size = (high - low) * rows
            s = dot_nt(kc_ref[near], q_bd)
            d = dot_nt(vc_ref[near], g_bd).astype(BF)
            top = jnp.max(s, axis=0, keepdims=True)
            e = jnp.exp(s - top)
            exp_ref[tile, :size] = e
            dw_ref[tile, :size] = d
            stat_ref[tile, 0:1] = top
            stat_ref[tile, 1:2] = jnp.sum(e, axis=0, keepdims=True)
            stat_ref[tile, 2:3] = jnp.sum(e * d.astype(F32), axis=0, keepdims=True)


def tile_row_of(group):
    odd = lax.rem(lax.axis_index("rows"), 2)
    return odd if group == 0 else 1 - odd


def halo_kernel(tile_cols, group, qbd_ref, gbd_ref, stat_ref, halo_ref, exp_ref, dw_ref, sum_ref, kx_ref, vx_ref):
    edge = tile_cols * PATCH
    me = lax.axis_index("rows")
    inner = (me > 0) & (me < lax.axis_size("rows") - 1)
    for n, ref in enumerate((kx_ref, vx_ref)):
        ref[...] = jnp.concatenate(column_tiles(halo_ref[n * edge : (n + 1) * edge], tile_cols), axis=0).astype(BF)
    for c in range(tile_cols):
        tile = tile_row_of(group) * tile_cols + c
        low, high = columns_near(c, tile_cols)
        near = slice(low * PATCH, high * PATCH)
        s = dot_nt(kx_ref[near], qbd_ref[tile])
        if group == 0:
            s = jnp.where(inner, s, -1e30)
        d = dot_nt(vx_ref[near], gbd_ref[tile]).astype(BF)
        own_top = stat_ref[tile, 0:1]
        top = jnp.maximum(own_top, jnp.max(s, axis=0, keepdims=True))
        e = jnp.exp(s - top)
        ratio = jnp.exp(own_top - top)
        exp_ref[c, near] = e
        dw_ref[c, near] = d
        sum_ref[c, 0:1] = top
        sum_ref[c, 1:2] = stat_ref[tile, 1:2] * ratio + jnp.sum(e, axis=0, keepdims=True)
        sum_ref[c, 2:3] = stat_ref[tile, 2:3] * ratio + jnp.sum(e * d.astype(F32), axis=0, keepdims=True)
        sum_ref[c, 3:4] = ratio


def far_kernel(tile_cols, split_regs, *refs):
    qbd_ref, gbd_ref = refs[:2]
    halos, a_ref = (refs[2:5], refs[5:8]), refs[8]
    refs = refs[3:]
    edge = tile_cols * PATCH
    regs = []
    if split_regs:
        own_ref, two_ref, three_ref = refs[6:9]
        refs = refs[9:]
        cut = own_ref.shape[1]
        for n in range(2):
            base = 2 * edge + n * cut
            regs.append(jnp.concatenate([own_ref[n], two_ref[n], three_ref[n], a_ref[base : base + cut]], axis=0))
    else:
        regs = [refs[6][n] for n in range(2)]
        refs = refs[7:]
    final_ref, px_ref, dsx_ref, kr_ref, vr_ref, back_a_ref, back_b_ref = refs[:7]
    reg_outs = refs[7:]
    kr_ref[...], vr_ref[...] = regs
    feature = a_ref.shape[1]
    places = [(group, c) for group in range(2) for c in range(tile_cols)]
    tiles = [tile_row_of(group) * tile_cols + c for group, c in places]
    scores = [dot_nt(kr_ref[...], qbd_ref[tile]) for tile in tiles]
    grads = [dot_nt(vr_ref[...], gbd_ref[tile]).astype(BF).astype(F32) for tile in tiles]
    parts = []
    for n, (group, c) in enumerate(places):
        sum_ref = halos[group][2]
        s, d = scores[n], grads[n]
        old_top = sum_ref[c, 0:1]
        top = jnp.maximum(old_top, jnp.max(s, axis=0, keepdims=True))
        e = jnp.exp(s - top)
        ratio = jnp.exp(old_top - top)
        inverse = 1.0 / (sum_ref[c, 1:2] * ratio + jnp.sum(e, axis=0, keepdims=True))
        row_dot = (sum_ref[c, 2:3] * ratio + jnp.sum(e * d, axis=0, keepdims=True)) * inverse
        scale = ratio * inverse
        final_ref[n, 0:1] = sum_ref[c, 3:4] * scale
        final_ref[n, 1:2] = row_dot
        p = e * inverse
        parts.append((scale, row_dot, p.astype(BF), (p * (d - row_dot)).astype(BF)))
    for n, (group, c) in enumerate(places):
        exp_ref, dw_ref, _ = halos[group]
        scale, row_dot, p_reg, ds_reg = parts[n]
        low, high = columns_near(c, tile_cols)
        near = slice(low * PATCH, high * PATCH)
        p = exp_ref[c, near] * scale
        px_ref[n, near] = p.astype(BF)
        dsx_ref[n, near] = (p * (dw_ref[c, near].astype(F32) - row_dot)).astype(BF)
        px_ref[n, edge:] = p_reg
        dsx_ref[n, edge:] = ds_reg
        for ref in (px_ref, dsx_ref):
            if low > 0:
                ref[n, : low * PATCH] = jnp.zeros((low * PATCH, feature), BF)
            if high < tile_cols:
                ref[n, high * PATCH : edge] = jnp.zeros(((tile_cols - high) * PATCH, feature), BF)
    dk_reg = dv_reg = None
    for group in range(2):
        dk_t = dv_t = None
        for c in range(tile_cols):
            n = group * tile_cols + c
            dk = dot_nn(dsx_ref[n], qbd_ref[tiles[n]])
            dv = dot_nn(px_ref[n], gbd_ref[tiles[n]])
            dk_t = dk if dk_t is None else dk_t + dk
            dv_t = dv if dv_t is None else dv_t + dv
        back_ref = (back_b_ref, back_a_ref)[group]
        back_ref[:edge] = dk_t[:edge].astype(BF)
        back_ref[edge : 2 * edge] = dv_t[:edge].astype(BF)
        dk_reg = dk_t[edge:] if dk_reg is None else dk_reg + dk_t[edge:]
        dv_reg = dv_t[edge:] if dv_reg is None else dv_reg + dv_t[edge:]
    for n, reg in enumerate((dk_reg, dv_reg)):
        if split_regs:
            base = 2 * edge + n * cut
            reg_outs[0][n] = reg[:cut]
            reg_outs[1][n] = reg[cut : 2 * cut].astype(BF)
            reg_outs[2][n] = reg[2 * cut : 3 * cut].astype(BF)
            back_a_ref[base : base + cut] = reg[3 * cut :].astype(BF)
        else:
            reg_outs[0][n] = reg


def rest_kernel(
    tile_cols,
    qbd_ref,
    gbd_ref,
    kt_ref,
    vt_ref,
    exp_ref,
    dw_ref,
    final_ref,
    px_ref,
    dsx_ref,
    kb_ref,
    vb_ref,
    ka_ref,
    va_ref,
    kr_ref,
    vr_ref,
    *refs,
):
    o_ref, dq_ref, dk_ref, dv_ref = refs[:4]
    feature = kt_ref.shape[0]
    heads = feature // HEAD
    line = tile_cols * PATCH
    tile_rows = qbd_ref.shape[0] // tile_cols
    rows = tile_rows * PATCH
    for group, (kx_ref, vx_ref) in enumerate(((kb_ref, vb_ref), (ka_ref, va_ref))):
        t = tile_row_of(group)
        kxt = jnp.concatenate([kx_ref[...], kr_ref[...]], axis=0).T
        vxt = jnp.concatenate([vx_ref[...], vr_ref[...]], axis=0).T
        o_cols, dq_cols = [], []
        for c in range(tile_cols):
            tile = t * tile_cols + c
            n = group * tile_cols + c
            low, high = columns_near(c, tile_cols)
            near = slice(low * rows, high * rows)
            size = (high - low) * rows
            p = exp_ref[tile, :size] * final_ref[n, 0:1]
            d_scores = (p * (dw_ref[tile, :size].astype(F32) - final_ref[n, 1:2])).astype(BF)
            weights = p.astype(BF)
            dk = dot_nn(d_scores, qbd_ref[tile])
            dv = dot_nn(weights, gbd_ref[tile])
            first = group == 0
            for ref, value in ((dk_ref, dk), (dv_ref, dv)):
                for x in range(low, high):
                    part = value[(x - low) * rows : (x - low + 1) * rows]
                    if first and (x == c + 1 or (c == 0)):
                        ref[x] = part
                    else:
                        ref[x] += part
            o_t = dot_nn(vt_ref[:, near], weights) + dot_nn(vxt, px_ref[n])
            dq_t = dot_nn(kt_ref[:, near], d_scores) + dot_nn(kxt, dsx_ref[n])
            o_cols.append(from_transposed(o_t, heads))
            dq_cols.append(from_transposed(dq_t, heads) * FACTOR)
        lines = pl.ds(pl.multiple_of(t * line, line), line)
        o_ref[lines] = patch_order(o_cols).astype(BF)
        dq_ref[lines] = patch_order(dq_cols).astype(BF)


def registers_kernel(part_ref, three_ref, two_ref, out_ref):
    out_ref[...] = part_ref[...] + two_ref[...].astype(F32) + three_ref[...].astype(F32)


def finish_kernel(split_regs, dk_ref, dv_ref, a_ref, b_ref, *refs):
    if split_regs:
        own_ref, gk_ref, gv_ref, part_ref = refs
        cut = own_ref.shape[1]
        base = a_ref.shape[0] - 2 * cut
        for n in range(2):
            part_ref[n] = own_ref[n] + a_ref[base + n * cut : base + (n + 1) * cut].astype(F32)
    else:
        gk_ref, gv_ref = refs
    me = lax.axis_index("rows")
    even = lax.rem(me, 2) == 0
    has_top = me > 0
    has_bottom = me < lax.axis_size("rows") - 1
    tile_cols = dk_ref.shape[0]
    edge = tile_cols * PATCH
    for n, (acc_ref, out_ref) in enumerate(((dk_ref, gk_ref), (dv_ref, gv_ref))):
        from_a = a_ref[n * edge : (n + 1) * edge]
        from_b = b_ref[n * edge : (n + 1) * edge]
        top = jnp.where(has_top, jnp.where(even, from_b, from_a).astype(F32), 0.0)
        bottom = jnp.where(has_bottom, jnp.where(even, from_a, from_b).astype(F32), 0.0)
        rows = acc_ref.shape[1]
        columns = []
        for c in range(tile_cols):
            high = acc_ref[c, :PATCH] + top[c * PATCH : (c + 1) * PATCH]
            low = acc_ref[c, rows - PATCH :] + bottom[c * PATCH : (c + 1) * PATCH]
            columns.append(jnp.concatenate([high, low], axis=0))
        out_ref[...] = patch_order(columns).astype(BF)


def shape(dims, dtype):
    return jax.ShapeDtypeStruct(dims, dtype)


def call(kernel, name, ins, outs, flops, in_specs=None, scratch=()):
    size = sum(x.size * x.dtype.itemsize for x in ins) + sum(x.size * x.dtype.itemsize for x in outs)
    return pl.pallas_call(
        kernel,
        out_shape=tuple(outs),
        in_specs=in_specs or [VMEM] * len(ins),
        out_specs=(VMEM,) * len(outs),
        scratch_shapes=list(scratch),
        compiler_params=pltpu.CompilerParams(vmem_limit_bytes=24 * 1024 * 1024),
        cost_estimate=pl.CostEstimate(flops=flops, bytes_accessed=size, transcendentals=0),
        name=name,
    )(*ins)


def shards(query, keys, values, registers, cotangent):
    count = lax.axis_size("rows")
    split_regs = count == 4
    tile_cols = query.shape[1] // TILE
    tile_rows = query.shape[0] // TILE
    assert tile_rows == 2
    feature = query.shape[2]
    total = query.shape[0] * query.shape[1]
    edge = tile_cols * PATCH
    own = registers.shape[1]
    reg_count = own * count
    q, k, v, g = (
        pltpu.with_memory_space_constraint(x.reshape(total, feature), pltpu.HBM)
        for x in (query, keys, values, cotangent)
    )
    extra = 2 * own if split_regs else 0
    two = [(i, i ^ 2) for i in range(count)]
    three = [(i, i ^ 3) for i in range(count)]

    registers = pltpu.with_memory_space_constraint(registers, pltpu.HBM)
    pay_a, pay_b, reg_held = call(
        prepare_kernel,
        "prepare",
        (k, v, registers),
        (
            shape((2 * edge + extra, feature), BF),
            shape((2 * edge, feature), BF),
            shape(registers.shape, BF),
        ),
        0,
        in_specs=[HBM] * 3,
        scratch=[pltpu.SemaphoreType.DMA((7,))],
    )
    got_b = swap_b(pay_b)
    got_a = swap(pay_a, pairs_a(count))
    if split_regs:
        regs = (reg_held, swap(reg_held, two), swap(reg_held, three))
    else:
        regs = (lax.all_gather(registers, "rows", axis=1, tiled=True),)

    tiles = tile_rows * tile_cols
    rows = tile_rows * PATCH
    most = min(3, tile_cols) * rows
    window = edge + reg_count
    qbd, gbd, kt, vt, exps, dw, stats = call(
        functools.partial(own_kernel, tile_cols),
        "own",
        (q, g, k, v),
        (
            shape((tiles, feature, feature), BF),
            shape((tiles, feature, feature), BF),
            shape((feature, total), BF),
            shape((feature, total), BF),
            shape((tiles, most, feature), F32),
            shape((tiles, most, feature), BF),
            shape((tiles, 8, feature), F32),
        ),
        600_000_000,
        in_specs=[HBM] * 4,
        scratch=[pltpu.VMEM((total, feature), BF)] * 6 + [pltpu.SemaphoreType.DMA((4,))],
    )
    if split_regs:
        reg_shapes = (
            shape((2, own, feature), F32),
            shape((2, own, feature), BF),
            shape((2, own, feature), BF),
        )
    else:
        reg_shapes = (shape((2, reg_count, feature), F32),)
    halos = []
    for group, got in enumerate((got_b, got_a)):
        halos.append(
            call(
                functools.partial(halo_kernel, tile_cols, group),
                "halo",
                (qbd, gbd, stats, got),
                (
                    shape((tile_cols, edge, feature), F32),
                    shape((tile_cols, edge, feature), BF),
                    shape((tile_cols, 8, feature), F32),
                    shape((edge, feature), BF),
                    shape((edge, feature), BF),
                ),
                32 * tile_cols * edge * feature * feature,
            )
        )
    final, px, dsx, kr, vr, back_a, back_b, *back_regs = call(
        functools.partial(far_kernel, tile_cols, split_regs),
        "far",
        (qbd, gbd) + tuple(halos[0][:3]) + tuple(halos[1][:3]) + (got_a,) + regs,
        (
            shape((tiles, 8, feature), F32),
            shape((tiles, window, feature), BF),
            shape((tiles, window, feature), BF),
            shape((reg_count, feature), BF),
            shape((reg_count, feature), BF),
            shape((2 * edge + extra, feature), BF),
            shape((2 * edge, feature), BF),
        )
        + reg_shapes,
        8 * tiles * window * feature * feature,
    )
    back_from_b = swap_b(back_b)
    back_from_a = swap(back_a, pairs_a(count))
    attended, grad_query, dk, dv = call(
        functools.partial(rest_kernel, tile_cols),
        "rest",
        (qbd, gbd, kt, vt, exps, dw, final, px, dsx) + tuple(halos[0][3:]) + tuple(halos[1][3:]) + (kr, vr),
        (
            shape((total, feature), BF),
            shape((total, feature), BF),
            shape((tile_cols, rows, feature), F32),
            shape((tile_cols, rows, feature), F32),
        ),
        600_000_000,
    )
    mine = (back_regs[0],) if split_regs else ()
    grad_keys, grad_values, *part = call(
        functools.partial(finish_kernel, split_regs),
        "finish",
        (dk, dv, back_from_a, back_from_b) + mine,
        (shape((total, feature), BF), shape((total, feature), BF)) + tuple(shape(x.shape, F32) for x in mine),
        0,
    )
    if split_regs:
        (grad_registers,) = call(
            registers_kernel,
            "registers",
            (part[0], swap(back_regs[2], three), swap(back_regs[1], two)),
            (shape((2, own, feature), F32),),
            0,
        )
    else:
        grad_registers = lax.psum_scatter(back_regs[0], "rows", scatter_dimension=1, tiled=True)
    whole = query.shape
    return (
        attended.reshape(whole),
        grad_query.reshape(whole),
        grad_keys.reshape(whole),
        grad_values.reshape(whole),
        grad_registers,
    )


def solution(mesh):
    slab = P(("groups", "rows"), None, "cols")
    in_specs = (slab, slab, slab, P(None, "rows", "cols"), slab)
    out_specs = (slab, slab, slab, slab, P("groups", "rows", "cols"))
    return jax.shard_map(shards, mesh=mesh, in_specs=in_specs, out_specs=out_specs, check_vma=False)
```

```python
import functools

import jax
import jax.numpy as jnp
from jax import lax
from jax.experimental import pallas as pl
from jax.experimental.pallas import tpu as pltpu
from jax.sharding import PartitionSpec as P

HEAD = 64
TILE = 8
PATCH = TILE * TILE
FACTOR = HEAD ** (-0.5)
BF = jnp.bfloat16
F32 = jnp.float32
VMEM = pl.BlockSpec(memory_space=pltpu.VMEM)
HBM = pl.BlockSpec(memory_space=pltpu.HBM)


def swap(array, pairs):
    return lax.ppermute(array, "rows", pairs)


def pairs_a(count):
    return [(i, i ^ 1) for i in range(count)]


def swap_b(array):
    count, across = lax.axis_size("rows"), lax.axis_size("cols")
    pairs = []
    for row in range(count):
        other = row if row in (0, count - 1) else row + 1 if row % 2 else row - 1
        for col in range(across):
            to = min(col ^ 1, across - 1) if other == row else col
            pairs.append((row * across + col, other * across + to))
    return lax.ppermute(array, ("rows", "cols"), pairs)


def column_tiles(block, tile_cols):
    feature = block.shape[1]
    wide = block.astype(F32).reshape(-1, tile_cols, TILE, feature)
    return [wide[:, c].reshape(-1, feature) for c in range(tile_cols)]


def patch_order(columns):
    feature = columns[0].shape[1]
    parts = [x.reshape(-1, 1, TILE, feature) for x in columns]
    return jnp.concatenate(parts, axis=1).reshape(-1, feature)


def slots(heads):
    return [0, 2, 1, 3] if heads == 4 else list(range(heads))


def block_diagonal(tile, heads):
    order = slots(heads)
    feature = tile.shape[1]
    lane_head = lax.broadcasted_iota(jnp.int32, tile.shape, 1) // HEAD
    zero = jnp.zeros_like(tile)
    return jnp.concatenate([jnp.where(lane_head == h, tile, zero) for h in order], axis=0)


def from_transposed(out_t, heads):
    if heads == 4:
        first = lax.broadcasted_iota(jnp.int32, (HEAD, 2 * PATCH), 1) < PATCH
        left = jnp.where(first, out_t[:HEAD, : 2 * PATCH], out_t[2 * HEAD : 3 * HEAD, : 2 * PATCH])
        right = jnp.where(first, out_t[HEAD : 2 * HEAD, 2 * PATCH :], out_t[3 * HEAD :, 2 * PATCH :])
        turned = jnp.concatenate([left, right], axis=0).T
        return jnp.concatenate([turned[:PATCH], turned[PATCH:]], axis=1)
    turned = out_t.T
    lane_head = lax.broadcasted_iota(jnp.int32, (PATCH, heads * HEAD), 1) // HEAD
    total = turned[:PATCH]
    for h in range(1, heads):
        total = jnp.where(lane_head == h, turned[h * PATCH : (h + 1) * PATCH], total)
    return total


def dot_nt(a, b):
    return lax.dot_general(a, b, (((1,), (1,)), ((), ())), preferred_element_type=F32)


def dot_nn(a, b):
    return lax.dot_general(a, b, (((1,), (0,)), ((), ())), preferred_element_type=F32)


def copy_all(moves, sems):
    copies = [pltpu.make_async_copy(x, y, sems.at[n]) for n, (x, y) in enumerate(moves)]
    for copy in copies:
        copy.start()
    for copy in copies:
        copy.wait()


def prepare_kernel(k_ref, v_ref, reg_ref, a_ref, b_ref, held_ref, sems):
    even = lax.rem(lax.axis_index("rows"), 2) == 0
    edge = k_ref.shape[0] // 2
    last = k_ref.shape[0] - edge
    at_a = pl.multiple_of(jnp.where(even, last, 0), edge)
    at_b = pl.multiple_of(jnp.where(even, 0, last), edge)
    moves = []
    for n, ref in enumerate((k_ref, v_ref)):
        moves.append((ref.at[pl.ds(at_b, edge)], b_ref.at[pl.ds(n * edge, edge)]))
        moves.append((ref.at[pl.ds(at_a, edge)], a_ref.at[pl.ds(n * edge, edge)]))
    own = reg_ref.shape[1]
    if a_ref.shape[0] > 2 * edge:
        for n in range(2):
            moves.append((reg_ref.at[n], a_ref.at[pl.ds(2 * edge + n * own, own)]))
    moves.append((reg_ref, held_ref))
    copy_all(moves, sems)


def columns_near(c, tile_cols):
    return max(c - 1, 0), min(c + 2, tile_cols)


def own_kernel(tile_cols, *refs):
    qbd_ref, gbd_ref, kt_ref, vt_ref, exp_ref, dw_ref, stat_ref, kc_ref, vc_ref = refs[4:13]
    q_ref, g_ref, k_ref, v_ref = held = refs[13:17]
    copy_all(list(zip(refs[:4], held)), refs[17])
    heads = q_ref.shape[1] // HEAD
    line = tile_cols * PATCH
    tile_rows = q_ref.shape[0] // line
    rows = tile_rows * PATCH
    for x_ref, c_ref, t_ref in ((k_ref, kc_ref, kt_ref), (v_ref, vc_ref, vt_ref)):
        for c, column in enumerate(column_tiles(x_ref[...], tile_cols)):
            column = column.astype(BF)
            c_ref[c * rows : (c + 1) * rows] = column
            t_ref[:, c * rows : (c + 1) * rows] = column.T
    for t in range(tile_rows):
        q_cols = column_tiles(q_ref[t * line : (t + 1) * line], tile_cols)
        g_cols = column_tiles(g_ref[t * line : (t + 1) * line], tile_cols)
        for c in range(tile_cols):
            tile = t * tile_cols + c
            q_bd = block_diagonal((q_cols[c] * FACTOR).astype(BF), heads)
            g_bd = block_diagonal(g_cols[c].astype(BF), heads)
            qbd_ref[tile] = q_bd
            gbd_ref[tile] = g_bd
            low, high = columns_near(c, tile_cols)
            near = slice(low * rows, high * rows)
            size = (high - low) * rows
            s = dot_nt(kc_ref[near], q_bd)
            d = dot_nt(vc_ref[near], g_bd).astype(BF)
            top = jnp.max(s, axis=0, keepdims=True)
            e = jnp.exp(s - top)
            exp_ref[tile, :size] = e
            dw_ref[tile, :size] = d
            stat_ref[tile, 0:1] = top
            stat_ref[tile, 1:2] = jnp.sum(e, axis=0, keepdims=True)
            stat_ref[tile, 2:3] = jnp.sum(e * d.astype(F32), axis=0, keepdims=True)


def tile_row_of(group):
    odd = lax.rem(lax.axis_index("rows"), 2)
    return odd if group == 0 else 1 - odd


def halo_kernel(tile_cols, group, qbd_ref, gbd_ref, stat_ref, halo_ref, exp_ref, dw_ref, sum_ref, kx_ref, vx_ref):
    edge = tile_cols * PATCH
    me = lax.axis_index("rows")
    inner = (me > 0) & (me < lax.axis_size("rows") - 1)
    for n, ref in enumerate((kx_ref, vx_ref)):
        ref[...] = jnp.concatenate(column_tiles(halo_ref[n * edge : (n + 1) * edge], tile_cols), axis=0).astype(BF)
    for c in range(tile_cols):
        tile = tile_row_of(group) * tile_cols + c
        low, high = columns_near(c, tile_cols)
        near = slice(low * PATCH, high * PATCH)
        s = dot_nt(kx_ref[near], qbd_ref[tile])
        if group == 0:
            s = jnp.where(inner, s, -1e30)
        d = dot_nt(vx_ref[near], gbd_ref[tile]).astype(BF)
        own_top = stat_ref[tile, 0:1]
        top = jnp.maximum(own_top, jnp.max(s, axis=0, keepdims=True))
        e = jnp.exp(s - top)
        ratio = jnp.exp(own_top - top)
        exp_ref[c, near] = e
        dw_ref[c, near] = d
        sum_ref[c, 0:1] = top
        sum_ref[c, 1:2] = stat_ref[tile, 1:2] * ratio + jnp.sum(e, axis=0, keepdims=True)
        sum_ref[c, 2:3] = stat_ref[tile, 2:3] * ratio + jnp.sum(e * d.astype(F32), axis=0, keepdims=True)
        sum_ref[c, 3:4] = ratio


def far_kernel(tile_cols, split_regs, *refs):
    qbd_ref, gbd_ref = refs[:2]
    halos, a_ref = (refs[2:5], refs[5:8]), refs[8]
    refs = refs[3:]
    edge = tile_cols * PATCH
    regs = []
    if split_regs:
        own_ref, two_ref, three_ref = refs[6:9]
        refs = refs[9:]
        cut = own_ref.shape[1]
        for n in range(2):
            base = 2 * edge + n * cut
            regs.append(jnp.concatenate([own_ref[n], two_ref[n], three_ref[n], a_ref[base : base + cut]], axis=0))
    else:
        regs = [refs[6][n] for n in range(2)]
        refs = refs[7:]
    final_ref, px_ref, dsx_ref, kr_ref, vr_ref, back_a_ref, back_b_ref = refs[:7]
    reg_outs = refs[7:]
    kr_ref[...], vr_ref[...] = regs
    feature = a_ref.shape[1]
    places = [(group, c) for group in range(2) for c in range(tile_cols)]
    tiles = [tile_row_of(group) * tile_cols + c for group, c in places]
    scores = [dot_nt(kr_ref[...], qbd_ref[tile]) for tile in tiles]
    grads = [dot_nt(vr_ref[...], gbd_ref[tile]).astype(BF).astype(F32) for tile in tiles]
    parts = []
    for n, (group, c) in enumerate(places):
        sum_ref = halos[group][2]
        s, d = scores[n], grads[n]
        old_top = sum_ref[c, 0:1]
        top = jnp.maximum(old_top, jnp.max(s, axis=0, keepdims=True))
        e = jnp.exp(s - top)
        ratio = jnp.exp(old_top - top)
        inverse = 1.0 / (sum_ref[c, 1:2] * ratio + jnp.sum(e, axis=0, keepdims=True))
        row_dot = (sum_ref[c, 2:3] * ratio + jnp.sum(e * d, axis=0, keepdims=True)) * inverse
        scale = ratio * inverse
        final_ref[n, 0:1] = sum_ref[c, 3:4] * scale
        final_ref[n, 1:2] = row_dot
        p = e * inverse
        parts.append((scale, row_dot, p.astype(BF), (p * (d - row_dot)).astype(BF)))
    for n, (group, c) in enumerate(places):
        exp_ref, dw_ref, _ = halos[group]
        scale, row_dot, p_reg, ds_reg = parts[n]
        low, high = columns_near(c, tile_cols)
        near = slice(low * PATCH, high * PATCH)
        p = exp_ref[c, near] * scale
        px_ref[n, near] = p.astype(BF)
        dsx_ref[n, near] = (p * (dw_ref[c, near].astype(F32) - row_dot)).astype(BF)
        px_ref[n, edge:] = p_reg
        dsx_ref[n, edge:] = ds_reg
        for ref in (px_ref, dsx_ref):
            if low > 0:
                ref[n, : low * PATCH] = jnp.zeros((low * PATCH, feature), BF)
            if high < tile_cols:
                ref[n, high * PATCH : edge] = jnp.zeros(((tile_cols - high) * PATCH, feature), BF)
    dk_reg = dv_reg = None
    for group in range(2):
        dk_t = dv_t = None
        for c in range(tile_cols):
            n = group * tile_cols + c
            dk = dot_nn(dsx_ref[n], qbd_ref[tiles[n]])
            dv = dot_nn(px_ref[n], gbd_ref[tiles[n]])
            dk_t = dk if dk_t is None else dk_t + dk
            dv_t = dv if dv_t is None else dv_t + dv
        back_ref = (back_b_ref, back_a_ref)[group]
        back_ref[:edge] = dk_t[:edge].astype(BF)
        back_ref[edge : 2 * edge] = dv_t[:edge].astype(BF)
        dk_reg = dk_t[edge:] if dk_reg is None else dk_reg + dk_t[edge:]
        dv_reg = dv_t[edge:] if dv_reg is None else dv_reg + dv_t[edge:]
    for n, reg in enumerate((dk_reg, dv_reg)):
        if split_regs:
            base = 2 * edge + n * cut
            reg_outs[0][n] = reg[:cut]
            reg_outs[1][n] = reg[cut : 2 * cut].astype(BF)
            reg_outs[2][n] = reg[2 * cut : 3 * cut].astype(BF)
            back_a_ref[base : base + cut] = reg[3 * cut :].astype(BF)
        else:
            reg_outs[0][n] = reg


def rest_kernel(
    tile_cols,
    qbd_ref,
    gbd_ref,
    kt_ref,
    vt_ref,
    exp_ref,
    dw_ref,
    final_ref,
    px_ref,
    dsx_ref,
    kb_ref,
    vb_ref,
    ka_ref,
    va_ref,
    kr_ref,
    vr_ref,
    *refs,
):
    o_ref, dq_ref, dk_ref, dv_ref, weights_ref, ds_ref, held_o_ref, held_dq_ref, sems = refs
    feature = kt_ref.shape[0]
    heads = feature // HEAD
    line = tile_cols * PATCH
    tile_rows = qbd_ref.shape[0] // tile_cols
    rows = tile_rows * PATCH
    places = [(group, c) for group in range(2) for c in range(tile_cols)]
    tiles = [tile_row_of(group) * tile_cols + c for group, c in places]
    for n, (_, c) in enumerate(places):
        low, high = columns_near(c, tile_cols)
        size = (high - low) * rows
        p = exp_ref[tiles[n], :size] * final_ref[n, 0:1]
        weights_ref[n, :size] = p.astype(BF)
        ds_ref[n, :size] = (p * (dw_ref[tiles[n], :size].astype(F32) - final_ref[n, 1:2])).astype(BF)
    copies = []
    for group, (kx_ref, vx_ref) in enumerate(((kb_ref, vb_ref), (ka_ref, va_ref))):
        kxt = jnp.concatenate([kx_ref[...], kr_ref[...]], axis=0).T
        vxt = jnp.concatenate([vx_ref[...], vr_ref[...]], axis=0).T
        o_cols, dq_cols = [], []
        for c in range(tile_cols):
            n = group * tile_cols + c
            low, high = columns_near(c, tile_cols)
            near = slice(low * rows, high * rows)
            size = (high - low) * rows
            o_t = dot_nn(vt_ref[:, near], weights_ref[n, :size]) + dot_nn(vxt, px_ref[n])
            dq_t = dot_nn(kt_ref[:, near], ds_ref[n, :size]) + dot_nn(kxt, dsx_ref[n])
            o_cols.append(from_transposed(o_t, heads))
            dq_cols.append(from_transposed(dq_t, heads) * FACTOR)
        lines = pl.ds(pl.multiple_of(tile_row_of(group) * line, line), line)
        for out_ref, columns, held_ref in ((o_ref, o_cols, held_o_ref), (dq_ref, dq_cols, held_dq_ref)):
            held_ref[group] = patch_order(columns).astype(BF)
            copies.append(pltpu.make_async_copy(held_ref.at[group], out_ref.at[lines], sems.at[len(copies)]))
            copies[-1].start()
    sums_k, sums_v = [None] * tile_cols, [None] * tile_cols
    for n, (_, c) in enumerate(places):
        low, high = columns_near(c, tile_cols)
        size = (high - low) * rows
        dk = dot_nn(ds_ref[n, :size], qbd_ref[tiles[n]])
        dv = dot_nn(weights_ref[n, :size], gbd_ref[tiles[n]])
        for sums, value in ((sums_k, dk), (sums_v, dv)):
            for x in range(low, high):
                part = value[(x - low) * rows : (x - low + 1) * rows]
                sums[x] = part if sums[x] is None else sums[x] + part
    for x in range(tile_cols):
        dk_ref[x] = sums_k[x]
        dv_ref[x] = sums_v[x]
    for copy in copies:
        copy.wait()


def registers_kernel(part_ref, three_ref, two_ref, out_ref):
    out_ref[...] = part_ref[...] + two_ref[...].astype(F32) + three_ref[...].astype(F32)


def finish_kernel(split_regs, dk_ref, dv_ref, a_ref, b_ref, *refs):
    if split_regs:
        own_ref, gk_ref, gv_ref, part_ref = refs
        cut = own_ref.shape[1]
        base = a_ref.shape[0] - 2 * cut
        for n in range(2):
            part_ref[n] = own_ref[n] + a_ref[base + n * cut : base + (n + 1) * cut].astype(F32)
    else:
        gk_ref, gv_ref = refs
    me = lax.axis_index("rows")
    even = lax.rem(me, 2) == 0
    has_top = me > 0
    has_bottom = me < lax.axis_size("rows") - 1
    tile_cols = dk_ref.shape[0]
    edge = tile_cols * PATCH
    for n, (acc_ref, out_ref) in enumerate(((dk_ref, gk_ref), (dv_ref, gv_ref))):
        from_a = a_ref[n * edge : (n + 1) * edge]
        from_b = b_ref[n * edge : (n + 1) * edge]
        top = jnp.where(has_top, jnp.where(even, from_b, from_a).astype(F32), 0.0)
        bottom = jnp.where(has_bottom, jnp.where(even, from_a, from_b).astype(F32), 0.0)
        rows = acc_ref.shape[1]
        columns = []
        for c in range(tile_cols):
            high = acc_ref[c, :PATCH] + top[c * PATCH : (c + 1) * PATCH]
            low = acc_ref[c, rows - PATCH :] + bottom[c * PATCH : (c + 1) * PATCH]
            columns.append(jnp.concatenate([high, low], axis=0))
        out_ref[...] = patch_order(columns).astype(BF)


def shape(dims, dtype):
    return jax.ShapeDtypeStruct(dims, dtype)


def call(kernel, name, ins, outs, flops, in_specs=None, out_specs=None, scratch=()):
    size = sum(x.size * x.dtype.itemsize for x in ins) + sum(x.size * x.dtype.itemsize for x in outs)
    return pl.pallas_call(
        kernel,
        out_shape=tuple(outs),
        in_specs=in_specs or [VMEM] * len(ins),
        out_specs=out_specs or (VMEM,) * len(outs),
        scratch_shapes=list(scratch),
        compiler_params=pltpu.CompilerParams(vmem_limit_bytes=24 * 1024 * 1024),
        cost_estimate=pl.CostEstimate(flops=flops, bytes_accessed=size, transcendentals=0),
        name=name,
    )(*ins)


def shards(query, keys, values, registers, cotangent):
    count = lax.axis_size("rows")
    split_regs = count == 4
    tile_cols = query.shape[1] // TILE
    tile_rows = query.shape[0] // TILE
    assert tile_rows == 2
    feature = query.shape[2]
    total = query.shape[0] * query.shape[1]
    edge = tile_cols * PATCH
    own = registers.shape[1]
    reg_count = own * count
    q, k, v, g = (
        pltpu.with_memory_space_constraint(x.reshape(total, feature), pltpu.HBM)
        for x in (query, keys, values, cotangent)
    )
    extra = 2 * own if split_regs else 0
    two = [(i, i ^ 2) for i in range(count)]
    three = [(i, i ^ 3) for i in range(count)]

    registers = pltpu.with_memory_space_constraint(registers, pltpu.HBM)
    pay_a, pay_b, reg_held = call(
        prepare_kernel,
        "prepare",
        (k, v, registers),
        (
            shape((2 * edge + extra, feature), BF),
            shape((2 * edge, feature), BF),
            shape(registers.shape, BF),
        ),
        0,
        in_specs=[HBM] * 3,
        scratch=[pltpu.SemaphoreType.DMA((7,))],
    )
    got_b = swap_b(pay_b)
    got_a = swap(pay_a, pairs_a(count))
    if split_regs:
        regs = (reg_held, swap(reg_held, two), swap(reg_held, three))
    else:
        regs = (lax.all_gather(registers, "rows", axis=1, tiled=True),)

    tiles = tile_rows * tile_cols
    rows = tile_rows * PATCH
    most = min(3, tile_cols) * rows
    window = edge + reg_count
    qbd, gbd, kt, vt, exps, dw, stats = call(
        functools.partial(own_kernel, tile_cols),
        "own",
        (q, g, k, v),
        (
            shape((tiles, feature, feature), BF),
            shape((tiles, feature, feature), BF),
            shape((feature, total), BF),
            shape((feature, total), BF),
            shape((tiles, most, feature), F32),
            shape((tiles, most, feature), BF),
            shape((tiles, 8, feature), F32),
        ),
        600_000_000,
        in_specs=[HBM] * 4,
        scratch=[pltpu.VMEM((total, feature), BF)] * 6 + [pltpu.SemaphoreType.DMA((4,))],
    )
    if split_regs:
        reg_shapes = (
            shape((2, own, feature), F32),
            shape((2, own, feature), BF),
            shape((2, own, feature), BF),
        )
    else:
        reg_shapes = (shape((2, reg_count, feature), F32),)
    halos = []
    for group, got in enumerate((got_b, got_a)):
        halos.append(
            call(
                functools.partial(halo_kernel, tile_cols, group),
                "halo",
                (qbd, gbd, stats, got),
                (
                    shape((tile_cols, edge, feature), F32),
                    shape((tile_cols, edge, feature), BF),
                    shape((tile_cols, 8, feature), F32),
                    shape((edge, feature), BF),
                    shape((edge, feature), BF),
                ),
                32 * tile_cols * edge * feature * feature,
            )
        )
    final, px, dsx, kr, vr, back_a, back_b, *back_regs = call(
        functools.partial(far_kernel, tile_cols, split_regs),
        "far",
        (qbd, gbd) + tuple(halos[0][:3]) + tuple(halos[1][:3]) + (got_a,) + regs,
        (
            shape((tiles, 8, feature), F32),
            shape((tiles, window, feature), BF),
            shape((tiles, window, feature), BF),
            shape((reg_count, feature), BF),
            shape((reg_count, feature), BF),
            shape((2 * edge + extra, feature), BF),
            shape((2 * edge, feature), BF),
        )
        + reg_shapes,
        8 * tiles * window * feature * feature,
    )
    back_from_b = swap_b(back_b)
    back_from_a = swap(back_a, pairs_a(count))
    attended, grad_query, dk, dv = call(
        functools.partial(rest_kernel, tile_cols),
        "rest",
        (qbd, gbd, kt, vt, exps, dw, final, px, dsx) + tuple(halos[0][3:]) + tuple(halos[1][3:]) + (kr, vr),
        (
            shape((total, feature), BF),
            shape((total, feature), BF),
            shape((tile_cols, rows, feature), F32),
            shape((tile_cols, rows, feature), F32),
        ),
        600_000_000,
        out_specs=(HBM, HBM, VMEM, VMEM),
        scratch=[pltpu.VMEM((tiles, most, feature), BF)] * 2
        + [pltpu.VMEM((tile_rows, edge, feature), BF)] * 2
        + [pltpu.SemaphoreType.DMA((4,))],
    )
    mine = (back_regs[0],) if split_regs else ()
    grad_keys, grad_values, *part = call(
        functools.partial(finish_kernel, split_regs),
        "finish",
        (dk, dv, back_from_a, back_from_b) + mine,
        (shape((total, feature), BF), shape((total, feature), BF)) + tuple(shape(x.shape, F32) for x in mine),
        0,
    )
    if split_regs:
        (grad_registers,) = call(
            registers_kernel,
            "registers",
            (part[0], swap(back_regs[2], three), swap(back_regs[1], two)),
            (shape((2, own, feature), F32),),
            0,
        )
    else:
        grad_registers = lax.psum_scatter(back_regs[0], "rows", scatter_dimension=1, tiled=True)
    whole = query.shape
    return (
        attended.reshape(whole),
        grad_query.reshape(whole),
        grad_keys.reshape(whole),
        grad_values.reshape(whole),
        grad_registers,
    )


def solution(mesh):
    slab = P(("groups", "rows"), None, "cols")
    in_specs = (slab, slab, slab, P(None, "rows", "cols"), slab)
    out_specs = (slab, slab, slab, slab, P("groups", "rows", "cols"))
    return jax.shard_map(shards, mesh=mesh, in_specs=in_specs, out_specs=out_specs, check_vma=False)
```

```python
import functools

import jax
import jax.numpy as jnp
from jax import lax
from jax.experimental import pallas as pl
from jax.experimental.pallas import tpu as pltpu
from jax.sharding import PartitionSpec as P

HEAD = 64
TILE = 8
PATCH = TILE * TILE
FACTOR = HEAD ** (-0.5)
BF = jnp.bfloat16
F32 = jnp.float32
VMEM = pl.BlockSpec(memory_space=pltpu.VMEM)
HBM = pl.BlockSpec(memory_space=pltpu.HBM)


def swap(array, pairs):
    return lax.ppermute(array, "rows", pairs)


def pairs_a(count):
    return [(i, i ^ 1) for i in range(count)]


def swap_b(array):
    count, across = lax.axis_size("rows"), lax.axis_size("cols")
    pairs = []
    for row in range(count):
        other = row if row in (0, count - 1) else row + 1 if row % 2 else row - 1
        for col in range(across):
            to = min(col ^ 1, across - 1) if other == row else col
            pairs.append((row * across + col, other * across + to))
    return lax.ppermute(array, ("rows", "cols"), pairs)


def column_tiles(block, tile_cols):
    feature = block.shape[1]
    wide = block.astype(F32).reshape(-1, tile_cols, TILE, feature)
    return [wide[:, c].reshape(-1, feature) for c in range(tile_cols)]


def patch_order(columns):
    feature = columns[0].shape[1]
    parts = [x.reshape(-1, 1, TILE, feature) for x in columns]
    return jnp.concatenate(parts, axis=1).reshape(-1, feature)


def slots(heads):
    return [0, 2, 1, 3] if heads == 4 else list(range(heads))


def block_diagonal(tile, heads):
    order = slots(heads)
    feature = tile.shape[1]
    lane_head = lax.broadcasted_iota(jnp.int32, tile.shape, 1) // HEAD
    zero = jnp.zeros_like(tile)
    return jnp.concatenate([jnp.where(lane_head == h, tile, zero) for h in order], axis=0)


def from_transposed(out_t, heads):
    if heads == 4:
        first = lax.broadcasted_iota(jnp.int32, (HEAD, 2 * PATCH), 1) < PATCH
        left = jnp.where(first, out_t[:HEAD, : 2 * PATCH], out_t[2 * HEAD : 3 * HEAD, : 2 * PATCH])
        right = jnp.where(first, out_t[HEAD : 2 * HEAD, 2 * PATCH :], out_t[3 * HEAD :, 2 * PATCH :])
        turned = jnp.concatenate([left, right], axis=0).T
        return jnp.concatenate([turned[:PATCH], turned[PATCH:]], axis=1)
    turned = out_t.T
    lane_head = lax.broadcasted_iota(jnp.int32, (PATCH, heads * HEAD), 1) // HEAD
    total = turned[:PATCH]
    for h in range(1, heads):
        total = jnp.where(lane_head == h, turned[h * PATCH : (h + 1) * PATCH], total)
    return total


def dot_nt(a, b):
    return lax.dot_general(a, b, (((1,), (1,)), ((), ())), preferred_element_type=F32)


def dot_nn(a, b):
    return lax.dot_general(a, b, (((1,), (0,)), ((), ())), preferred_element_type=F32)


def copy_all(moves, sems):
    copies = [pltpu.make_async_copy(x, y, sems.at[n]) for n, (x, y) in enumerate(moves)]
    for copy in copies:
        copy.start()
    for copy in copies:
        copy.wait()


def prepare_kernel(k_ref, v_ref, reg_ref, a_ref, b_ref, held_ref, sems):
    even = lax.rem(lax.axis_index("rows"), 2) == 0
    edge = k_ref.shape[0] // 2
    last = k_ref.shape[0] - edge
    at_a = pl.multiple_of(jnp.where(even, last, 0), edge)
    at_b = pl.multiple_of(jnp.where(even, 0, last), edge)
    moves = []
    for n, ref in enumerate((k_ref, v_ref)):
        moves.append((ref.at[pl.ds(at_b, edge)], b_ref.at[pl.ds(n * edge, edge)]))
        moves.append((ref.at[pl.ds(at_a, edge)], a_ref.at[pl.ds(n * edge, edge)]))
    own = reg_ref.shape[1]
    if a_ref.shape[0] > 2 * edge:
        for n in range(2):
            moves.append((reg_ref.at[n], a_ref.at[pl.ds(2 * edge + n * own, own)]))
    moves.append((reg_ref, held_ref))
    copy_all(moves, sems)


def columns_near(c, tile_cols):
    return max(c - 1, 0), min(c + 2, tile_cols)


def own_kernel(tile_cols, *refs):
    qbd_ref, gbd_ref, kt_ref, vt_ref, exp_ref, dw_ref, stat_ref, kc_ref, vc_ref = refs[4:13]
    q_ref, g_ref, k_ref, v_ref = held = refs[13:17]
    copy_all(list(zip(refs[:4], held)), refs[17])
    heads = q_ref.shape[1] // HEAD
    line = tile_cols * PATCH
    tile_rows = q_ref.shape[0] // line
    rows = tile_rows * PATCH
    for x_ref, c_ref, t_ref in ((k_ref, kc_ref, kt_ref), (v_ref, vc_ref, vt_ref)):
        for c, column in enumerate(column_tiles(x_ref[...], tile_cols)):
            column = column.astype(BF)
            c_ref[c * rows : (c + 1) * rows] = column
            t_ref[:, c * rows : (c + 1) * rows] = column.T
    for t in range(tile_rows):
        q_cols = column_tiles(q_ref[t * line : (t + 1) * line], tile_cols)
        g_cols = column_tiles(g_ref[t * line : (t + 1) * line], tile_cols)
        for c in range(tile_cols):
            tile = t * tile_cols + c
            q_bd = block_diagonal((q_cols[c] * FACTOR).astype(BF), heads)
            g_bd = block_diagonal(g_cols[c].astype(BF), heads)
            qbd_ref[tile] = q_bd
            gbd_ref[tile] = g_bd
            low, high = columns_near(c, tile_cols)
            near = slice(low * rows, high * rows)
            size = (high - low) * rows
            s = dot_nt(kc_ref[near], q_bd)
            d = dot_nt(vc_ref[near], g_bd).astype(BF)
            top = jnp.max(s, axis=0, keepdims=True)
            e = jnp.exp(s - top)
            exp_ref[tile, :size] = e
            dw_ref[tile, :size] = d
            stat_ref[tile, 0:1] = top
            stat_ref[tile, 1:2] = jnp.sum(e, axis=0, keepdims=True)
            stat_ref[tile, 2:3] = jnp.sum(e * d.astype(F32), axis=0, keepdims=True)


def tile_row_of(group):
    odd = lax.rem(lax.axis_index("rows"), 2)
    return odd if group == 0 else 1 - odd


def halo_kernel(tile_cols, group, qbd_ref, gbd_ref, stat_ref, halo_ref, exp_ref, dw_ref, sum_ref, kx_ref, vx_ref):
    edge = tile_cols * PATCH
    me = lax.axis_index("rows")
    inner = (me > 0) & (me < lax.axis_size("rows") - 1)
    for n, ref in enumerate((kx_ref, vx_ref)):
        ref[...] = jnp.concatenate(column_tiles(halo_ref[n * edge : (n + 1) * edge], tile_cols), axis=0).astype(BF)
    for c in range(tile_cols):
        tile = tile_row_of(group) * tile_cols + c
        low, high = columns_near(c, tile_cols)
        near = slice(low * PATCH, high * PATCH)
        s = dot_nt(kx_ref[near], qbd_ref[tile])
        if group == 0:
            s = jnp.where(inner, s, -1e30)
        d = dot_nt(vx_ref[near], gbd_ref[tile]).astype(BF)
        own_top = stat_ref[tile, 0:1]
        top = jnp.maximum(own_top, jnp.max(s, axis=0, keepdims=True))
        e = jnp.exp(s - top)
        ratio = jnp.exp(own_top - top)
        exp_ref[c, near] = e
        dw_ref[c, near] = d
        sum_ref[c, 0:1] = top
        sum_ref[c, 1:2] = stat_ref[tile, 1:2] * ratio + jnp.sum(e, axis=0, keepdims=True)
        sum_ref[c, 2:3] = stat_ref[tile, 2:3] * ratio + jnp.sum(e * d.astype(F32), axis=0, keepdims=True)
        sum_ref[c, 3:4] = ratio


def far_kernel(tile_cols, split_regs, *refs):
    qbd_ref, gbd_ref = refs[:2]
    halos, a_ref = (refs[2:5], refs[5:8]), refs[8]
    refs = refs[3:]
    edge = tile_cols * PATCH
    regs = []
    if split_regs:
        own_ref, two_ref, three_ref = refs[6:9]
        refs = refs[9:]
        cut = own_ref.shape[1]
        for n in range(2):
            base = 2 * edge + n * cut
            regs.append(jnp.concatenate([own_ref[n], two_ref[n], three_ref[n], a_ref[base : base + cut]], axis=0))
    else:
        regs = [refs[6][n] for n in range(2)]
        refs = refs[7:]
    final_ref, px_ref, dsx_ref, kr_ref, vr_ref, back_a_ref, back_b_ref = refs[:7]
    reg_outs = refs[7:]
    kr_ref[...], vr_ref[...] = regs
    feature = a_ref.shape[1]
    places = [(group, c) for group in range(2) for c in range(tile_cols)]
    tiles = [tile_row_of(group) * tile_cols + c for group, c in places]
    scores = [dot_nt(kr_ref[...], qbd_ref[tile]) for tile in tiles]
    grads = [dot_nt(vr_ref[...], gbd_ref[tile]).astype(BF).astype(F32) for tile in tiles]
    parts = []
    for n, (group, c) in enumerate(places):
        sum_ref = halos[group][2]
        s, d = scores[n], grads[n]
        old_top = sum_ref[c, 0:1]
        top = jnp.maximum(old_top, jnp.max(s, axis=0, keepdims=True))
        e = jnp.exp(s - top)
        ratio = jnp.exp(old_top - top)
        inverse = 1.0 / (sum_ref[c, 1:2] * ratio + jnp.sum(e, axis=0, keepdims=True))
        row_dot = (sum_ref[c, 2:3] * ratio + jnp.sum(e * d, axis=0, keepdims=True)) * inverse
        scale = ratio * inverse
        final_ref[n, 0:1] = sum_ref[c, 3:4] * scale
        final_ref[n, 1:2] = row_dot
        p = e * inverse
        parts.append((scale, row_dot, p.astype(BF), (p * (d - row_dot)).astype(BF)))
    for n, (group, c) in enumerate(places):
        exp_ref, dw_ref, _ = halos[group]
        scale, row_dot, p_reg, ds_reg = parts[n]
        low, high = columns_near(c, tile_cols)
        near = slice(low * PATCH, high * PATCH)
        p = exp_ref[c, near] * scale
        size = (high - low) * PATCH
        whole = size + p_reg.shape[0]
        px_ref[n, :size] = p.astype(BF)
        dsx_ref[n, :size] = (p * (dw_ref[c, near].astype(F32) - row_dot)).astype(BF)
        px_ref[n, size:whole] = p_reg
        dsx_ref[n, size:whole] = ds_reg
    dk_reg = dv_reg = None
    for group in range(2):
        parts_k, parts_v = [None] * tile_cols, [None] * tile_cols
        for c in range(tile_cols):
            n = group * tile_cols + c
            low, high = columns_near(c, tile_cols)
            size = (high - low) * PATCH
            whole = size + kr_ref.shape[0]
            dk = dot_nn(dsx_ref[n, :whole], qbd_ref[tiles[n]])
            dv = dot_nn(px_ref[n, :whole], gbd_ref[tiles[n]])
            for sums, value in ((parts_k, dk), (parts_v, dv)):
                for x in range(low, high):
                    part = value[(x - low) * PATCH : (x - low + 1) * PATCH]
                    sums[x] = part if sums[x] is None else sums[x] + part
            dk_reg = dk[size:] if dk_reg is None else dk_reg + dk[size:]
            dv_reg = dv[size:] if dv_reg is None else dv_reg + dv[size:]
        back_ref = (back_b_ref, back_a_ref)[group]
        back_ref[:edge] = jnp.concatenate(parts_k, axis=0).astype(BF)
        back_ref[edge : 2 * edge] = jnp.concatenate(parts_v, axis=0).astype(BF)
    for n, reg in enumerate((dk_reg, dv_reg)):
        if split_regs:
            base = 2 * edge + n * cut
            reg_outs[0][n] = reg[:cut]
            reg_outs[1][n] = reg[cut : 2 * cut].astype(BF)
            reg_outs[2][n] = reg[2 * cut : 3 * cut].astype(BF)
            back_a_ref[base : base + cut] = reg[3 * cut :].astype(BF)
        else:
            reg_outs[0][n] = reg


def rest_kernel(
    tile_cols,
    qbd_ref,
    gbd_ref,
    kt_ref,
    vt_ref,
    exp_ref,
    dw_ref,
    final_ref,
    px_ref,
    dsx_ref,
    kb_ref,
    vb_ref,
    ka_ref,
    va_ref,
    kr_ref,
    vr_ref,
    *refs,
):
    o_ref, dq_ref, dk_ref, dv_ref = refs[:4]
    feature = kt_ref.shape[0]
    heads = feature // HEAD
    line = tile_cols * PATCH
    tile_rows = qbd_ref.shape[0] // tile_cols
    rows = tile_rows * PATCH
    for group, (kx_ref, vx_ref) in enumerate(((kb_ref, vb_ref), (ka_ref, va_ref))):
        t = tile_row_of(group)
        kxt = jnp.concatenate([kx_ref[...], kr_ref[...]], axis=0).T
        vxt = jnp.concatenate([vx_ref[...], vr_ref[...]], axis=0).T
        o_cols, dq_cols = [], []
        for c in range(tile_cols):
            tile = t * tile_cols + c
            n = group * tile_cols + c
            low, high = columns_near(c, tile_cols)
            near = slice(low * rows, high * rows)
            size = (high - low) * rows
            p = exp_ref[tile, :size] * final_ref[n, 0:1]
            d_scores = (p * (dw_ref[tile, :size].astype(F32) - final_ref[n, 1:2])).astype(BF)
            weights = p.astype(BF)
            dk = dot_nn(d_scores, qbd_ref[tile])
            dv = dot_nn(weights, gbd_ref[tile])
            first = group == 0
            for ref, value in ((dk_ref, dk), (dv_ref, dv)):
                for x in range(low, high):
                    part = value[(x - low) * rows : (x - low + 1) * rows]
                    if first and (x == c + 1 or (c == 0)):
                        ref[x] = part
                    else:
                        ref[x] += part
            far = []
            for ref in (px_ref, dsx_ref):
                halo = (high - low) * PATCH
                pieces = [ref[n, :halo], ref[n, halo : halo + kr_ref.shape[0]]]
                if high < tile_cols:
                    pieces.insert(1, jnp.zeros(((tile_cols - high) * PATCH, feature), BF))
                if low > 0:
                    pieces.insert(0, jnp.zeros((low * PATCH, feature), BF))
                far.append(jnp.concatenate(pieces, axis=0))
            o_t = dot_nn(vt_ref[:, near], weights) + dot_nn(vxt, far[0])
            dq_t = dot_nn(kt_ref[:, near], d_scores) + dot_nn(kxt, far[1])
            o_cols.append(from_transposed(o_t, heads))
            dq_cols.append(from_transposed(dq_t, heads) * FACTOR)
        lines = pl.ds(pl.multiple_of(t * line, line), line)
        o_ref[lines] = patch_order(o_cols).astype(BF)
        dq_ref[lines] = patch_order(dq_cols).astype(BF)


def registers_kernel(part_ref, three_ref, two_ref, out_ref):
    out_ref[...] = part_ref[...] + two_ref[...].astype(F32) + three_ref[...].astype(F32)


def finish_kernel(split_regs, dk_ref, dv_ref, a_ref, b_ref, *refs):
    if split_regs:
        own_ref, gk_ref, gv_ref, part_ref = refs
        cut = own_ref.shape[1]
        base = a_ref.shape[0] - 2 * cut
        for n in range(2):
            part_ref[n] = own_ref[n] + a_ref[base + n * cut : base + (n + 1) * cut].astype(F32)
    else:
        gk_ref, gv_ref = refs
    me = lax.axis_index("rows")
    even = lax.rem(me, 2) == 0
    has_top = me > 0
    has_bottom = me < lax.axis_size("rows") - 1
    tile_cols = dk_ref.shape[0]
    edge = tile_cols * PATCH
    for n, (acc_ref, out_ref) in enumerate(((dk_ref, gk_ref), (dv_ref, gv_ref))):
        from_a = a_ref[n * edge : (n + 1) * edge]
        from_b = b_ref[n * edge : (n + 1) * edge]
        top = jnp.where(has_top, jnp.where(even, from_b, from_a).astype(F32), 0.0)
        bottom = jnp.where(has_bottom, jnp.where(even, from_a, from_b).astype(F32), 0.0)
        rows = acc_ref.shape[1]
        columns = []
        for c in range(tile_cols):
            high = acc_ref[c, :PATCH] + top[c * PATCH : (c + 1) * PATCH]
            low = acc_ref[c, rows - PATCH :] + bottom[c * PATCH : (c + 1) * PATCH]
            columns.append(jnp.concatenate([high, low], axis=0))
        out_ref[...] = patch_order(columns).astype(BF)


def shape(dims, dtype):
    return jax.ShapeDtypeStruct(dims, dtype)


def call(kernel, name, ins, outs, flops, in_specs=None, scratch=()):
    size = sum(x.size * x.dtype.itemsize for x in ins) + sum(x.size * x.dtype.itemsize for x in outs)
    return pl.pallas_call(
        kernel,
        out_shape=tuple(outs),
        in_specs=in_specs or [VMEM] * len(ins),
        out_specs=(VMEM,) * len(outs),
        scratch_shapes=list(scratch),
        compiler_params=pltpu.CompilerParams(vmem_limit_bytes=24 * 1024 * 1024),
        cost_estimate=pl.CostEstimate(flops=flops, bytes_accessed=size, transcendentals=0),
        name=name,
    )(*ins)


def shards(query, keys, values, registers, cotangent):
    count = lax.axis_size("rows")
    split_regs = count == 4
    tile_cols = query.shape[1] // TILE
    tile_rows = query.shape[0] // TILE
    assert tile_rows == 2
    feature = query.shape[2]
    total = query.shape[0] * query.shape[1]
    edge = tile_cols * PATCH
    own = registers.shape[1]
    reg_count = own * count
    q, k, v, g = (
        pltpu.with_memory_space_constraint(x.reshape(total, feature), pltpu.HBM)
        for x in (query, keys, values, cotangent)
    )
    extra = 2 * own if split_regs else 0
    two = [(i, i ^ 2) for i in range(count)]
    three = [(i, i ^ 3) for i in range(count)]

    registers = pltpu.with_memory_space_constraint(registers, pltpu.HBM)
    pay_a, pay_b, reg_held = call(
        prepare_kernel,
        "prepare",
        (k, v, registers),
        (
            shape((2 * edge + extra, feature), BF),
            shape((2 * edge, feature), BF),
            shape(registers.shape, BF),
        ),
        0,
        in_specs=[HBM] * 3,
        scratch=[pltpu.SemaphoreType.DMA((7,))],
    )
    got_b = swap_b(pay_b)
    got_a = swap(pay_a, pairs_a(count))
    if split_regs:
        regs = (reg_held, swap(reg_held, two), swap(reg_held, three))
    else:
        regs = (lax.all_gather(registers, "rows", axis=1, tiled=True),)

    tiles = tile_rows * tile_cols
    rows = tile_rows * PATCH
    most = min(3, tile_cols) * rows
    window = edge + reg_count
    qbd, gbd, kt, vt, exps, dw, stats = call(
        functools.partial(own_kernel, tile_cols),
        "own",
        (q, g, k, v),
        (
            shape((tiles, feature, feature), BF),
            shape((tiles, feature, feature), BF),
            shape((feature, total), BF),
            shape((feature, total), BF),
            shape((tiles, most, feature), F32),
            shape((tiles, most, feature), BF),
            shape((tiles, 8, feature), F32),
        ),
        600_000_000,
        in_specs=[HBM] * 4,
        scratch=[pltpu.VMEM((total, feature), BF)] * 6 + [pltpu.SemaphoreType.DMA((4,))],
    )
    if split_regs:
        reg_shapes = (
            shape((2, own, feature), F32),
            shape((2, own, feature), BF),
            shape((2, own, feature), BF),
        )
    else:
        reg_shapes = (shape((2, reg_count, feature), F32),)
    halos = []
    for group, got in enumerate((got_b, got_a)):
        halos.append(
            call(
                functools.partial(halo_kernel, tile_cols, group),
                "halo",
                (qbd, gbd, stats, got),
                (
                    shape((tile_cols, edge, feature), F32),
                    shape((tile_cols, edge, feature), BF),
                    shape((tile_cols, 8, feature), F32),
                    shape((edge, feature), BF),
                    shape((edge, feature), BF),
                ),
                32 * tile_cols * edge * feature * feature,
            )
        )
    final, px, dsx, kr, vr, back_a, back_b, *back_regs = call(
        functools.partial(far_kernel, tile_cols, split_regs),
        "far",
        (qbd, gbd) + tuple(halos[0][:3]) + tuple(halos[1][:3]) + (got_a,) + regs,
        (
            shape((tiles, 8, feature), F32),
            shape((tiles, window, feature), BF),
            shape((tiles, window, feature), BF),
            shape((reg_count, feature), BF),
            shape((reg_count, feature), BF),
            shape((2 * edge + extra, feature), BF),
            shape((2 * edge, feature), BF),
        )
        + reg_shapes,
        8 * tiles * window * feature * feature,
    )
    back_from_b = swap_b(back_b)
    back_from_a = swap(back_a, pairs_a(count))
    attended, grad_query, dk, dv = call(
        functools.partial(rest_kernel, tile_cols),
        "rest",
        (qbd, gbd, kt, vt, exps, dw, final, px, dsx) + tuple(halos[0][3:]) + tuple(halos[1][3:]) + (kr, vr),
        (
            shape((total, feature), BF),
            shape((total, feature), BF),
            shape((tile_cols, rows, feature), F32),
            shape((tile_cols, rows, feature), F32),
        ),
        600_000_000,
    )
    mine = (back_regs[0],) if split_regs else ()
    grad_keys, grad_values, *part = call(
        functools.partial(finish_kernel, split_regs),
        "finish",
        (dk, dv, back_from_a, back_from_b) + mine,
        (shape((total, feature), BF), shape((total, feature), BF)) + tuple(shape(x.shape, F32) for x in mine),
        0,
    )
    if split_regs:
        (grad_registers,) = call(
            registers_kernel,
            "registers",
            (part[0], swap(back_regs[2], three), swap(back_regs[1], two)),
            (shape((2, own, feature), F32),),
            0,
        )
    else:
        grad_registers = lax.psum_scatter(back_regs[0], "rows", scatter_dimension=1, tiled=True)
    whole = query.shape
    return (
        attended.reshape(whole),
        grad_query.reshape(whole),
        grad_keys.reshape(whole),
        grad_values.reshape(whole),
        grad_registers,
    )


def solution(mesh):
    slab = P(("groups", "rows"), None, "cols")
    in_specs = (slab, slab, slab, P(None, "rows", "cols"), slab)
    out_specs = (slab, slab, slab, slab, P("groups", "rows", "cols"))
    return jax.shard_map(shards, mesh=mesh, in_specs=in_specs, out_specs=out_specs, check_vma=False)
```

```python
import functools

import jax
import jax.numpy as jnp
from jax import lax
from jax.experimental import pallas as pl
from jax.experimental.pallas import tpu as pltpu
from jax.sharding import PartitionSpec as P

HEAD = 64
TILE = 8
PATCH = TILE * TILE
FACTOR = HEAD ** (-0.5)
BF = jnp.bfloat16
F32 = jnp.float32
VMEM = pl.BlockSpec(memory_space=pltpu.VMEM)
HBM = pl.BlockSpec(memory_space=pltpu.HBM)


def swap(array, pairs):
    return lax.ppermute(array, "rows", pairs)


def pairs_a(count):
    return [(i, i ^ 1) for i in range(count)]


def swap_b(array):
    count, across = lax.axis_size("rows"), lax.axis_size("cols")
    pairs = []
    for row in range(count):
        other = row if row in (0, count - 1) else row + 1 if row % 2 else row - 1
        for col in range(across):
            to = min(col ^ 1, across - 1) if other == row else col
            pairs.append((row * across + col, other * across + to))
    return lax.ppermute(array, ("rows", "cols"), pairs)


def column_tiles(block, tile_cols):
    feature = block.shape[1]
    wide = block.astype(F32).reshape(-1, tile_cols, TILE, feature)
    return [wide[:, c].reshape(-1, feature) for c in range(tile_cols)]


def patch_order(columns):
    feature = columns[0].shape[1]
    parts = [x.reshape(-1, 1, TILE, feature) for x in columns]
    return jnp.concatenate(parts, axis=1).reshape(-1, feature)


def pick(block, low, high, tile_cols):
    if high - low == tile_cols:
        return block
    feature = block.shape[1]
    return block.reshape(-1, tile_cols, TILE, feature)[:, low:high].reshape(-1, feature)


def spread(block, low, high, tile_cols):
    if high - low == tile_cols:
        return block
    feature = block.shape[1]
    parts = [block.reshape(-1, high - low, TILE, feature)]
    count = parts[0].shape[0]
    if low > 0:
        parts.insert(0, jnp.zeros((count, low, TILE, feature), block.dtype))
    if high < tile_cols:
        parts.append(jnp.zeros((count, tile_cols - high, TILE, feature), block.dtype))
    return jnp.concatenate(parts, axis=1).reshape(-1, feature)


def slots(heads):
    return [0, 2, 1, 3] if heads == 4 else list(range(heads))


def block_diagonal(tile, heads):
    order = slots(heads)
    feature = tile.shape[1]
    lane_head = lax.broadcasted_iota(jnp.int32, tile.shape, 1) // HEAD
    zero = jnp.zeros_like(tile)
    return jnp.concatenate([jnp.where(lane_head == h, tile, zero) for h in order], axis=0)


def from_transposed(out_t, heads):
    if heads == 4:
        first = lax.broadcasted_iota(jnp.int32, (HEAD, 2 * PATCH), 1) < PATCH
        left = jnp.where(first, out_t[:HEAD, : 2 * PATCH], out_t[2 * HEAD : 3 * HEAD, : 2 * PATCH])
        right = jnp.where(first, out_t[HEAD : 2 * HEAD, 2 * PATCH :], out_t[3 * HEAD :, 2 * PATCH :])
        turned = jnp.concatenate([left, right], axis=0).T
        return jnp.concatenate([turned[:PATCH], turned[PATCH:]], axis=1)
    turned = out_t.T
    lane_head = lax.broadcasted_iota(jnp.int32, (PATCH, heads * HEAD), 1) // HEAD
    total = turned[:PATCH]
    for h in range(1, heads):
        total = jnp.where(lane_head == h, turned[h * PATCH : (h + 1) * PATCH], total)
    return total


def dot_nt(a, b):
    return lax.dot_general(a, b, (((1,), (1,)), ((), ())), preferred_element_type=F32)


def dot_nn(a, b):
    return lax.dot_general(a, b, (((1,), (0,)), ((), ())), preferred_element_type=F32)


def copy_all(moves, sems):
    copies = [pltpu.make_async_copy(x, y, sems.at[n]) for n, (x, y) in enumerate(moves)]
    for copy in copies:
        copy.start()
    for copy in copies:
        copy.wait()


def prepare_kernel(k_ref, v_ref, reg_ref, a_ref, b_ref, held_ref, sems):
    even = lax.rem(lax.axis_index("rows"), 2) == 0
    edge = k_ref.shape[0] // 2
    last = k_ref.shape[0] - edge
    at_a = pl.multiple_of(jnp.where(even, last, 0), edge)
    at_b = pl.multiple_of(jnp.where(even, 0, last), edge)
    moves = []
    for n, ref in enumerate((k_ref, v_ref)):
        moves.append((ref.at[pl.ds(at_b, edge)], b_ref.at[pl.ds(n * edge, edge)]))
        moves.append((ref.at[pl.ds(at_a, edge)], a_ref.at[pl.ds(n * edge, edge)]))
    own = reg_ref.shape[1]
    if a_ref.shape[0] > 2 * edge:
        for n in range(2):
            moves.append((reg_ref.at[n], a_ref.at[pl.ds(2 * edge + n * own, own)]))
    moves.append((reg_ref, held_ref))
    copy_all(moves, sems)


def columns_near(c, tile_cols):
    return max(c - 1, 0), min(c + 2, tile_cols)


def own_kernel(tile_cols, *refs):
    qbd_ref, gbd_ref, kt_ref, vt_ref, exp_ref, dw_ref, stat_ref, kc_ref, vc_ref = refs[4:13]
    q_ref, g_ref, k_ref, v_ref = held = refs[13:17]
    copy_all(list(zip(refs[:4], held)), refs[17])
    heads = q_ref.shape[1] // HEAD
    line = tile_cols * PATCH
    tile_rows = q_ref.shape[0] // line
    rows = tile_rows * PATCH
    for x_ref, c_ref, t_ref in ((k_ref, kc_ref, kt_ref), (v_ref, vc_ref, vt_ref)):
        for c, column in enumerate(column_tiles(x_ref[...], tile_cols)):
            column = column.astype(BF)
            c_ref[c * rows : (c + 1) * rows] = column
            t_ref[:, c * rows : (c + 1) * rows] = column.T
    for t in range(tile_rows):
        q_cols = column_tiles(q_ref[t * line : (t + 1) * line], tile_cols)
        g_cols = column_tiles(g_ref[t * line : (t + 1) * line], tile_cols)
        for c in range(tile_cols):
            tile = t * tile_cols + c
            q_bd = block_diagonal((q_cols[c] * FACTOR).astype(BF), heads)
            g_bd = block_diagonal(g_cols[c].astype(BF), heads)
            qbd_ref[tile] = q_bd
            gbd_ref[tile] = g_bd
            low, high = columns_near(c, tile_cols)
            near = slice(low * rows, high * rows)
            size = (high - low) * rows
            s = dot_nt(kc_ref[near], q_bd)
            d = dot_nt(vc_ref[near], g_bd).astype(BF)
            top = jnp.max(s, axis=0, keepdims=True)
            e = jnp.exp(s - top)
            exp_ref[tile, :size] = e
            dw_ref[tile, :size] = d
            stat_ref[tile, 0:1] = top
            stat_ref[tile, 1:2] = jnp.sum(e, axis=0, keepdims=True)
            stat_ref[tile, 2:3] = jnp.sum(e * d.astype(F32), axis=0, keepdims=True)


def tile_row_of(group):
    odd = lax.rem(lax.axis_index("rows"), 2)
    return odd if group == 0 else 1 - odd


def halo_kernel(tile_cols, group, qbd_ref, gbd_ref, stat_ref, halo_ref, exp_ref, dw_ref, sum_ref):
    edge = tile_cols * PATCH
    me = lax.axis_index("rows")
    inner = (me > 0) & (me < lax.axis_size("rows") - 1)
    tiles = [tile_row_of(group) * tile_cols + c for c in range(tile_cols)]
    scores = [dot_nt(halo_ref[:edge], qbd_ref[tile]) for tile in tiles]
    grads = [dot_nt(halo_ref[edge : 2 * edge], gbd_ref[tile]) for tile in tiles]
    olds = [[stat_ref[tile, n : n + 1] for n in range(3)] for tile in tiles]
    for c in range(tile_cols):
        low, high = columns_near(c, tile_cols)
        size = (high - low) * PATCH
        s = pick(scores[c], low, high, tile_cols)
        if group == 0:
            s = jnp.where(inner, s, -1e30)
        d = pick(grads[c], low, high, tile_cols).astype(BF)
        own_top, own_sum, own_dot = olds[c]
        top = jnp.maximum(own_top, jnp.max(s, axis=0, keepdims=True))
        e = jnp.exp(s - top)
        ratio = jnp.exp(own_top - top)
        exp_ref[c, :size] = e
        dw_ref[c, :size] = d
        sum_ref[c, 0:1] = top
        sum_ref[c, 1:2] = own_sum * ratio + jnp.sum(e, axis=0, keepdims=True)
        sum_ref[c, 2:3] = own_dot * ratio + jnp.sum(e * d.astype(F32), axis=0, keepdims=True)
        sum_ref[c, 3:4] = ratio


def far_kernel(tile_cols, split_regs, *refs):
    qbd_ref, gbd_ref = refs[:2]
    halos, a_ref = (refs[2:5], refs[5:8]), refs[8]
    refs = refs[3:]
    edge = tile_cols * PATCH
    regs = []
    if split_regs:
        own_ref, two_ref, three_ref = refs[6:9]
        refs = refs[9:]
        cut = own_ref.shape[1]
        for n in range(2):
            base = 2 * edge + n * cut
            regs.append(jnp.concatenate([own_ref[n], two_ref[n], three_ref[n], a_ref[base : base + cut]], axis=0))
    else:
        regs = [refs[6][n] for n in range(2)]
        refs = refs[7:]
    final_ref, px_ref, dsx_ref, kr_ref, vr_ref, back_a_ref, back_b_ref = refs[:7]
    reg_outs = refs[7:]
    kr_ref[...], vr_ref[...] = regs
    feature = a_ref.shape[1]
    places = [(group, c) for group in range(2) for c in range(tile_cols)]
    tiles = [tile_row_of(group) * tile_cols + c for group, c in places]
    scores = [dot_nt(kr_ref[...], qbd_ref[tile]) for tile in tiles]
    grads = [dot_nt(vr_ref[...], gbd_ref[tile]).astype(BF).astype(F32) for tile in tiles]
    parts = []
    for n, (group, c) in enumerate(places):
        sum_ref = halos[group][2]
        s, d = scores[n], grads[n]
        old_top = sum_ref[c, 0:1]
        top = jnp.maximum(old_top, jnp.max(s, axis=0, keepdims=True))
        e = jnp.exp(s - top)
        ratio = jnp.exp(old_top - top)
        inverse = 1.0 / (sum_ref[c, 1:2] * ratio + jnp.sum(e, axis=0, keepdims=True))
        row_dot = (sum_ref[c, 2:3] * ratio + jnp.sum(e * d, axis=0, keepdims=True)) * inverse
        scale = ratio * inverse
        final_ref[n, 0:1] = sum_ref[c, 3:4] * scale
        final_ref[n, 1:2] = row_dot
        p = e * inverse
        parts.append((scale, row_dot, p.astype(BF), (p * (d - row_dot)).astype(BF)))
    for n, (group, c) in enumerate(places):
        exp_ref, dw_ref, _ = halos[group]
        scale, row_dot, p_reg, ds_reg = parts[n]
        low, high = columns_near(c, tile_cols)
        size = (high - low) * PATCH
        p = exp_ref[c, :size] * scale
        ds = p * (dw_ref[c, :size].astype(F32) - row_dot)
        px_ref[n, :edge] = spread(p, low, high, tile_cols).astype(BF)
        dsx_ref[n, :edge] = spread(ds, low, high, tile_cols).astype(BF)
        px_ref[n, edge:] = p_reg
        dsx_ref[n, edge:] = ds_reg
    dk_reg = dv_reg = None
    for group in range(2):
        dk_t = dv_t = None
        for c in range(tile_cols):
            n = group * tile_cols + c
            dk = dot_nn(dsx_ref[n], qbd_ref[tiles[n]])
            dv = dot_nn(px_ref[n], gbd_ref[tiles[n]])
            dk_t = dk if dk_t is None else dk_t + dk
            dv_t = dv if dv_t is None else dv_t + dv
        back_ref = (back_b_ref, back_a_ref)[group]
        back_ref[:edge] = dk_t[:edge].astype(BF)
        back_ref[edge : 2 * edge] = dv_t[:edge].astype(BF)
        dk_reg = dk_t[edge:] if dk_reg is None else dk_reg + dk_t[edge:]
        dv_reg = dv_t[edge:] if dv_reg is None else dv_reg + dv_t[edge:]
    for n, reg in enumerate((dk_reg, dv_reg)):
        if split_regs:
            base = 2 * edge + n * cut
            reg_outs[0][n] = reg[:cut]
            reg_outs[1][n] = reg[cut : 2 * cut].astype(BF)
            reg_outs[2][n] = reg[2 * cut : 3 * cut].astype(BF)
            back_a_ref[base : base + cut] = reg[3 * cut :].astype(BF)
        else:
            reg_outs[0][n] = reg


def rest_kernel(
    tile_cols,
    qbd_ref,
    gbd_ref,
    kt_ref,
    vt_ref,
    exp_ref,
    dw_ref,
    final_ref,
    px_ref,
    dsx_ref,
    from_b_ref,
    from_a_ref,
    kr_ref,
    vr_ref,
    *refs,
):
    o_ref, dq_ref, dk_ref, dv_ref = refs[:4]
    feature = kt_ref.shape[0]
    heads = feature // HEAD
    line = tile_cols * PATCH
    tile_rows = qbd_ref.shape[0] // tile_cols
    rows = tile_rows * PATCH
    edge = tile_cols * PATCH
    for group, halo_ref in enumerate((from_b_ref, from_a_ref)):
        t = tile_row_of(group)
        kxt = jnp.concatenate([halo_ref[:edge], kr_ref[...]], axis=0).T
        vxt = jnp.concatenate([halo_ref[edge : 2 * edge], vr_ref[...]], axis=0).T
        o_cols, dq_cols = [], []
        for c in range(tile_cols):
            tile = t * tile_cols + c
            n = group * tile_cols + c
            low, high = columns_near(c, tile_cols)
            near = slice(low * rows, high * rows)
            size = (high - low) * rows
            p = exp_ref[tile, :size] * final_ref[n, 0:1]
            d_scores = (p * (dw_ref[tile, :size].astype(F32) - final_ref[n, 1:2])).astype(BF)
            weights = p.astype(BF)
            dk = dot_nn(d_scores, qbd_ref[tile])
            dv = dot_nn(weights, gbd_ref[tile])
            first = group == 0
            for ref, value in ((dk_ref, dk), (dv_ref, dv)):
                for x in range(low, high):
                    part = value[(x - low) * rows : (x - low + 1) * rows]
                    if first and (x == c + 1 or (c == 0)):
                        ref[x] = part
                    else:
                        ref[x] += part
            o_t = dot_nn(vt_ref[:, near], weights) + dot_nn(vxt, px_ref[n])
            dq_t = dot_nn(kt_ref[:, near], d_scores) + dot_nn(kxt, dsx_ref[n])
            o_cols.append(from_transposed(o_t, heads))
            dq_cols.append(from_transposed(dq_t, heads) * FACTOR)
        lines = pl.ds(pl.multiple_of(t * line, line), line)
        o_ref[lines] = patch_order(o_cols).astype(BF)
        dq_ref[lines] = patch_order(dq_cols).astype(BF)


def registers_kernel(part_ref, three_ref, two_ref, out_ref):
    out_ref[...] = part_ref[...] + two_ref[...].astype(F32) + three_ref[...].astype(F32)


def finish_kernel(split_regs, dk_ref, dv_ref, a_ref, b_ref, *refs):
    if split_regs:
        own_ref, gk_ref, gv_ref, part_ref = refs
        cut = own_ref.shape[1]
        base = a_ref.shape[0] - 2 * cut
        for n in range(2):
            part_ref[n] = own_ref[n] + a_ref[base + n * cut : base + (n + 1) * cut].astype(F32)
    else:
        gk_ref, gv_ref = refs
    me = lax.axis_index("rows")
    even = lax.rem(me, 2) == 0
    has_top = me > 0
    has_bottom = me < lax.axis_size("rows") - 1
    tile_cols = dk_ref.shape[0]
    edge = tile_cols * PATCH
    for n, (acc_ref, out_ref) in enumerate(((dk_ref, gk_ref), (dv_ref, gv_ref))):
        from_a = a_ref[n * edge : (n + 1) * edge]
        from_b = b_ref[n * edge : (n + 1) * edge]
        top = jnp.where(has_top, jnp.where(even, from_b, from_a).astype(F32), 0.0)
        bottom = jnp.where(has_bottom, jnp.where(even, from_a, from_b).astype(F32), 0.0)
        total = patch_order([acc_ref[c] for c in range(tile_cols)])
        out_ref[:edge] = (total[:edge] + top).astype(BF)
        out_ref[edge:] = (total[edge:] + bottom).astype(BF)


def shape(dims, dtype):
    return jax.ShapeDtypeStruct(dims, dtype)


def call(kernel, name, ins, outs, flops, in_specs=None, scratch=()):
    size = sum(x.size * x.dtype.itemsize for x in ins) + sum(x.size * x.dtype.itemsize for x in outs)
    return pl.pallas_call(
        kernel,
        out_shape=tuple(outs),
        in_specs=in_specs or [VMEM] * len(ins),
        out_specs=(VMEM,) * len(outs),
        scratch_shapes=list(scratch),
        compiler_params=pltpu.CompilerParams(vmem_limit_bytes=24 * 1024 * 1024),
        cost_estimate=pl.CostEstimate(flops=flops, bytes_accessed=size, transcendentals=0),
        name=name,
    )(*ins)


def shards(query, keys, values, registers, cotangent):
    count = lax.axis_size("rows")
    split_regs = count == 4
    tile_cols = query.shape[1] // TILE
    tile_rows = query.shape[0] // TILE
    assert tile_rows == 2
    feature = query.shape[2]
    total = query.shape[0] * query.shape[1]
    edge = tile_cols * PATCH
    own = registers.shape[1]
    reg_count = own * count
    q, k, v, g = (
        pltpu.with_memory_space_constraint(x.reshape(total, feature), pltpu.HBM)
        for x in (query, keys, values, cotangent)
    )
    extra = 2 * own if split_regs else 0
    two = [(i, i ^ 2) for i in range(count)]
    three = [(i, i ^ 3) for i in range(count)]

    registers = pltpu.with_memory_space_constraint(registers, pltpu.HBM)
    pay_a, pay_b, reg_held = call(
        prepare_kernel,
        "prepare",
        (k, v, registers),
        (
            shape((2 * edge + extra, feature), BF),
            shape((2 * edge, feature), BF),
            shape(registers.shape, BF),
        ),
        0,
        in_specs=[HBM] * 3,
        scratch=[pltpu.SemaphoreType.DMA((7,))],
    )
    got_b = swap_b(pay_b)
    got_a = swap(pay_a, pairs_a(count))
    if split_regs:
        regs = (reg_held, swap(reg_held, two), swap(reg_held, three))
    else:
        regs = (lax.all_gather(registers, "rows", axis=1, tiled=True),)

    tiles = tile_rows * tile_cols
    rows = tile_rows * PATCH
    most = min(3, tile_cols) * rows
    window = edge + reg_count
    qbd, gbd, kt, vt, exps, dw, stats = call(
        functools.partial(own_kernel, tile_cols),
        "own",
        (q, g, k, v),
        (
            shape((tiles, feature, feature), BF),
            shape((tiles, feature, feature), BF),
            shape((feature, total), BF),
            shape((feature, total), BF),
            shape((tiles, most, feature), F32),
            shape((tiles, most, feature), BF),
            shape((tiles, 8, feature), F32),
        ),
        600_000_000,
        in_specs=[HBM] * 4,
        scratch=[pltpu.VMEM((total, feature), BF)] * 6 + [pltpu.SemaphoreType.DMA((4,))],
    )
    if split_regs:
        reg_shapes = (
            shape((2, own, feature), F32),
            shape((2, own, feature), BF),
            shape((2, own, feature), BF),
        )
    else:
        reg_shapes = (shape((2, reg_count, feature), F32),)
    halos = []
    for group, got in enumerate((got_b, got_a)):
        halos.append(
            call(
                functools.partial(halo_kernel, tile_cols, group),
                "halo",
                (qbd, gbd, stats, got),
                (
                    shape((tile_cols, edge, feature), F32),
                    shape((tile_cols, edge, feature), BF),
                    shape((tile_cols, 8, feature), F32),
                ),
                32 * tile_cols * edge * feature * feature,
            )
        )
    final, px, dsx, kr, vr, back_a, back_b, *back_regs = call(
        functools.partial(far_kernel, tile_cols, split_regs),
        "far",
        (qbd, gbd) + tuple(halos[0]) + tuple(halos[1]) + (got_a,) + regs,
        (
            shape((tiles, 8, feature), F32),
            shape((tiles, window, feature), BF),
            shape((tiles, window, feature), BF),
            shape((reg_count, feature), BF),
            shape((reg_count, feature), BF),
            shape((2 * edge + extra, feature), BF),
            shape((2 * edge, feature), BF),
        )
        + reg_shapes,
        8 * tiles * window * feature * feature,
    )
    back_from_b = swap_b(back_b)
    back_from_a = swap(back_a, pairs_a(count))
    attended, grad_query, dk, dv = call(
        functools.partial(rest_kernel, tile_cols),
        "rest",
        (qbd, gbd, kt, vt, exps, dw, final, px, dsx, got_b, got_a, kr, vr),
        (
            shape((total, feature), BF),
            shape((total, feature), BF),
            shape((tile_cols, rows, feature), F32),
            shape((tile_cols, rows, feature), F32),
        ),
        600_000_000,
    )
    mine = (back_regs[0],) if split_regs else ()
    grad_keys, grad_values, *part = call(
        functools.partial(finish_kernel, split_regs),
        "finish",
        (dk, dv, back_from_a, back_from_b) + mine,
        (shape((total, feature), BF), shape((total, feature), BF)) + tuple(shape(x.shape, F32) for x in mine),
        0,
    )
    if split_regs:
        (grad_registers,) = call(
            registers_kernel,
            "registers",
            (part[0], swap(back_regs[2], three), swap(back_regs[1], two)),
            (shape((2, own, feature), F32),),
            0,
        )
    else:
        grad_registers = lax.psum_scatter(back_regs[0], "rows", scatter_dimension=1, tiled=True)
    whole = query.shape
    return (
        attended.reshape(whole),
        grad_query.reshape(whole),
        grad_keys.reshape(whole),
        grad_values.reshape(whole),
        grad_registers,
    )


def solution(mesh):
    slab = P(("groups", "rows"), None, "cols")
    in_specs = (slab, slab, slab, P(None, "rows", "cols"), slab)
    out_specs = (slab, slab, slab, slab, P("groups", "rows", "cols"))
    return jax.shard_map(shards, mesh=mesh, in_specs=in_specs, out_specs=out_specs, check_vma=False)
```

```python
import functools

import jax
import jax.numpy as jnp
from jax import lax
from jax.experimental import pallas as pl
from jax.experimental.pallas import tpu as pltpu
from jax.sharding import PartitionSpec as P

HEAD = 64
TILE = 8
PATCH = TILE * TILE
FACTOR = HEAD ** (-0.5)
BF = jnp.bfloat16
F32 = jnp.float32
VMEM = pl.BlockSpec(memory_space=pltpu.VMEM)
HBM = pl.BlockSpec(memory_space=pltpu.HBM)


def swap(array, pairs):
    return lax.ppermute(array, "rows", pairs)


def pairs_a(count):
    return [(i, i ^ 1) for i in range(count)]


def swap_b(array):
    count, across = lax.axis_size("rows"), lax.axis_size("cols")
    pairs = []
    for row in range(count):
        other = row if row in (0, count - 1) else row + 1 if row % 2 else row - 1
        for col in range(across):
            to = min(col ^ 1, across - 1) if other == row else col
            pairs.append((row * across + col, other * across + to))
    return lax.ppermute(array, ("rows", "cols"), pairs)


def column_tiles(block, tile_cols):
    feature = block.shape[1]
    wide = block.astype(F32).reshape(-1, tile_cols, TILE, feature)
    return [wide[:, c].reshape(-1, feature) for c in range(tile_cols)]


def patch_order(columns):
    feature = columns[0].shape[1]
    parts = [x.reshape(-1, 1, TILE, feature) for x in columns]
    return jnp.concatenate(parts, axis=1).reshape(-1, feature)


def pick(block, low, high, tile_cols):
    if high - low == tile_cols:
        return block
    feature = block.shape[1]
    return block.reshape(-1, tile_cols, TILE, feature)[:, low:high].reshape(-1, feature)


def spread(block, low, high, tile_cols):
    if high - low == tile_cols:
        return block
    feature = block.shape[1]
    parts = [block.reshape(-1, high - low, TILE, feature)]
    count = parts[0].shape[0]
    if low > 0:
        parts.insert(0, jnp.zeros((count, low, TILE, feature), block.dtype))
    if high < tile_cols:
        parts.append(jnp.zeros((count, tile_cols - high, TILE, feature), block.dtype))
    return jnp.concatenate(parts, axis=1).reshape(-1, feature)


def slots(heads):
    return [0, 2, 1, 3] if heads == 4 else list(range(heads))


def block_diagonal(tile, heads):
    order = slots(heads)
    feature = tile.shape[1]
    lane_head = lax.broadcasted_iota(jnp.int32, tile.shape, 1) // HEAD
    zero = jnp.zeros_like(tile)
    return jnp.concatenate([jnp.where(lane_head == h, tile, zero) for h in order], axis=0)


def from_transposed(out_t, heads):
    if heads == 4:
        first = lax.broadcasted_iota(jnp.int32, (HEAD, 2 * PATCH), 1) < PATCH
        left = jnp.where(first, out_t[:HEAD, : 2 * PATCH], out_t[2 * HEAD : 3 * HEAD, : 2 * PATCH])
        right = jnp.where(first, out_t[HEAD : 2 * HEAD, 2 * PATCH :], out_t[3 * HEAD :, 2 * PATCH :])
        turned = jnp.concatenate([left, right], axis=0).T
        return jnp.concatenate([turned[:PATCH], turned[PATCH:]], axis=1)
    turned = out_t.T
    lane_head = lax.broadcasted_iota(jnp.int32, (PATCH, heads * HEAD), 1) // HEAD
    total = turned[:PATCH]
    for h in range(1, heads):
        total = jnp.where(lane_head == h, turned[h * PATCH : (h + 1) * PATCH], total)
    return total


def dot_nt(a, b):
    return lax.dot_general(a, b, (((1,), (1,)), ((), ())), preferred_element_type=F32)


def dot_nn(a, b):
    return lax.dot_general(a, b, (((1,), (0,)), ((), ())), preferred_element_type=F32)


def copy_all(moves, sems):
    copies = [pltpu.make_async_copy(x, y, sems.at[n]) for n, (x, y) in enumerate(moves)]
    for copy in copies:
        copy.start()
    for copy in copies:
        copy.wait()


def prepare_kernel(k_ref, v_ref, reg_ref, a_ref, b_ref, held_ref, sems):
    even = lax.rem(lax.axis_index("rows"), 2) == 0
    edge = k_ref.shape[0] // 2
    last = k_ref.shape[0] - edge
    at_a = pl.multiple_of(jnp.where(even, last, 0), edge)
    at_b = pl.multiple_of(jnp.where(even, 0, last), edge)
    moves = []
    for n, ref in enumerate((k_ref, v_ref)):
        moves.append((ref.at[pl.ds(at_b, edge)], b_ref.at[pl.ds(n * edge, edge)]))
        moves.append((ref.at[pl.ds(at_a, edge)], a_ref.at[pl.ds(n * edge, edge)]))
    own = reg_ref.shape[1]
    if a_ref.shape[0] > 2 * edge:
        for n in range(2):
            moves.append((reg_ref.at[n], a_ref.at[pl.ds(2 * edge + n * own, own)]))
    moves.append((reg_ref, held_ref))
    copy_all(moves, sems)


def columns_near(c, tile_cols):
    return max(c - 1, 0), min(c + 2, tile_cols)


def own_kernel(tile_cols, *refs):
    qbd_ref, gbd_ref, kt_ref, vt_ref, exp_ref, dw_ref, stat_ref, kc_ref, vc_ref = refs[4:13]
    q_ref, g_ref, k_ref, v_ref = held = refs[13:17]
    copy_all(list(zip(refs[:4], held)), refs[17])
    heads = q_ref.shape[1] // HEAD
    line = tile_cols * PATCH
    tile_rows = q_ref.shape[0] // line
    rows = tile_rows * PATCH
    for x_ref, c_ref, t_ref in ((k_ref, kc_ref, kt_ref), (v_ref, vc_ref, vt_ref)):
        for c, column in enumerate(column_tiles(x_ref[...], tile_cols)):
            column = column.astype(BF)
            c_ref[c * rows : (c + 1) * rows] = column
            t_ref[:, c * rows : (c + 1) * rows] = column.T
    for t in range(tile_rows):
        q_cols = column_tiles(q_ref[t * line : (t + 1) * line], tile_cols)
        g_cols = column_tiles(g_ref[t * line : (t + 1) * line], tile_cols)
        for c in range(tile_cols):
            tile = t * tile_cols + c
            q_bd = block_diagonal((q_cols[c] * FACTOR).astype(BF), heads)
            g_bd = block_diagonal(g_cols[c].astype(BF), heads)
            qbd_ref[tile] = q_bd
            gbd_ref[tile] = g_bd
            low, high = columns_near(c, tile_cols)
            near = slice(low * rows, high * rows)
            size = (high - low) * rows
            s = dot_nt(kc_ref[near], q_bd)
            d = dot_nt(vc_ref[near], g_bd).astype(BF)
            top = jnp.max(s, axis=0, keepdims=True)
            e = jnp.exp(s - top)
            exp_ref[tile, :size] = e
            dw_ref[tile, :size] = d
            stat_ref[tile, 0:1] = top
            stat_ref[tile, 1:2] = jnp.sum(e, axis=0, keepdims=True)
            stat_ref[tile, 2:3] = jnp.sum(e * d.astype(F32), axis=0, keepdims=True)


def tile_row_of(group):
    odd = lax.rem(lax.axis_index("rows"), 2)
    return odd if group == 0 else 1 - odd


def halo_kernel(tile_cols, group, qbd_ref, gbd_ref, stat_ref, halo_ref, exp_ref, dw_ref, sum_ref):
    edge = tile_cols * PATCH
    me = lax.axis_index("rows")
    inner = (me > 0) & (me < lax.axis_size("rows") - 1)
    tiles = [tile_row_of(group) * tile_cols + c for c in range(tile_cols)]
    scores = [dot_nt(halo_ref[:edge], qbd_ref[tile]) for tile in tiles]
    grads = [dot_nt(halo_ref[edge : 2 * edge], gbd_ref[tile]) for tile in tiles]
    olds = [[stat_ref[tile, n : n + 1] for n in range(3)] for tile in tiles]
    for c in range(tile_cols):
        low, high = columns_near(c, tile_cols)
        size = (high - low) * PATCH
        s = pick(scores[c], low, high, tile_cols)
        if group == 0:
            s = jnp.where(inner, s, -1e30)
        d = pick(grads[c], low, high, tile_cols).astype(BF)
        own_top, own_sum, own_dot = olds[c]
        top = jnp.maximum(own_top, jnp.max(s, axis=0, keepdims=True))
        e = jnp.exp(s - top)
        ratio = jnp.exp(own_top - top)
        exp_ref[c, :size] = e
        dw_ref[c, :size] = d
        sum_ref[c, 0:1] = top
        sum_ref[c, 1:2] = own_sum * ratio + jnp.sum(e, axis=0, keepdims=True)
        sum_ref[c, 2:3] = own_dot * ratio + jnp.sum(e * d.astype(F32), axis=0, keepdims=True)
        sum_ref[c, 3:4] = ratio


def far_kernel(tile_cols, split_regs, *refs):
    qbd_ref, gbd_ref = refs[:2]
    halos, a_ref = (refs[2:5], refs[5:8]), refs[8]
    refs = refs[3:]
    edge = tile_cols * PATCH
    regs = []
    if split_regs:
        own_ref, two_ref, three_ref = refs[6:9]
        refs = refs[9:]
        cut = own_ref.shape[1]
        for n in range(2):
            base = 2 * edge + n * cut
            regs.append(jnp.concatenate([own_ref[n], two_ref[n], three_ref[n], a_ref[base : base + cut]], axis=0))
    else:
        regs = [refs[6][n] for n in range(2)]
        refs = refs[7:]
    final_ref, px_ref, dsx_ref, kr_ref, vr_ref, back_a_ref, back_b_ref = refs[:7]
    reg_outs = refs[7:]
    kr_ref[...], vr_ref[...] = regs
    feature = a_ref.shape[1]
    places = [(group, c) for group in range(2) for c in range(tile_cols)]
    tiles = [tile_row_of(group) * tile_cols + c for group, c in places]
    scores = [dot_nt(kr_ref[...], qbd_ref[tile]) for tile in tiles]
    grads = [dot_nt(vr_ref[...], gbd_ref[tile]).astype(BF).astype(F32) for tile in tiles]
    parts = []
    for n, (group, c) in enumerate(places):
        sum_ref = halos[group][2]
        s, d = scores[n], grads[n]
        old_top = sum_ref[c, 0:1]
        top = jnp.maximum(old_top, jnp.max(s, axis=0, keepdims=True))
        e = jnp.exp(s - top)
        ratio = jnp.exp(old_top - top)
        inverse = 1.0 / (sum_ref[c, 1:2] * ratio + jnp.sum(e, axis=0, keepdims=True))
        row_dot = (sum_ref[c, 2:3] * ratio + jnp.sum(e * d, axis=0, keepdims=True)) * inverse
        scale = ratio * inverse
        final_ref[n, 0:1] = sum_ref[c, 3:4] * scale
        final_ref[n, 1:2] = row_dot
        p = e * inverse
        parts.append((scale, row_dot, p.astype(BF), (p * (d - row_dot)).astype(BF)))
    for n, (group, c) in enumerate(places):
        exp_ref, dw_ref, _ = halos[group]
        scale, row_dot, p_reg, ds_reg = parts[n]
        low, high = columns_near(c, tile_cols)
        size = (high - low) * PATCH
        p = exp_ref[c, :size] * scale
        ds = p * (dw_ref[c, :size].astype(F32) - row_dot)
        px_ref[n, :edge] = spread(p, low, high, tile_cols).astype(BF)
        dsx_ref[n, :edge] = spread(ds, low, high, tile_cols).astype(BF)
        px_ref[n, edge:] = p_reg
        dsx_ref[n, edge:] = ds_reg
    dk_reg = dv_reg = None
    for group in range(2):
        dk_t = dv_t = None
        for c in range(tile_cols):
            n = group * tile_cols + c
            dk = dot_nn(dsx_ref[n], qbd_ref[tiles[n]])
            dv = dot_nn(px_ref[n], gbd_ref[tiles[n]])
            dk_t = dk if dk_t is None else dk_t + dk
            dv_t = dv if dv_t is None else dv_t + dv
        back_ref = (back_b_ref, back_a_ref)[group]
        back_ref[:edge] = dk_t[:edge].astype(BF)
        back_ref[edge : 2 * edge] = dv_t[:edge].astype(BF)
        dk_reg = dk_t[edge:] if dk_reg is None else dk_reg + dk_t[edge:]
        dv_reg = dv_t[edge:] if dv_reg is None else dv_reg + dv_t[edge:]
    for n, reg in enumerate((dk_reg, dv_reg)):
        if split_regs:
            base = 2 * edge + n * cut
            reg_outs[0][n] = reg[:cut]
            reg_outs[1][n] = reg[cut : 2 * cut].astype(BF)
            reg_outs[2][n] = reg[2 * cut : 3 * cut].astype(BF)
            back_a_ref[base : base + cut] = reg[3 * cut :].astype(BF)
        else:
            reg_outs[0][n] = reg


def rest_kernel(
    tile_cols,
    qbd_ref,
    gbd_ref,
    kt_ref,
    vt_ref,
    exp_ref,
    dw_ref,
    final_ref,
    px_ref,
    dsx_ref,
    from_b_ref,
    from_a_ref,
    kr_ref,
    vr_ref,
    *refs,
):
    o_ref, dq_ref, dk_ref, dv_ref = refs[:4]
    feature = kt_ref.shape[0]
    heads = feature // HEAD
    line = tile_cols * PATCH
    tile_rows = qbd_ref.shape[0] // tile_cols
    rows = tile_rows * PATCH
    edge = tile_cols * PATCH
    for group, halo_ref in enumerate((from_b_ref, from_a_ref)):
        t = tile_row_of(group)
        kxt = jnp.concatenate([halo_ref[:edge], kr_ref[...]], axis=0).T
        vxt = jnp.concatenate([halo_ref[edge : 2 * edge], vr_ref[...]], axis=0).T
        o_cols, dq_cols = [], []
        for c in range(tile_cols):
            tile = t * tile_cols + c
            n = group * tile_cols + c
            low, high = columns_near(c, tile_cols)
            near = slice(low * rows, high * rows)
            size = (high - low) * rows
            p = exp_ref[tile, :size] * final_ref[n, 0:1]
            d_scores = (p * (dw_ref[tile, :size].astype(F32) - final_ref[n, 1:2])).astype(BF)
            weights = p.astype(BF)
            dk = dot_nn(d_scores, qbd_ref[tile])
            dv = dot_nn(weights, gbd_ref[tile])
            first = group == 0
            for ref, value in ((dk_ref, dk), (dv_ref, dv)):
                for x in range(low, high):
                    part = value[(x - low) * rows : (x - low + 1) * rows]
                    if first and (x == c + 1 or (c == 0)):
                        ref[x] = part
                    else:
                        ref[x] += part
            o_t = dot_nn(vt_ref[:, near], weights) + dot_nn(vxt, px_ref[n])
            dq_t = dot_nn(kt_ref[:, near], d_scores) + dot_nn(kxt, dsx_ref[n])
            o_cols.append(from_transposed(o_t, heads))
            dq_cols.append(from_transposed(dq_t, heads) * FACTOR)
        lines = pl.ds(pl.multiple_of(t * line, line), line)
        o_ref[lines] = patch_order(o_cols).astype(BF)
        dq_ref[lines] = patch_order(dq_cols).astype(BF)


def finish_kernel(split_regs, dk_ref, dv_ref, a_ref, b_ref, *refs):
    if split_regs:
        own_ref, gk_ref, gv_ref, part_ref = refs
        cut = own_ref.shape[1]
        base = a_ref.shape[0] - 2 * cut
        for n in range(2):
            part_ref[n] = own_ref[n] + a_ref[base + n * cut : base + (n + 1) * cut].astype(F32)
    else:
        gk_ref, gv_ref = refs
    me = lax.axis_index("rows")
    even = lax.rem(me, 2) == 0
    has_top = me > 0
    has_bottom = me < lax.axis_size("rows") - 1
    tile_cols = dk_ref.shape[0]
    edge = tile_cols * PATCH
    for n, (acc_ref, out_ref) in enumerate(((dk_ref, gk_ref), (dv_ref, gv_ref))):
        from_a = a_ref[n * edge : (n + 1) * edge]
        from_b = b_ref[n * edge : (n + 1) * edge]
        top = jnp.where(has_top, jnp.where(even, from_b, from_a).astype(F32), 0.0)
        bottom = jnp.where(has_bottom, jnp.where(even, from_a, from_b).astype(F32), 0.0)
        total = patch_order([acc_ref[c] for c in range(tile_cols)])
        out_ref[:edge] = (total[:edge] + top).astype(BF)
        out_ref[edge:] = (total[edge:] + bottom).astype(BF)


def shape(dims, dtype):
    return jax.ShapeDtypeStruct(dims, dtype)


def call(kernel, name, ins, outs, flops, in_specs=None, scratch=()):
    size = sum(x.size * x.dtype.itemsize for x in ins) + sum(x.size * x.dtype.itemsize for x in outs)
    return pl.pallas_call(
        kernel,
        out_shape=tuple(outs),
        in_specs=in_specs or [VMEM] * len(ins),
        out_specs=(VMEM,) * len(outs),
        scratch_shapes=list(scratch),
        compiler_params=pltpu.CompilerParams(vmem_limit_bytes=24 * 1024 * 1024),
        cost_estimate=pl.CostEstimate(flops=flops, bytes_accessed=size, transcendentals=0),
        name=name,
    )(*ins)


def shards(query, keys, values, registers, cotangent):
    count = lax.axis_size("rows")
    split_regs = count == 4
    tile_cols = query.shape[1] // TILE
    tile_rows = query.shape[0] // TILE
    assert tile_rows == 2
    feature = query.shape[2]
    total = query.shape[0] * query.shape[1]
    edge = tile_cols * PATCH
    own = registers.shape[1]
    reg_count = own * count
    q, k, v, g = (
        pltpu.with_memory_space_constraint(x.reshape(total, feature), pltpu.HBM)
        for x in (query, keys, values, cotangent)
    )
    extra = 2 * own if split_regs else 0
    two = [(i, i ^ 2) for i in range(count)]
    three = [(i, i ^ 3) for i in range(count)]

    registers = pltpu.with_memory_space_constraint(registers, pltpu.HBM)
    pay_a, pay_b, reg_held = call(
        prepare_kernel,
        "prepare",
        (k, v, registers),
        (
            shape((2 * edge + extra, feature), BF),
            shape((2 * edge, feature), BF),
            shape(registers.shape, BF),
        ),
        0,
        in_specs=[HBM] * 3,
        scratch=[pltpu.SemaphoreType.DMA((7,))],
    )
    got_b = swap_b(pay_b)
    got_a = swap(pay_a, pairs_a(count))
    if split_regs:
        regs = (reg_held, swap(reg_held, two), swap(reg_held, three))
    else:
        regs = (lax.all_gather(registers, "rows", axis=1, tiled=True),)

    tiles = tile_rows * tile_cols
    rows = tile_rows * PATCH
    most = min(3, tile_cols) * rows
    window = edge + reg_count
    qbd, gbd, kt, vt, exps, dw, stats = call(
        functools.partial(own_kernel, tile_cols),
        "own",
        (q, g, k, v),
        (
            shape((tiles, feature, feature), BF),
            shape((tiles, feature, feature), BF),
            shape((feature, total), BF),
            shape((feature, total), BF),
            shape((tiles, most, feature), F32),
            shape((tiles, most, feature), BF),
            shape((tiles, 8, feature), F32),
        ),
        600_000_000,
        in_specs=[HBM] * 4,
        scratch=[pltpu.VMEM((total, feature), BF)] * 6 + [pltpu.SemaphoreType.DMA((4,))],
    )
    if split_regs:
        reg_shapes = (
            shape((2, own, feature), F32),
            shape((2, own, feature), BF),
            shape((2, own, feature), BF),
        )
    else:
        reg_shapes = (shape((2, reg_count, feature), F32),)
    halos = []
    for group, got in enumerate((got_b, got_a)):
        halos.append(
            call(
                functools.partial(halo_kernel, tile_cols, group),
                "halo",
                (qbd, gbd, stats, got),
                (
                    shape((tile_cols, edge, feature), F32),
                    shape((tile_cols, edge, feature), BF),
                    shape((tile_cols, 8, feature), F32),
                ),
                32 * tile_cols * edge * feature * feature,
            )
        )
    final, px, dsx, kr, vr, back_a, back_b, *back_regs = call(
        functools.partial(far_kernel, tile_cols, split_regs),
        "far",
        (qbd, gbd) + tuple(halos[0]) + tuple(halos[1]) + (got_a,) + regs,
        (
            shape((tiles, 8, feature), F32),
            shape((tiles, window, feature), BF),
            shape((tiles, window, feature), BF),
            shape((reg_count, feature), BF),
            shape((reg_count, feature), BF),
            shape((2 * edge + extra, feature), BF),
            shape((2 * edge, feature), BF),
        )
        + reg_shapes,
        8 * tiles * window * feature * feature,
    )
    back_from_b = swap_b(back_b)
    back_from_a = swap(back_a, pairs_a(count))
    attended, grad_query, dk, dv = call(
        functools.partial(rest_kernel, tile_cols),
        "rest",
        (qbd, gbd, kt, vt, exps, dw, final, px, dsx, got_b, got_a, kr, vr),
        (
            shape((total, feature), BF),
            shape((total, feature), BF),
            shape((tile_cols, rows, feature), F32),
            shape((tile_cols, rows, feature), F32),
        ),
        600_000_000,
    )
    mine = (back_regs[0],) if split_regs else ()
    grad_keys, grad_values, *part = call(
        functools.partial(finish_kernel, split_regs),
        "finish",
        (dk, dv, back_from_a, back_from_b) + mine,
        (shape((total, feature), BF), shape((total, feature), BF)) + tuple(shape(x.shape, F32) for x in mine),
        0,
    )
    if split_regs:
        grad_registers = (
            part[0] + swap(back_regs[2], three).astype(F32) + swap(back_regs[1], two).astype(F32)
        )
    else:
        grad_registers = lax.psum_scatter(back_regs[0], "rows", scatter_dimension=1, tiled=True)
    whole = query.shape
    return (
        attended.reshape(whole),
        grad_query.reshape(whole),
        grad_keys.reshape(whole),
        grad_values.reshape(whole),
        grad_registers,
    )


def solution(mesh):
    slab = P(("groups", "rows"), None, "cols")
    in_specs = (slab, slab, slab, P(None, "rows", "cols"), slab)
    out_specs = (slab, slab, slab, slab, P("groups", "rows", "cols"))
    return jax.shard_map(shards, mesh=mesh, in_specs=in_specs, out_specs=out_specs, check_vma=False)
```
